128 devices in a mesh: track: 16 (over y, z), strip: 8 (over x, core).
Axes of the slice: x: 4, y: 4, z: 4, core: 2. Of those that a mesh axis runs over, the one named last changes fastest.
Arguments:
- cube: float32 [512, 2560, 224], P('track', 'strip'), may hold values from -64 to 64
- mask: int32 [64, 320], P('track', 'strip'), may hold values 0 or 1
Outputs:
- filtered: float32 [512, 2560, 224], P('track', 'strip')
The draws below stay inside these ranges and needn't reach their ends.
All inputs are finite; a program needn't handle non-finite values. No bound on the sum of `mask` on one device may be relied on, other than what follows from the above.
Results may differ from the reference program's by a relative error of at most 0.00019.
Values sent between devices are 32-bit elements; how exact they have to be, the bound alone decides.
No kernel may reach another device: no remote copies, remote signals or barrier semaphores. Data moves between devices by JAX's collectives and lax.ppermute only.
A program may use at most 128 MiB of HBM per device.

```python
import math
import jax
import jax.numpy as jnp
from jax import lax

B = 224
TILE = 8
NR = 512
NC = 2560


def draw_cube(key, part):
    key = jax.random.fold_in(key, 7)
    sub_keys = jax.random.split(key, 6)
    mixing = jnp.eye(B, dtype=jnp.float32) + 0.5 * jax.random.normal(sub_keys[0], (B, B), jnp.float32) / math.sqrt(B)
    tile_shape = (NR // TILE, TILE, NC // TILE, TILE, B)
    inner = 0.3 * jax.random.normal(sub_keys[2], tile_shape, jnp.float32)
    noise = jax.random.normal(sub_keys[5], (NR, NC, B), jnp.float32)
    offset = 0.5
    parcels = offset + jax.random.normal(sub_keys[1], (NR // TILE, 1, NC // TILE, 1, B), jnp.float32)
    abundance = (parcels + inner).reshape(NR * NC, B)
    signal = jnp.dot(abundance, mixing, precision=lax.Precision.HIGHEST).reshape(NR, NC, B)
    band_scale = jnp.exp(jax.random.uniform(sub_keys[3], (B,), jnp.float32, math.log(0.5), math.log(5.0)))
    noise_scale = jnp.exp(jax.random.uniform(sub_keys[4], (B,), jnp.float32, math.log(0.05), math.log(0.3)))
    return jnp.clip(signal * band_scale + noise * noise_scale, -64.0, 64.0)


def plant(array, stream_key, least, largest):
    index_at = [jax.random.randint(jax.random.fold_in(stream_key, axis), (), 0, length) for axis, length in enumerate(array.shape)]
    longest = array.shape.index(max(array.shape))
    neighbour = index_at[:longest] + [(index_at[longest] + 1) % array.shape[longest]] + index_at[longest + 1:]
    return array.at[tuple(index_at)].set(least).at[tuple(neighbour)].set(largest)


def setup_inputs(seed: int = 0) -> dict:
    key_list = jax.random.split(jax.random.key(seed), 3)
    return {
        "cube": draw_cube(jax.random.fold_in(key_list[2], 71), 0),
        "mask": plant((jax.random.randint(key_list[1], (NR // TILE, NC // TILE), 0, 4) < 3).astype(jnp.int32), jax.random.fold_in(key_list[1], 1), 0, 1),
    }


def gram(weighted, plain):
    return lax.dot_general(weighted, plain, (((0,), (0,)), ((), ())), precision=lax.Precision.HIGHEST)

def reference(cube, mask):
    validity = jnp.repeat(jnp.repeat(mask.astype(jnp.float32), TILE, 0), TILE, 1)
    flat_pixels = cube.reshape(-1, B)
    pixel_mask = validity.reshape(-1, 1)
    pixel_count = jnp.sum(pixel_mask)
    pixel_sum = jnp.sum(flat_pixels * pixel_mask, 0)
    pixel_square = gram(flat_pixels * pixel_mask, flat_pixels)
    differences = (cube[1:] - cube[:-1]).reshape(-1, B)
    weights = (validity[1:] * validity[:-1]).reshape(-1, 1)
    pair_count = jnp.sum(weights)
    pair_sum = jnp.sum(differences * weights, 0)
    pair_square = gram(differences * weights, differences)
    band_mean = pixel_sum / pixel_count
    signal_cov = (pixel_square - pixel_sum[:, None] * pixel_sum[None, :] / pixel_count) / (pixel_count - 1.0)
    noise_cov = (pair_square - pair_sum[:, None] * pair_sum[None, :] / pair_count) / (pair_count - 1.0)
    combined = signal_cov + noise_cov
    factor = jnp.linalg.cholesky(combined)
    noise_gain = jax.scipy.linalg.cho_solve((factor, True), noise_cov)
    shifted = jnp.dot(flat_pixels - band_mean, noise_gain, precision=lax.Precision.HIGHEST)
    return (pixel_mask * (flat_pixels - shifted)).reshape(cube.shape)
```

```python
import functools

import jax
import jax.numpy as jnp
from jax import lax
from jax.experimental import pallas as pl
from jax.experimental.pallas import tpu as pltpu
from jax.sharding import PartitionSpec as P

TILE = 8
W = 256
F32 = jnp.float32
BF16 = jnp.bfloat16
ROWS = 8
VMEM_LIMIT = 48 * 2**20


def split(x):
    high = x.astype(BF16)
    return high, (x - high.astype(F32)).astype(BF16)


def split3(x):
    high = x.astype(BF16)
    rest = x - high.astype(F32)
    middle = rest.astype(BF16)
    return high, middle, (rest - middle.astype(F32)).astype(BF16)


def dot(a, b):
    return lax.dot_general(a, b, (((1,), (0,)), ((), ())), preferred_element_type=F32)


def dot_t(a, b):
    return lax.dot_general(a, b, (((0,), (0,)), ((), ())), preferred_element_type=F32)


def dot3(a, b):
    a_high, a_low = split(a)
    b_high, b_low = split(b)
    return dot(
        jnp.concatenate([a_high, a_high, a_low], 1),
        jnp.concatenate([b_high, b_low, b_high], 0),
    )


def dot6(a, b):
    ah, am, al = split3(a)
    bh, bm, bl = split3(b)
    return dot(
        jnp.concatenate([ah, ah, am, ah, am, al], 1),
        jnp.concatenate([bh, bm, bh, bl, bm, bh], 0),
    )


def fill_validity(mask_ref, tile_row, out_ref):
    for c in range(out_ref.shape[0] // TILE):
        value = mask_ref[tile_row, c].astype(F32)
        out_ref[c * TILE : (c + 1) * TILE, :] = jnp.full((TILE, out_ref.shape[1]), value, F32)


def gram_kernel(mask_ref, cube_ref, pixel_ref, pair_ref, last_row, valid, seam, pixels, pairs):
    step = pl.program_id(0)
    cols, bands = cube_ref.shape[1:]

    @pl.when(step == 0)
    def _():
        last_row[...] = jnp.zeros_like(last_row)
        valid[...] = jnp.zeros_like(valid)
        pixel_ref[...] = jnp.zeros_like(pixel_ref)
        pair_ref[...] = jnp.zeros_like(pair_ref)

    seam[...] = valid[...]
    fill_validity(mask_ref, step, valid)
    seam[...] = seam[...] * valid[...]
    previous = last_row[...]
    for r in range(ROWS):
        pixel = cube_ref[r] * valid[:, :bands]
        weight = seam if r == 0 else valid
        difference = pixel - previous
        if r == 0:
            difference = difference * seam[:, :bands]
        previous = pixel
        at = slice(r * cols, (r + 1) * cols)
        for value, ones, buffer in ((pixel, valid, pixels), (difference, weight, pairs)):
            high, low = split(jnp.concatenate([value, ones[:, : W - bands]], 1))
            buffer[at, :W] = high
            buffer[at, W:] = low
    last_row[...] = previous
    for ref, buffer in ((pixel_ref, pixels), (pair_ref, pairs)):
        ref[:, : 2 * W] += dot_t(buffer[:, :W], buffer[...])
        ref[:, 2 * W :] += dot_t(buffer[:, W:], buffer[:, W:])


def grams(cube, mask):
    rows, cols, bands = cube.shape
    return pl.pallas_call(
        gram_kernel,
        out_shape=[jax.ShapeDtypeStruct((W, 3 * W), F32)] * 2,
        grid=(rows // ROWS,),
        in_specs=[
            pl.BlockSpec(memory_space=pltpu.SMEM),
            pl.BlockSpec((ROWS, cols, bands), lambda i: (i, 0, 0)),
        ],
        out_specs=[pl.BlockSpec((W, 3 * W), lambda i: (0, 0))] * 2,
        scratch_shapes=[
            pltpu.VMEM((cols, bands), F32),
            pltpu.VMEM((cols, W), F32),
            pltpu.VMEM((cols, W), F32),
            pltpu.VMEM((ROWS * cols, 2 * W), BF16),
            pltpu.VMEM((ROWS * cols, 2 * W), BF16),
        ],
        compiler_params=pltpu.CompilerParams(vmem_limit_bytes=VMEM_LIMIT),
        cost_estimate=pl.CostEstimate(flops=6 * 2 * rows * cols * W * W, bytes_accessed=4 * rows * cols * W, transcendentals=0),
        name="grams",
    )(mask, cube)


def indices(shape):
    return lax.broadcasted_iota(jnp.int32, shape, 0), lax.broadcasted_iota(jnp.int32, shape, 1)


def pack_kernel(core_ref, mask_ref, cube_ref, below_ref, pixel_ref, pair_ref, mine_ref, other_ref, valid, packed):
    bands = cube_ref.shape[2]
    half = bands // 2
    fill_validity(mask_ref, mask_ref.shape[0] - 1, valid)
    weight = valid[...] * jnp.broadcast_to(below_ref[:, bands : bands + 1], valid.shape)
    difference = (below_ref[:, :bands] - cube_ref[0]) * weight[:, :bands]
    high, low = split(jnp.concatenate([difference, weight[:, : W - bands]], 1))
    both = jnp.concatenate([high, low], 1)

    def whole(ref, cross, lows):
        cross = cross + ref[:, : 2 * W]
        mixed = cross[:, W:]
        return cross[:, :W] + mixed + mixed.T + (lows + ref[:, 2 * W :])

    pair = whole(pair_ref, dot_t(high, both), dot_t(low, low))
    pixel = whole(pixel_ref, jnp.zeros((W, 2 * W), F32), jnp.zeros((W, W), F32))
    row, column = indices((W, W))
    out = jnp.where(column <= row, pair, 0.0)
    moved = pltpu.roll(pixel, 1, 1)
    out = jnp.where((column > row) & (column <= bands + 1), moved, out)
    pair_sum = pltpu.roll(pair, 2, 1)
    out = jnp.where(column == bands + 2, pair_sum, out)
    counts = jnp.where(row == 0, pixel[bands : bands + 1, bands : bands + 1], 0.0)
    counts = jnp.where(row == 1, pair[bands : bands + 1, bands : bands + 1], counts)
    out = jnp.where(column == bands + 3, counts, out)
    packed[...] = out
    core = core_ref[0]
    mine_ref[...] = packed[pl.ds(pl.multiple_of(core * half, 8), half), :]
    other_ref[...] = packed[pl.ds(pl.multiple_of((1 - core) * half, 8), half), :]


def pack(core, cube, mask, below, pixel, pair):
    rows, cols, bands = cube.shape
    vmem = lambda a: pl.BlockSpec(a.shape, lambda i: (0,) * a.ndim)
    half = jax.ShapeDtypeStruct((bands // 2, W), F32)
    return pl.pallas_call(
        pack_kernel,
        out_shape=[half, half],
        grid=(1,),
        in_specs=[
            pl.BlockSpec(memory_space=pltpu.SMEM),
            pl.BlockSpec(memory_space=pltpu.SMEM),
            pl.BlockSpec((1, cols, bands), lambda i: (rows - 1, 0, 0)),
            vmem(below),
            vmem(pixel),
            vmem(pair),
        ],
        out_specs=[vmem(half), vmem(half)],
        scratch_shapes=[pltpu.VMEM((cols, W), F32), pltpu.VMEM((W, W), F32)],
        compiler_params=pltpu.CompilerParams(vmem_limit_bytes=VMEM_LIMIT),
        name="pack",
    )(core, mask, cube, below, pixel, pair)


def square_sum(x):
    return jnp.sum(x * x)


def solve_kernel(bands, core_ref, mine_ref, other_ref, gain_ref, mean_ref, left, right):
    half = bands // 2
    core = core_ref[0]
    packed = jnp.concatenate([mine_ref[...], other_ref[...]], 0)
    swapped = jnp.concatenate([other_ref[...], mine_ref[...]], 0)
    packed = jnp.where(core == 0, packed, swapped)
    packed = jnp.concatenate([packed, jnp.zeros((W - bands, W), F32)], 0)
    row, column = indices((W, W))
    on_diagonal = row == column
    inside = (row < bands) & (column < bands)
    pixel_count = packed[0:1, bands + 3 : bands + 4]
    pair_count = packed[1:2, bands + 3 : bands + 4]

    def whole(triangle):
        return triangle + triangle.T - jnp.where(on_diagonal, triangle, 0.0)

    pixel = whole(jnp.where((column >= row) & (column <= bands), pltpu.roll(packed, W - 1, 1), 0.0))
    lower = jnp.where((column <= row) & inside, packed, 0.0)
    sums = jnp.where((column == bands) & (row < bands), pltpu.roll(packed, W - 2, 1), 0.0)
    pair = whole(lower + sums)

    def covariance(square, count):
        total = square[bands : bands + 1, :]
        total_rows = square[:, bands : bands + 1]
        return jnp.where(inside, (square - total_rows * total / count) / (count - 1.0), 0.0)

    signal = covariance(pixel, pixel_count)
    noise = covariance(pair, pair_count)
    combined = signal + noise
    mean_ref[...] = pixel[bands : bands + 1, :] / pixel_count
    diagonal = jnp.where(on_diagonal, combined, 0.0)
    scale_row = lax.rsqrt(jnp.where(column[0:1] < bands, jnp.sum(diagonal, 0, keepdims=True), 1.0))
    scale_column = lax.rsqrt(jnp.where(row[:, 0:1] < bands, jnp.sum(diagonal, 1, keepdims=True), 1.0))
    identity = jnp.where(on_diagonal, 1.0, 0.0)
    matrix = jnp.where(inside, combined * scale_column * scale_row, identity)
    target = noise * scale_column * scale_row

    start = 1.0 / jnp.max(jnp.sum(jnp.abs(matrix), 1, keepdims=True))
    left[:W, :] = start * identity
    left[W:, :] = identity - start * matrix

    def more(carry):
        count, size = carry
        return (count < 24) & (size > 4e-6)

    def squaring(carry):
        count, _ = carry
        new = dot3(left[...], left[W:, :])
        left[:W, :] = left[:W, :] + new[:W]
        left[W:, :] = new[W:]
        return count + 1, square_sum(new[W:])

    lax.while_loop(more, squaring, (0, jnp.float32(1e9)))
    inverse = left[:W, :]
    right[...] = dot3(inverse, target)

    def refining(carry):
        count, _ = carry
        residual = target - dot6(matrix, right[...])
        change = dot3(left[:W, :], residual)
        gain = right[...] + change
        right[...] = gain
        return count + 1, square_sum(change) / square_sum(gain)

    def rough(carry):
        count, size = carry
        return (count < 8) & jnp.logical_not(size <= 1e-6)

    _, size = lax.while_loop(rough, refining, (0, jnp.float32(1e9)))

    @pl.when(jnp.logical_not(size <= 1e-6))
    def _():
        left[:W, :] = matrix
        right[...] = target

        def eliminate(k, _):
            here = row[:, 0:1] == k
            pivot_left = left[pl.ds(k, 1), :]
            pivot_right = right[pl.ds(k, 1), :]
            values = jnp.sum(jnp.where(column == k, left[:W, :], 0.0), 1, keepdims=True)
            pivot = jnp.sum(jnp.where(here, values, 0.0))
            factor = jnp.where(here, (values - 1.0) / pivot, values / pivot)
            left[:W, :] = left[:W, :] - factor * pivot_left
            right[...] = right[...] - factor * pivot_right
            return 0

        lax.fori_loop(0, bands, eliminate, 0)

    gain = right[...] * scale_column * (1.0 / scale_row)
    high, low = split(gain)
    gain_ref[:, :W] = high
    gain_ref[:, W:] = low


def solve(core, mine, other, bands):
    vmem = lambda a: pl.BlockSpec(a.shape, lambda i: (0,) * a.ndim)
    outs = [jax.ShapeDtypeStruct((W, 2 * W), BF16), jax.ShapeDtypeStruct((1, W), F32)]
    return pl.pallas_call(
        functools.partial(solve_kernel, bands),
        out_shape=outs,
        grid=(1,),
        in_specs=[pl.BlockSpec(memory_space=pltpu.SMEM), vmem(mine), vmem(other)],
        out_specs=[vmem(a) for a in outs],
        scratch_shapes=[pltpu.VMEM((2 * W, W), F32), pltpu.VMEM((W, W), F32)],
        compiler_params=pltpu.CompilerParams(vmem_limit_bytes=VMEM_LIMIT),
        name="solve",
    )(core, mine, other)


def filter_kernel(mask_ref, gain_ref, mean_ref, cube_ref, out_ref, valid):
    bands = cube_ref.shape[2]
    fill_validity(mask_ref, pl.program_id(0), valid)
    mean = mean_ref[:, :bands]
    high_gain = gain_ref[:bands, :bands]
    low_gain = gain_ref[:bands, W : W + bands]
    for r in range(ROWS):
        pixel = cube_ref[r]
        high, low = split(pixel - mean)
        shifted = dot(high, high_gain) + dot(high, low_gain) + dot(low, high_gain)
        out_ref[r] = valid[:, :bands] * (pixel - shifted)


def apply_filter(cube, mask, gain, mean):
    rows, cols, bands = cube.shape
    return pl.pallas_call(
        filter_kernel,
        out_shape=jax.ShapeDtypeStruct(cube.shape, F32),
        grid=(rows // ROWS,),
        in_specs=[
            pl.BlockSpec(memory_space=pltpu.SMEM),
            pl.BlockSpec(gain.shape, lambda i: (0, 0)),
            pl.BlockSpec(mean.shape, lambda i: (0, 0)),
            pl.BlockSpec((ROWS, cols, bands), lambda i: (i, 0, 0)),
        ],
        out_specs=pl.BlockSpec((ROWS, cols, bands), lambda i: (i, 0, 0)),
        scratch_shapes=[pltpu.VMEM((cols, W), F32)],
        compiler_params=pltpu.CompilerParams(vmem_limit_bytes=VMEM_LIMIT),
        cost_estimate=pl.CostEstimate(flops=3 * 2 * rows * cols * W * W, bytes_accessed=8 * rows * cols * W, transcendentals=0),
        name="filter",
    )(mask, gain, mean, cube)


def ring(x, axis, length, stride, by):
    pairs = []
    for i in range(lax.axis_size(axis)):
        place = i // stride % length
        pairs.append((i, i + ((place + by) % length - place) * stride))
    return lax.ppermute(x, axis, pairs)


def ring_sum(x, axis, length, stride):
    return x + ring(x, axis, length, stride, 1) + ring(x, axis, length, stride, 2) + ring(x, axis, length, stride, 3)


def per_device(cube, mask):
    bands = cube.shape[2]
    size = lax.axis_size("track")
    first = jnp.repeat(mask[0].astype(F32), TILE)[:, None]
    row = jnp.concatenate([cube[0], first], 1)
    below = lax.ppermute(row, "track", [(i, i - 1) for i in range(1, size)])
    core = (lax.axis_index("strip") % 2).astype(jnp.int32)[None]
    pixel, pair = grams(cube, mask)
    mine, other = pack(core, cube, mask, below, pixel, pair)
    total = mine + ring(other, "strip", 2, 1, 1)
    total = ring_sum(total, "strip", 4, 2)
    total = ring_sum(total, "track", 4, 4)
    total = ring_sum(total, "track", 4, 1)
    gain, mean = solve(core, total, ring(total, "strip", 2, 1, 1), bands)
    return apply_filter(cube, mask, gain, mean)


def solution(mesh):
    return jax.shard_map(
        per_device,
        mesh=mesh,
        in_specs=(P("track", "strip", None), P("track", "strip")),
        out_specs=P("track", "strip", None),
        check_vma=False,
    )
```

```python
import functools

import jax
import jax.numpy as jnp
from jax import lax
from jax.experimental import pallas as pl
from jax.experimental.pallas import tpu as pltpu
from jax.sharding import PartitionSpec as P

TILE = 8
W = 256
F32 = jnp.float32
BF16 = jnp.bfloat16
MIB = 2**20


def split(x):
    high = x.astype(BF16)
    return high, (x - high.astype(F32)).astype(BF16)


def split3(x):
    high = x.astype(BF16)
    rest = x - high.astype(F32)
    middle = rest.astype(BF16)
    return high, middle, (rest - middle.astype(F32)).astype(BF16)


def dot(a, b):
    return lax.dot_general(a, b, (((1,), (0,)), ((), ())), preferred_element_type=F32)


def dot_t(a, b):
    return lax.dot_general(a, b, (((0,), (0,)), ((), ())), preferred_element_type=F32)


def dot3(a, b):
    a_high, a_low = split(a)
    b_high, b_low = split(b)
    return dot(
        jnp.concatenate([a_high, a_high, a_low], 1),
        jnp.concatenate([b_high, b_low, b_high], 0),
    )


def dot6(a, b):
    ah, am, al = split3(a)
    bh, bm, bl = split3(b)
    return dot(
        jnp.concatenate([ah, ah, am, ah, am, al], 1),
        jnp.concatenate([bh, bm, bh, bl, bm, bh], 0),
    )


def in_vmem():
    return pl.BlockSpec(memory_space=pltpu.VMEM)


def in_hbm():
    return pl.BlockSpec(memory_space=pltpu.HBM)


def params(mib):
    return pltpu.CompilerParams(vmem_limit_bytes=mib * MIB)


def fill_validity(mask_ref, tile_row, out_ref):
    for c in range(out_ref.shape[0] // TILE):
        value = mask_ref[tile_row, c].astype(F32)
        out_ref[c * TILE : (c + 1) * TILE, :] = jnp.full((TILE, out_ref.shape[1]), value, F32)


def first_row_kernel(mask_hbm, cube_hbm, out_ref, mask, row, sems):
    bands = row.shape[2]
    copies = [
        pltpu.make_async_copy(mask_hbm, mask, sems.at[0]),
        pltpu.make_async_copy(cube_hbm.at[pl.ds(0, 1)], row, sems.at[1]),
    ]
    for copy in copies:
        copy.start()
    for copy in copies:
        copy.wait()
    fill_validity(mask, 0, out_ref)
    out_ref[:, :bands] = row[0]


def first_row(mask, cube):
    _, cols, bands = cube.shape
    return pl.pallas_call(
        first_row_kernel,
        out_shape=pltpu.VMEM((cols, W), F32),
        in_specs=[in_hbm(), in_hbm()],
        out_specs=in_vmem(),
        scratch_shapes=[
            pltpu.SMEM(mask.shape, jnp.int32),
            pltpu.VMEM((1, cols, bands), F32),
            pltpu.SemaphoreType.DMA((2,)),
        ],
        compiler_params=params(46),
        name="first_row",
    )(mask, cube)


GROUP = 4


def moments_kernel(
    mask_hbm, cube_hbm, halves_ref, valid_ref, last_ref, pixel_ref, pair_ref, rest_ref, mask, raw, seam, pairs_a, pairs_b, sems
):
    rows, cols, bands = raw.shape
    groups = rows // GROUP

    def fetch(g):
        at = pl.ds(g * GROUP, GROUP)
        return pltpu.make_async_copy(cube_hbm.at[at], raw.at[at], sems.at[g])

    mask_copy = pltpu.make_async_copy(mask_hbm, mask, sems.at[groups])
    mask_copy.start()
    for g in range(groups):
        fetch(g).start()
    pixel_ref[...] = jnp.zeros_like(pixel_ref)
    pair_ref[...] = jnp.zeros_like(pair_ref)
    for buffer in (halves_ref, pairs_a, pairs_b):
        count = buffer.shape[0]
        buffer[:, bands:W] = jnp.ones((count, W - bands), BF16)
        buffer[:, W + bands :] = jnp.zeros((count, W - bands), BF16)
    mask_copy.wait()

    def put(value, buffer, r, squares):
        high = value.astype(BF16)
        rest = value - high.astype(F32)
        buffer[r * cols : (r + 1) * cols, :bands] = high
        buffer[r * cols : (r + 1) * cols, W : W + bands] = rest.astype(BF16)
        return squares + jnp.sum((rest * rest).reshape(cols // 8, 8, bands), 0)

    def products(halves, pairs):
        pixel_ref[...] += dot_t(halves[:, :W], halves[...])
        pair_ref[...] += dot_t(pairs[:, :W], pairs[...])

    squares = [jnp.zeros((8, bands), F32)] * 2
    previous = None
    pending = None
    for g in range(groups):
        pairs = (pairs_a, pairs_b)[g % 2]
        halves = halves_ref.at[pl.ds(g * GROUP * cols, GROUP * cols)]
        if pending is not None:
            products(*pending)
        fetch(g).wait()
        for r in range(GROUP):
            row = g * GROUP + r
            valid = valid_ref.at[row // TILE]
            if row % TILE == 0:
                fill_validity(mask, row // TILE, valid)
                if row:
                    seam[...] = valid_ref[row // TILE - 1] * valid[...]
            pixel = raw[row] * valid[:, :bands]
            if row == 0:
                difference = jnp.zeros_like(pixel)
            elif row % TILE == 0:
                difference = (pixel - previous) * seam[:, :bands]
            else:
                difference = pixel - previous
            previous = pixel
            squares[0] = put(pixel, halves, r, squares[0])
            squares[1] = put(difference, pairs, r, squares[1])
        pending = (halves, pairs)
    products(*pending)
    last_ref[...] = previous
    for k in range(2):
        rest_ref[k, :, :bands] = squares[k]
        rest_ref[k, :, bands:] = jnp.zeros((8, W - bands), F32)


def moments(mask, cube):
    rows, cols, bands = cube.shape
    pixels = rows * cols
    return pl.pallas_call(
        moments_kernel,
        out_shape=[
            pltpu.VMEM((pixels, 2 * W), BF16),
            pltpu.VMEM((rows // TILE, cols, W), F32),
            pltpu.VMEM((cols, bands), F32),
            pltpu.VMEM((W, 2 * W), F32),
            pltpu.VMEM((W, 2 * W), F32),
            pltpu.VMEM((2, 8, W), F32),
        ],
        in_specs=[in_hbm(), in_hbm()],
        out_specs=[in_vmem()] * 6,
        scratch_shapes=[
            pltpu.SMEM(mask.shape, jnp.int32),
            pltpu.VMEM(cube.shape, F32),
            pltpu.VMEM((cols, W), F32),
            pltpu.VMEM((GROUP * cols, 2 * W), BF16),
            pltpu.VMEM((GROUP * cols, 2 * W), BF16),
            pltpu.SemaphoreType.DMA((rows // GROUP + 1,)),
        ],
        compiler_params=params(40),
        cost_estimate=pl.CostEstimate(flops=4 * 2 * pixels * W * W, bytes_accessed=4 * pixels * W, transcendentals=0),
        name="moments",
    )(mask, cube)


def indices(shape):
    return lax.broadcasted_iota(jnp.int32, shape, 0), lax.broadcasted_iota(jnp.int32, shape, 1)


def pack_kernel(
    core_ref, valid_ref, last_ref, below_ref, pixel_ref, pair_ref, rest_ref, mine_ref, other_ref, packed, buffer
):
    bands = last_ref.shape[1]
    half = bands // 2
    row, column = indices((W, W))
    on_diagonal = row == column
    last_valid = valid_ref[valid_ref.shape[0] - 1]
    weight = last_valid * jnp.broadcast_to(below_ref[:, bands : bands + 1], last_valid.shape)
    difference = (below_ref[:, :bands] - last_ref[...]) * weight[:, :bands]
    high, low = split(difference)
    rest = difference - high.astype(F32)
    buffer[:, bands:W] = jnp.ones((buffer.shape[0], W - bands), BF16)
    buffer[:, W + bands :] = jnp.zeros((buffer.shape[0], W - bands), BF16)
    buffer[:, :bands] = high
    buffer[:, W : W + bands] = low
    pairs = pair_ref[...] + dot_t(buffer[:, :W], buffer[...])
    squares = jnp.sum(rest * rest, 0, keepdims=True)

    def whole(parts, squares):
        mixed = parts[:, W:]
        squares = jnp.concatenate([squares, jnp.zeros((1, W - bands), F32)], 1)
        return parts[:, :W] + mixed + mixed.T + jnp.where(on_diagonal, squares, 0.0)

    pixel = whole(pixel_ref[...], jnp.sum(rest_ref[0, :, :bands], 0, keepdims=True))
    pair = whole(pairs, squares + jnp.sum(rest_ref[1, :, :bands], 0, keepdims=True))
    valid = valid_ref[:, :, :128]
    inner = jnp.sum(valid, 0)
    seams = jnp.sum(valid[1:] * valid[:-1], 0)
    pixel_count = TILE * jnp.sum(inner, 0, keepdims=True)
    pair_count = jnp.sum((TILE - 1) * inner + seams + weight[:, :128], 0, keepdims=True)
    out = jnp.where(column <= row, pair, 0.0)
    out = jnp.where((column > row) & (column <= bands + 1), pltpu.roll(pixel, 1, 1), out)
    out = jnp.where(column == bands + 2, pltpu.roll(pair, 2, 1), out)
    counts = jnp.where(row == 0, pixel_count[:, :1], 0.0)
    counts = jnp.where(row == 1, pair_count[:, :1], counts)
    packed[...] = jnp.where(column == bands + 3, counts, out)
    core = core_ref[0]
    mine_ref[...] = packed[pl.ds(pl.multiple_of(core * half, 8), half), :]
    other_ref[...] = packed[pl.ds(pl.multiple_of((1 - core) * half, 8), half), :]


def pack(core, valid, last, below, pixel, pair, rest):
    cols, bands = last.shape
    half = pltpu.VMEM((bands // 2, W), F32)
    return pl.pallas_call(
        pack_kernel,
        out_shape=[half, half],
        in_specs=[pl.BlockSpec(memory_space=pltpu.SMEM)] + [in_vmem()] * 6,
        out_specs=[in_vmem()] * 2,
        scratch_shapes=[pltpu.VMEM((W, W), F32), pltpu.VMEM((cols, 2 * W), BF16)],
        compiler_params=params(12),
        name="pack",
    )(core, valid, last, below, pixel, pair, rest)


def square_sum(x):
    return jnp.sum(x * x)


def solve_kernel(bands, core_ref, mine_ref, other_ref, weights_ref, left, right):
    core = core_ref[0]
    packed = jnp.concatenate([mine_ref[...], other_ref[...]], 0)
    swapped = jnp.concatenate([other_ref[...], mine_ref[...]], 0)
    packed = jnp.where(core == 0, packed, swapped)
    packed = jnp.concatenate([packed, jnp.zeros((W - bands, W), F32)], 0)
    row, column = indices((W, W))
    on_diagonal = row == column
    inside = (row < bands) & (column < bands)
    pixel_count = packed[0:1, bands + 3 : bands + 4]
    pair_count = packed[1:2, bands + 3 : bands + 4]

    def whole(triangle):
        return triangle + triangle.T - jnp.where(on_diagonal, triangle, 0.0)

    pixel = whole(jnp.where((column >= row) & (column <= bands), pltpu.roll(packed, W - 1, 1), 0.0))
    lower = jnp.where((column <= row) & inside, packed, 0.0)
    sums = jnp.where((column == bands) & (row < bands), pltpu.roll(packed, W - 2, 1), 0.0)
    pair = whole(lower + sums)

    def covariance(square, count):
        total = square[bands : bands + 1, :]
        total_rows = square[:, bands : bands + 1]
        return jnp.where(inside, (square - total_rows * total / count) / (count - 1.0), 0.0)

    signal = covariance(pixel, pixel_count)
    noise = covariance(pair, pair_count)
    combined = signal + noise
    mean = pixel[:, bands : bands + 1] / pixel_count
    diagonal = jnp.where(on_diagonal, combined, 0.0)
    scale_row = lax.rsqrt(jnp.where(column[0:1] < bands, jnp.sum(diagonal, 0, keepdims=True), 1.0))
    scale_column = lax.rsqrt(jnp.where(row[:, 0:1] < bands, jnp.sum(diagonal, 1, keepdims=True), 1.0))
    identity = jnp.where(on_diagonal, 1.0, 0.0)
    matrix = jnp.where(inside, combined * scale_column * scale_row, identity)
    target = noise * scale_column * scale_row

    start = 1.0 / jnp.max(jnp.sum(jnp.abs(matrix), 1, keepdims=True))
    left[:W, :] = start * identity
    left[W:, :] = identity - start * matrix

    def more(carry):
        count, size = carry
        return (count < 24) & (size > 4e-6)

    def squaring(carry):
        count, _ = carry
        new = dot3(left[...], left[W:, :])
        left[:W, :] = left[:W, :] + new[:W]
        left[W:, :] = new[W:]
        return count + 1, square_sum(new[W:])

    lax.while_loop(more, squaring, (0, jnp.float32(1e9)))
    right[...] = dot3(left[:W, :], target)

    def refining(carry):
        count, _ = carry
        residual = target - dot6(matrix, right[...])
        change = dot3(left[:W, :], residual)
        gain = right[...] + change
        right[...] = gain
        return count + 1, square_sum(change) / square_sum(gain)

    def rough(carry):
        count, size = carry
        return (count < 8) & jnp.logical_not(size <= 1e-6)

    _, size = lax.while_loop(rough, refining, (0, jnp.float32(1e9)))

    @pl.when(jnp.logical_not(size <= 1e-6))
    def _():
        left[:W, :] = matrix
        right[...] = target

        def eliminate(k, _):
            here = row[:, 0:1] == k
            pivot_left = left[pl.ds(k, 1), :]
            pivot_right = right[pl.ds(k, 1), :]
            values = jnp.sum(jnp.where(column == k, left[:W, :], 0.0), 1, keepdims=True)
            pivot = jnp.sum(jnp.where(here, values, 0.0))
            factor = jnp.where(here, (values - 1.0) / pivot, values / pivot)
            left[:W, :] = left[:W, :] - factor * pivot_left
            right[...] = right[...] - factor * pivot_right
            return 0

        lax.fori_loop(0, bands, eliminate, 0)

    gain = right[...] * scale_column * (1.0 / scale_row)
    shift = jnp.sum(jnp.where(row < bands, mean, 0.0) * gain, 0, keepdims=True)
    weights = jnp.where(row == bands, shift, jnp.where(inside, identity - gain, 0.0))
    high, low = split(weights)
    weights_ref[:W, :] = high
    weights_ref[W : 2 * W, :] = high
    weights_ref[2 * W :, :] = low


def solve(core, mine, other, bands):
    return pl.pallas_call(
        functools.partial(solve_kernel, bands),
        out_shape=pltpu.VMEM((3 * W, W), BF16),
        in_specs=[pl.BlockSpec(memory_space=pltpu.SMEM), in_vmem(), in_vmem()],
        out_specs=in_vmem(),
        scratch_shapes=[pltpu.VMEM((2 * W, W), F32), pltpu.VMEM((W, W), F32)],
        compiler_params=params(16),
        name="solve",
    )(core, mine, other)


def filter_kernel(halves_ref, valid_ref, weights_ref, out_hbm, staged, sems):
    slots, group, cols, bands = staged.shape
    groups = out_hbm.shape[0] // group

    def send(g):
        return pltpu.make_async_copy(staged.at[g % slots], out_hbm.at[pl.ds(g * group, group)], sems.at[g % slots])

    for g in range(groups):
        if g >= slots:
            send(g - slots).wait()
        halves = halves_ref[g * group * cols : (g + 1) * group * cols, :]
        result = dot(jnp.concatenate([halves, halves[:, :W]], 1), weights_ref[...])
        valid = valid_ref[g * group // TILE]
        for r in range(group):
            staged[g % slots, r] = valid[:, :bands] * result[r * cols : (r + 1) * cols, :bands]
        send(g).start()
    for g in range(groups - slots, groups):
        send(g).wait()


def apply_filter(halves, valid, weights, shape):
    rows, cols, bands = shape
    group, slots = 4, 4
    pixels = rows * cols
    return pl.pallas_call(
        filter_kernel,
        out_shape=jax.ShapeDtypeStruct(shape, F32),
        in_specs=[in_vmem()] * 3,
        out_specs=in_hbm(),
        scratch_shapes=[pltpu.VMEM((slots, group, cols, bands), F32), pltpu.SemaphoreType.DMA((slots,))],
        compiler_params=params(24),
        cost_estimate=pl.CostEstimate(flops=3 * 2 * pixels * W * W, bytes_accessed=4 * pixels * W, transcendentals=0),
        name="filter",
    )(halves, valid, weights)


RING = 4


def permute(x, target):
    track, strip = lax.axis_size("track"), lax.axis_size("strip")
    pairs = []
    for i in range(track):
        for j in range(strip):
            y, z, chip, core = target(i // RING, i % RING, j // 2, j % 2)
            pairs.append((i * strip + j, (y * RING + z) * strip + chip * 2 + core))
    return lax.ppermute(x, ("track", "strip"), pairs)


def other_core(x):
    return permute(x, lambda y, z, chip, core: (y, z, chip, 1 - core))


def ring_sum(x, axes):
    def moved(by):
        def target(y, z, chip, core):
            place = [y, z, chip]
            axis = axes[core]
            place[axis] = (place[axis] + (by if core == 0 else -by)) % RING
            return (*place, core)

        return permute(x, target)

    return lax.optimization_barrier(x + moved(1) + moved(3) + moved(2))


def per_device(cube, mask):
    bands = cube.shape[2]
    size = lax.axis_size("track")
    below = lax.ppermute(first_row(mask, cube), "track", [(i, i - 1) for i in range(1, size)])
    core = (lax.axis_index("strip") % 2).astype(jnp.int32)[None]
    halves, valid, last, pixel, pair, rest = moments(mask, cube)
    mine, other = pack(core, valid, last, below, pixel, pair, rest)
    total = mine + other_core(other)
    for axes in ((0, 1), (1, 2), (2, 0)):
        total = ring_sum(total, axes)
    weights = solve(core, total, other_core(total), bands)
    return apply_filter(halves, valid, weights, cube.shape)


def solution(mesh):
    return jax.shard_map(
        per_device,
        mesh=mesh,
        in_specs=(P("track", "strip", None), P("track", "strip")),
        out_specs=P("track", "strip", None),
        check_vma=False,
    )
```

```python
import functools

import jax
import jax.numpy as jnp
from jax import lax
from jax.experimental import pallas as pl
from jax.experimental.pallas import tpu as pltpu
from jax.sharding import PartitionSpec as P

TILE = 8
W = 256
F32 = jnp.float32
BF16 = jnp.bfloat16
MIB = 2**20


def split(x):
    high = x.astype(BF16)
    return high, (x - high.astype(F32)).astype(BF16)


def split3(x):
    high = x.astype(BF16)
    rest = x - high.astype(F32)
    middle = rest.astype(BF16)
    return high, middle, (rest - middle.astype(F32)).astype(BF16)


def dot(a, b):
    return lax.dot_general(a, b, (((1,), (0,)), ((), ())), preferred_element_type=F32)


def dot_t(a, b):
    return lax.dot_general(a, b, (((0,), (0,)), ((), ())), preferred_element_type=F32)


def dot3(a, b):
    a_high, a_low = split(a)
    b_high, b_low = split(b)
    return dot(
        jnp.concatenate([a_high, a_high, a_low], 1),
        jnp.concatenate([b_high, b_low, b_high], 0),
    )


def dot6(a, b):
    ah, am, al = split3(a)
    bh, bm, bl = split3(b)
    return dot(
        jnp.concatenate([ah, ah, am, ah, am, al], 1),
        jnp.concatenate([bh, bm, bh, bl, bm, bh], 0),
    )


def in_vmem():
    return pl.BlockSpec(memory_space=pltpu.VMEM)


def in_hbm():
    return pl.BlockSpec(memory_space=pltpu.HBM)


def params(mib):
    return pltpu.CompilerParams(vmem_limit_bytes=mib * MIB)


def fill_validity(mask_ref, tile_row, out_ref):
    for c in range(out_ref.shape[0] // TILE):
        value = mask_ref[tile_row, c].astype(F32)
        out_ref[c * TILE : (c + 1) * TILE, :] = jnp.full((TILE, out_ref.shape[1]), value, F32)


def first_row_kernel(mask_hbm, cube_hbm, out_ref, mask, row, sems):
    bands = row.shape[2]
    copies = [
        pltpu.make_async_copy(mask_hbm, mask, sems.at[0]),
        pltpu.make_async_copy(cube_hbm.at[pl.ds(0, 1)], row, sems.at[1]),
    ]
    for copy in copies:
        copy.start()
    for copy in copies:
        copy.wait()
    fill_validity(mask, 0, out_ref)
    out_ref[:, :bands] = row[0]


def first_row(mask, cube):
    _, cols, bands = cube.shape
    return pl.pallas_call(
        first_row_kernel,
        out_shape=pltpu.VMEM((cols, W), F32),
        in_specs=[in_hbm(), in_hbm()],
        out_specs=in_vmem(),
        scratch_shapes=[
            pltpu.SMEM(mask.shape, jnp.int32),
            pltpu.VMEM((1, cols, bands), F32),
            pltpu.SemaphoreType.DMA((2,)),
        ],
        compiler_params=params(46),
        name="first_row",
    )(mask, cube)


GROUP = 4
BLOCK = 64


def moments_kernel(
    mask_hbm, cube_hbm, halves_ref, valid_ref, last_ref, pixel_ref, pair_ref, rest_ref, mask, raw, pairs_a, pairs_b, sems
):
    rows, cols, bands = raw.shape
    groups = rows // GROUP

    def fetch(g):
        at = pl.ds(g * GROUP, GROUP)
        return pltpu.make_async_copy(cube_hbm.at[at], raw.at[at], sems.at[g])

    mask_copy = pltpu.make_async_copy(mask_hbm, mask, sems.at[groups])
    mask_copy.start()
    for g in range(groups):
        fetch(g).start()
    pixel_ref[...] = jnp.zeros_like(pixel_ref)
    pair_ref[...] = jnp.zeros_like(pair_ref)
    for buffer in (halves_ref, pairs_a, pairs_b):
        count = buffer.shape[0]
        buffer[:, bands:W] = jnp.ones((count, W - bands), BF16)
        buffer[:, W + bands :] = jnp.zeros((count, W - bands), BF16)
    mask_copy.wait()

    def put(value, buffer, at, lanes, squares):
        count = value.shape[0]
        high = value.astype(BF16)
        low = (value - high.astype(F32)).astype(BF16)
        buffer[at : at + count, lanes] = high
        buffer[at : at + count, slice(W + lanes.start, W + lanes.stop)] = low
        parts = (low * low).reshape(count // 16, 16, -1)
        total = parts[0]
        for k in range(1, count // 16):
            total = total + parts[k]
        return squares + jnp.sum(total.astype(F32).reshape(2, 8, -1), 0)

    def product(ref, buffer, half):
        at = slice(half * W, (half + 1) * W)
        ref[:, at] += dot_t(buffer[:, :W], buffer[:, at])

    def products(halves, pairs):
        return [(pixel_ref, halves, 0), (pixel_ref, halves, 1), (pair_ref, pairs, 0), (pair_ref, pairs, 1)]

    lane_halves = (slice(0, 128), slice(128, bands))
    squares = {(k, h): jnp.zeros((8, lanes.stop - lanes.start), F32) for k in range(2) for h, lanes in enumerate(lane_halves)}
    pending = []
    for g in range(groups):
        pairs = (pairs_a, pairs_b)[g % 2]
        halves = halves_ref.at[pl.ds(g * GROUP * cols, GROUP * cols)]
        fetch(g).wait()
        tile_row, within = divmod(g * GROUP, TILE)
        if within == 0:
            fill_validity(mask, tile_row, valid_ref.at[tile_row])
        for c in range(0, cols, BLOCK):
            if pending:
                product(*pending.pop(0))
            block = slice(c, c + BLOCK)
            valid = valid_ref[tile_row, block, :128]
            for h, lanes in enumerate(lane_halves):
                weight = valid[:, : lanes.stop - lanes.start]
                previous = last_ref[block, lanes] if g else None
                for r in range(GROUP):
                    pixel = raw[g * GROUP + r, block, lanes] * weight
                    if previous is None:
                        difference = jnp.zeros_like(pixel)
                    else:
                        difference = pixel - previous
                        if within == 0 and r == 0:
                            difference = difference * (valid_ref[tile_row - 1, block, : weight.shape[1]] * weight)
                    previous = pixel
                    squares[0, h] = put(pixel, halves, r * cols + c, lanes, squares[0, h])
                    squares[1, h] = put(difference, pairs, r * cols + c, lanes, squares[1, h])
                last_ref[block, lanes] = previous
        for late in pending:
            product(*late)
        pending = products(halves, pairs)
    for late in pending:
        product(*late)
    for k in range(2):
        rest_ref[k, :, bands:] = jnp.zeros((8, W - bands), F32)
        for h, lanes in enumerate(lane_halves):
            rest_ref[k, :, lanes] = squares[k, h]


def moments(mask, cube):
    rows, cols, bands = cube.shape
    pixels = rows * cols
    return pl.pallas_call(
        moments_kernel,
        out_shape=[
            pltpu.VMEM((pixels, 2 * W), BF16),
            pltpu.VMEM((rows // TILE, cols, W), F32),
            pltpu.VMEM((cols, bands), F32),
            pltpu.VMEM((W, 2 * W), F32),
            pltpu.VMEM((W, 2 * W), F32),
            pltpu.VMEM((2, 8, W), F32),
        ],
        in_specs=[in_hbm(), in_hbm()],
        out_specs=[in_vmem()] * 6,
        scratch_shapes=[
            pltpu.SMEM(mask.shape, jnp.int32),
            pltpu.VMEM(cube.shape, F32),
            pltpu.VMEM((GROUP * cols, 2 * W), BF16),
            pltpu.VMEM((GROUP * cols, 2 * W), BF16),
            pltpu.SemaphoreType.DMA((rows // GROUP + 1,)),
        ],
        compiler_params=params(40),
        cost_estimate=pl.CostEstimate(flops=4 * 2 * pixels * W * W, bytes_accessed=4 * pixels * W, transcendentals=0),
        name="moments",
    )(mask, cube)


def indices(shape):
    return lax.broadcasted_iota(jnp.int32, shape, 0), lax.broadcasted_iota(jnp.int32, shape, 1)


def pack_kernel(
    core_ref, valid_ref, last_ref, below_ref, pixel_ref, pair_ref, rest_ref, mine_ref, other_ref, packed, buffer
):
    bands = last_ref.shape[1]
    half = bands // 2
    row, column = indices((W, W))
    on_diagonal = row == column
    last_valid = valid_ref[valid_ref.shape[0] - 1]
    weight = last_valid * jnp.broadcast_to(below_ref[:, bands : bands + 1], last_valid.shape)
    difference = (below_ref[:, :bands] - last_ref[...]) * weight[:, :bands]
    high, low = split(difference)
    rest = difference - high.astype(F32)
    buffer[:, bands:W] = jnp.ones((buffer.shape[0], W - bands), BF16)
    buffer[:, W + bands :] = jnp.zeros((buffer.shape[0], W - bands), BF16)
    buffer[:, :bands] = high
    buffer[:, W : W + bands] = low
    pairs = pair_ref[...] + dot_t(buffer[:, :W], buffer[...])
    squares = jnp.sum(rest * rest, 0, keepdims=True)

    def whole(parts, squares):
        mixed = parts[:, W:]
        squares = jnp.concatenate([squares, jnp.zeros((1, W - bands), F32)], 1)
        return parts[:, :W] + mixed + mixed.T + jnp.where(on_diagonal, squares, 0.0)

    pixel = whole(pixel_ref[...], jnp.sum(rest_ref[0, :, :bands], 0, keepdims=True))
    pair = whole(pairs, squares + jnp.sum(rest_ref[1, :, :bands], 0, keepdims=True))
    valid = valid_ref[:, :, :128]
    inner = jnp.sum(valid, 0)
    seams = jnp.sum(valid[1:] * valid[:-1], 0)
    pixel_count = TILE * jnp.sum(inner, 0, keepdims=True)
    pair_count = jnp.sum((TILE - 1) * inner + seams + weight[:, :128], 0, keepdims=True)
    out = jnp.where(column <= row, pair, 0.0)
    out = jnp.where((column > row) & (column <= bands + 1), pltpu.roll(pixel, 1, 1), out)
    out = jnp.where(column == bands + 2, pltpu.roll(pair, 2, 1), out)
    counts = jnp.where(row == 0, pixel_count[:, :1], 0.0)
    counts = jnp.where(row == 1, pair_count[:, :1], counts)
    packed[...] = jnp.where(column == bands + 3, counts, out)
    core = core_ref[0]
    mine_ref[...] = packed[pl.ds(pl.multiple_of(core * half, 8), half), :]
    other_ref[...] = packed[pl.ds(pl.multiple_of((1 - core) * half, 8), half), :]


def pack(core, valid, last, below, pixel, pair, rest):
    cols, bands = last.shape
    half = pltpu.VMEM((bands // 2, W), F32)
    return pl.pallas_call(
        pack_kernel,
        out_shape=[half, half],
        in_specs=[pl.BlockSpec(memory_space=pltpu.SMEM)] + [in_vmem()] * 6,
        out_specs=[in_vmem()] * 2,
        scratch_shapes=[pltpu.VMEM((W, W), F32), pltpu.VMEM((cols, 2 * W), BF16)],
        compiler_params=params(12),
        name="pack",
    )(core, valid, last, below, pixel, pair, rest)


def square_sum(x):
    return jnp.sum(x * x)


def solve_kernel(bands, core_ref, mine_ref, other_ref, weights_ref, left, right):
    core = core_ref[0]
    packed = jnp.concatenate([mine_ref[...], other_ref[...]], 0)
    swapped = jnp.concatenate([other_ref[...], mine_ref[...]], 0)
    packed = jnp.where(core == 0, packed, swapped)
    packed = jnp.concatenate([packed, jnp.zeros((W - bands, W), F32)], 0)
    row, column = indices((W, W))
    on_diagonal = row == column
    inside = (row < bands) & (column < bands)
    pixel_count = packed[0:1, bands + 3 : bands + 4]
    pair_count = packed[1:2, bands + 3 : bands + 4]

    def whole(triangle):
        return triangle + triangle.T - jnp.where(on_diagonal, triangle, 0.0)

    pixel = whole(jnp.where((column >= row) & (column <= bands), pltpu.roll(packed, W - 1, 1), 0.0))
    lower = jnp.where((column <= row) & inside, packed, 0.0)
    sums = jnp.where((column == bands) & (row < bands), pltpu.roll(packed, W - 2, 1), 0.0)
    pair = whole(lower + sums)

    def covariance(square, count):
        total = square[bands : bands + 1, :]
        total_rows = square[:, bands : bands + 1]
        return jnp.where(inside, (square - total_rows * total / count) / (count - 1.0), 0.0)

    signal = covariance(pixel, pixel_count)
    noise = covariance(pair, pair_count)
    combined = signal + noise
    mean = pixel[:, bands : bands + 1] / pixel_count
    diagonal = jnp.where(on_diagonal, combined, 0.0)
    scale_row = lax.rsqrt(jnp.where(column[0:1] < bands, jnp.sum(diagonal, 0, keepdims=True), 1.0))
    scale_column = lax.rsqrt(jnp.where(row[:, 0:1] < bands, jnp.sum(diagonal, 1, keepdims=True), 1.0))
    identity = jnp.where(on_diagonal, 1.0, 0.0)
    matrix = jnp.where(inside, combined * scale_column * scale_row, identity)
    target = noise * scale_column * scale_row

    start = 1.0 / jnp.max(jnp.sum(jnp.abs(matrix), 1, keepdims=True))
    left[:W, :] = start * identity
    left[W:, :] = identity - start * matrix

    def more(carry):
        count, size = carry
        return (count < 24) & (size > 4e-6)

    def squaring(carry):
        count, _ = carry
        new = dot3(left[...], left[W:, :])
        left[:W, :] = left[:W, :] + new[:W]
        left[W:, :] = new[W:]
        return count + 1, square_sum(new[W:])

    lax.while_loop(more, squaring, (0, jnp.float32(1e9)))
    right[...] = dot3(left[:W, :], target)

    def refining(carry):
        count, _ = carry
        residual = target - dot6(matrix, right[...])
        change = dot3(left[:W, :], residual)
        gain = right[...] + change
        right[...] = gain
        return count + 1, square_sum(change) / square_sum(gain)

    def rough(carry):
        count, size = carry
        return (count < 8) & jnp.logical_not(size <= 1e-6)

    _, size = lax.while_loop(rough, refining, (0, jnp.float32(1e9)))

    @pl.when(jnp.logical_not(size <= 1e-6))
    def _():
        left[:W, :] = matrix
        right[...] = target

        def eliminate(k, _):
            here = row[:, 0:1] == k
            pivot_left = left[pl.ds(k, 1), :]
            pivot_right = right[pl.ds(k, 1), :]
            values = jnp.sum(jnp.where(column == k, left[:W, :], 0.0), 1, keepdims=True)
            pivot = jnp.sum(jnp.where(here, values, 0.0))
            factor = jnp.where(here, (values - 1.0) / pivot, values / pivot)
            left[:W, :] = left[:W, :] - factor * pivot_left
            right[...] = right[...] - factor * pivot_right
            return 0

        lax.fori_loop(0, bands, eliminate, 0)

    gain = right[...] * scale_column * (1.0 / scale_row)
    shift = jnp.sum(jnp.where(row < bands, mean, 0.0) * gain, 0, keepdims=True)
    weights = jnp.where(row == bands, shift, jnp.where(inside, identity - gain, 0.0))
    high, low = split(weights)
    weights_ref[:W, :] = high
    weights_ref[W : 2 * W, :] = high
    weights_ref[2 * W :, :] = low


def solve(core, mine, other, bands):
    return pl.pallas_call(
        functools.partial(solve_kernel, bands),
        out_shape=pltpu.VMEM((3 * W, W), BF16),
        in_specs=[pl.BlockSpec(memory_space=pltpu.SMEM), in_vmem(), in_vmem()],
        out_specs=in_vmem(),
        scratch_shapes=[pltpu.VMEM((2 * W, W), F32), pltpu.VMEM((W, W), F32)],
        compiler_params=params(16),
        name="solve",
    )(core, mine, other)


def filter_kernel(halves_ref, valid_ref, weights_ref, out_hbm, staged, sems):
    rows, cols, bands = staged.shape
    copies = []
    for r in range(rows):
        halves = halves_ref[r * cols : (r + 1) * cols, :]
        result = dot(jnp.concatenate([halves, halves[:, :W]], 1), weights_ref[...])
        staged[r] = valid_ref[r // TILE][:, :bands] * result[:, :bands]
        copies.append(pltpu.make_async_copy(staged.at[pl.ds(r, 1)], out_hbm.at[pl.ds(r, 1)], sems.at[r]))
        copies[-1].start()
    for copy in copies:
        copy.wait()


def apply_filter(halves, valid, weights, shape):
    rows, cols, bands = shape
    pixels = rows * cols
    return pl.pallas_call(
        filter_kernel,
        out_shape=jax.ShapeDtypeStruct(shape, F32),
        in_specs=[in_vmem()] * 3,
        out_specs=in_hbm(),
        scratch_shapes=[pltpu.VMEM(shape, F32), pltpu.SemaphoreType.DMA((rows,))],
        compiler_params=params(24),
        cost_estimate=pl.CostEstimate(flops=3 * 2 * pixels * W * W, bytes_accessed=4 * pixels * W, transcendentals=0),
        name="filter",
    )(halves, valid, weights)


RING = 4


def permute(x, target):
    track, strip = lax.axis_size("track"), lax.axis_size("strip")
    pairs = []
    for i in range(track):
        for j in range(strip):
            y, z, chip, core = target(i // RING, i % RING, j // 2, j % 2)
            pairs.append((i * strip + j, (y * RING + z) * strip + chip * 2 + core))
    return lax.ppermute(x, ("track", "strip"), pairs)


def other_core(x):
    return permute(x, lambda y, z, chip, core: (y, z, chip, 1 - core))


PARTNER = {1: (1, 0, 3, 2), 2: (2, 3, 0, 1), 3: (3, 2, 1, 0)}


def ring_sum(x, axes):
    def exchanged(which):
        def target(y, z, chip, core):
            place = [y, z, chip]
            axis = axes[core]
            place[axis] = PARTNER[which if core == 0 else RING - which][place[axis]]
            return (*place, core)

        return permute(x, target)

    return lax.optimization_barrier(x + exchanged(1) + exchanged(3) + exchanged(2))


def per_device(cube, mask):
    bands = cube.shape[2]
    size = lax.axis_size("track")
    below = lax.ppermute(first_row(mask, cube), "track", [(i, i - 1) for i in range(1, size)])
    core = (lax.axis_index("strip") % 2).astype(jnp.int32)[None]
    halves, valid, last, pixel, pair, rest = moments(mask, cube)
    mine, other = pack(core, valid, last, below, pixel, pair, rest)
    total = mine + other_core(other)
    for axes in ((0, 1), (1, 2), (2, 0)):
        total = ring_sum(total, axes)
    weights = solve(core, total, other_core(total), bands)
    return apply_filter(halves, valid, weights, cube.shape)


def solution(mesh):
    return jax.shard_map(
        per_device,
        mesh=mesh,
        in_specs=(P("track", "strip", None), P("track", "strip")),
        out_specs=P("track", "strip", None),
        check_vma=False,
    )
```

```python
import functools

import jax
import jax.numpy as jnp
from jax import lax
from jax.experimental import pallas as pl
from jax.experimental.pallas import tpu as pltpu
from jax.sharding import PartitionSpec as P

TILE = 8
W = 256
F32 = jnp.float32
BF16 = jnp.bfloat16
MIB = 2**20


def split(x):
    high = x.astype(BF16)
    return high, (x - high.astype(F32)).astype(BF16)


def split3(x):
    high = x.astype(BF16)
    rest = x - high.astype(F32)
    middle = rest.astype(BF16)
    return high, middle, (rest - middle.astype(F32)).astype(BF16)


def dot(a, b):
    return lax.dot_general(a, b, (((1,), (0,)), ((), ())), preferred_element_type=F32)


def dot_t(a, b):
    return lax.dot_general(a, b, (((0,), (0,)), ((), ())), preferred_element_type=F32)


def dot3(a, b):
    a_high, a_low = split(a)
    b_high, b_low = split(b)
    return dot(
        jnp.concatenate([a_high, a_high, a_low], 1),
        jnp.concatenate([b_high, b_low, b_high], 0),
    )


def dot6(a, b):
    ah, am, al = split3(a)
    bh, bm, bl = split3(b)
    return dot(
        jnp.concatenate([ah, ah, am, ah, am, al], 1),
        jnp.concatenate([bh, bm, bh, bl, bm, bh], 0),
    )


def in_vmem():
    return pl.BlockSpec(memory_space=pltpu.VMEM)


def in_hbm():
    return pl.BlockSpec(memory_space=pltpu.HBM)


def params(mib):
    return pltpu.CompilerParams(vmem_limit_bytes=mib * MIB)


def fill_validity(mask_ref, tile_row, out_ref):
    for c in range(out_ref.shape[0] // TILE):
        value = mask_ref[tile_row, c].astype(F32)
        out_ref[c * TILE : (c + 1) * TILE, :] = jnp.full((TILE, out_ref.shape[1]), value, F32)


def first_row_kernel(mask_hbm, cube_hbm, out_ref, mask, row, sems):
    bands = row.shape[2]
    copies = [
        pltpu.make_async_copy(mask_hbm, mask, sems.at[0]),
        pltpu.make_async_copy(cube_hbm.at[pl.ds(0, 1)], row, sems.at[1]),
    ]
    for copy in copies:
        copy.start()
    for copy in copies:
        copy.wait()
    fill_validity(mask, 0, out_ref)
    out_ref[:, :bands] = row[0]


def first_row(mask, cube):
    _, cols, bands = cube.shape
    return pl.pallas_call(
        first_row_kernel,
        out_shape=pltpu.VMEM((cols, W), F32),
        in_specs=[in_hbm(), in_hbm()],
        out_specs=in_vmem(),
        scratch_shapes=[
            pltpu.SMEM(mask.shape, jnp.int32),
            pltpu.VMEM((1, cols, bands), F32),
            pltpu.SemaphoreType.DMA((2,)),
        ],
        compiler_params=params(46),
        name="first_row",
    )(mask, cube)


GROUP = 4
BLOCK = 64


def moments_kernel(
    mask_hbm, cube_hbm, halves_ref, valid_ref, last_ref, pixel_ref, pair_ref, rest_ref, mask, raw, pairs_a, pairs_b, sems
):
    rows, cols, bands = raw.shape
    groups = rows // GROUP

    def fetch(g):
        at = pl.ds(g * GROUP, GROUP)
        return pltpu.make_async_copy(cube_hbm.at[at], raw.at[at], sems.at[g])

    mask_copy = pltpu.make_async_copy(mask_hbm, mask, sems.at[groups])
    mask_copy.start()
    for g in range(groups):
        fetch(g).start()
    pixel_ref[...] = jnp.zeros_like(pixel_ref)
    pair_ref[...] = jnp.zeros_like(pair_ref)
    for buffer in (halves_ref, pairs_a, pairs_b):
        count = buffer.shape[0]
        buffer[:, bands:W] = jnp.ones((count, W - bands), BF16)
        buffer[:, W + bands :] = jnp.zeros((count, W - bands), BF16)
    mask_copy.wait()

    def put(value, buffer, at, lanes, squares):
        count = value.shape[0]
        high = value.astype(BF16)
        low = (value - high.astype(F32)).astype(BF16)
        buffer[at : at + count, lanes] = high
        buffer[at : at + count, slice(W + lanes.start, W + lanes.stop)] = low
        parts = (low * low).reshape(count // 16, 16, -1)
        total = parts[0]
        for k in range(1, count // 16):
            total = total + parts[k]
        return squares + jnp.sum(total.astype(F32).reshape(2, 8, -1), 0)

    def product(ref, buffer, half):
        at = slice(half * W, (half + 1) * W)
        ref[:, at] += dot_t(buffer[:, :W], buffer[:, at])

    def products(halves, pairs):
        return [(pixel_ref, halves, 0), (pixel_ref, halves, 1), (pair_ref, pairs, 0), (pair_ref, pairs, 1)]

    lane_halves = (slice(0, 128), slice(128, bands))
    squares = {(k, h): jnp.zeros((8, lanes.stop - lanes.start), F32) for k in range(2) for h, lanes in enumerate(lane_halves)}
    pending = []
    for g in range(groups):
        pairs = (pairs_a, pairs_b)[g % 2]
        halves = halves_ref.at[pl.ds(g * GROUP * cols, GROUP * cols)]
        fetch(g).wait()
        tile_row, within = divmod(g * GROUP, TILE)
        if within == 0:
            fill_validity(mask, tile_row, valid_ref.at[tile_row])
        for c in range(0, cols, BLOCK):
            if pending:
                product(*pending.pop(0))
            block = slice(c, c + BLOCK)
            valid = valid_ref[tile_row, block, :128]
            for h, lanes in enumerate(lane_halves):
                weight = valid[:, : lanes.stop - lanes.start]
                previous = last_ref[block, lanes] if g else None
                for r in range(GROUP):
                    pixel = raw[g * GROUP + r, block, lanes] * weight
                    if previous is None:
                        difference = jnp.zeros_like(pixel)
                    else:
                        difference = pixel - previous
                        if within == 0 and r == 0:
                            difference = difference * (valid_ref[tile_row - 1, block, : weight.shape[1]] * weight)
                    previous = pixel
                    squares[0, h] = put(pixel, halves, r * cols + c, lanes, squares[0, h])
                    squares[1, h] = put(difference, pairs, r * cols + c, lanes, squares[1, h])
                last_ref[block, lanes] = previous
        for late in pending:
            product(*late)
        pending = products(halves, pairs)
    for late in pending:
        product(*late)
    for k in range(2):
        rest_ref[k, :, bands:] = jnp.zeros((8, W - bands), F32)
        for h, lanes in enumerate(lane_halves):
            rest_ref[k, :, lanes] = squares[k, h]


def moments(mask, cube):
    rows, cols, bands = cube.shape
    pixels = rows * cols
    return pl.pallas_call(
        moments_kernel,
        out_shape=[
            pltpu.VMEM((pixels, 2 * W), BF16),
            pltpu.VMEM((rows // TILE, cols, W), F32),
            pltpu.VMEM((cols, bands), F32),
            pltpu.VMEM((W, 2 * W), F32),
            pltpu.VMEM((W, 2 * W), F32),
            pltpu.VMEM((2, 8, W), F32),
        ],
        in_specs=[in_hbm(), in_hbm()],
        out_specs=[in_vmem()] * 6,
        scratch_shapes=[
            pltpu.SMEM(mask.shape, jnp.int32),
            pltpu.VMEM(cube.shape, F32),
            pltpu.VMEM((GROUP * cols, 2 * W), BF16),
            pltpu.VMEM((GROUP * cols, 2 * W), BF16),
            pltpu.SemaphoreType.DMA((rows // GROUP + 1,)),
        ],
        compiler_params=params(40),
        cost_estimate=pl.CostEstimate(flops=4 * 2 * pixels * W * W, bytes_accessed=4 * pixels * W, transcendentals=0),
        name="moments",
    )(mask, cube)


def indices(shape):
    return lax.broadcasted_iota(jnp.int32, shape, 0), lax.broadcasted_iota(jnp.int32, shape, 1)


def pack_kernel(
    core_ref, valid_ref, last_ref, below_ref, pixel_ref, pair_ref, rest_ref, mine_ref, other_ref, packed, buffer
):
    bands = last_ref.shape[1]
    half = bands // 2
    row, column = indices((W, W))
    on_diagonal = row == column
    last_valid = valid_ref[valid_ref.shape[0] - 1]
    weight = last_valid * jnp.broadcast_to(below_ref[:, bands : bands + 1], last_valid.shape)
    difference = (below_ref[:, :bands] - last_ref[...]) * weight[:, :bands]
    high, low = split(difference)
    rest = difference - high.astype(F32)
    buffer[:, bands:W] = jnp.ones((buffer.shape[0], W - bands), BF16)
    buffer[:, W + bands :] = jnp.zeros((buffer.shape[0], W - bands), BF16)
    buffer[:, :bands] = high
    buffer[:, W : W + bands] = low
    pairs = pair_ref[...] + dot_t(buffer[:, :W], buffer[...])
    squares = jnp.sum(rest * rest, 0, keepdims=True)

    def whole(parts, squares):
        mixed = parts[:, W:]
        squares = jnp.concatenate([squares, jnp.zeros((1, W - bands), F32)], 1)
        return parts[:, :W] + mixed + mixed.T + jnp.where(on_diagonal, squares, 0.0)

    pixel = whole(pixel_ref[...], jnp.sum(rest_ref[0, :, :bands], 0, keepdims=True))
    pair = whole(pairs, squares + jnp.sum(rest_ref[1, :, :bands], 0, keepdims=True))
    valid = valid_ref[:, :, :128]
    inner = jnp.sum(valid, 0)
    seams = jnp.sum(valid[1:] * valid[:-1], 0)
    pixel_count = TILE * jnp.sum(inner, 0, keepdims=True)
    pair_count = jnp.sum((TILE - 1) * inner + seams + weight[:, :128], 0, keepdims=True)
    out = jnp.where(column <= row, pair, 0.0)
    out = jnp.where((column > row) & (column <= bands + 1), pltpu.roll(pixel, 1, 1), out)
    out = jnp.where(column == bands + 2, pltpu.roll(pair, 2, 1), out)
    counts = jnp.where(row == 0, pixel_count[:, :1], 0.0)
    counts = jnp.where(row == 1, pair_count[:, :1], counts)
    packed[...] = jnp.where(column == bands + 3, counts, out)
    core = core_ref[0]
    mine_ref[...] = packed[pl.ds(pl.multiple_of(core * half, 8), half), :]
    other_ref[...] = packed[pl.ds(pl.multiple_of((1 - core) * half, 8), half), :]


def pack(core, valid, last, below, pixel, pair, rest):
    cols, bands = last.shape
    half = pltpu.VMEM((bands // 2, W), F32)
    return pl.pallas_call(
        pack_kernel,
        out_shape=[half, half],
        in_specs=[pl.BlockSpec(memory_space=pltpu.SMEM)] + [in_vmem()] * 6,
        out_specs=[in_vmem()] * 2,
        scratch_shapes=[pltpu.VMEM((W, W), F32), pltpu.VMEM((cols, 2 * W), BF16)],
        compiler_params=params(12),
        name="pack",
    )(core, valid, last, below, pixel, pair, rest)


def square_sum(x):
    return jnp.sum(x * x)


QUICK_STEPS = 7


def careful(matrix, target, identity, row, column, bands, left, right):
    start = 1.0 / jnp.max(jnp.sum(jnp.abs(matrix), 1, keepdims=True))
    left[:W, :] = start * identity
    left[W:, :] = identity - start * matrix

    def more(carry):
        count, size = carry
        return (count < 24) & (size > 4e-6)

    def squaring(carry):
        count, _ = carry
        new = dot3(left[...], left[W:, :])
        left[:W, :] = left[:W, :] + new[:W]
        left[W:, :] = new[W:]
        return count + 1, square_sum(new[W:])

    lax.while_loop(more, squaring, (0, jnp.float32(1e9)))
    right[...] = dot3(left[:W, :], target)

    def refining(carry):
        count, _ = carry
        residual = target - dot6(matrix, right[...])
        change = dot3(left[:W, :], residual)
        gain = right[...] + change
        right[...] = gain
        return count + 1, square_sum(change) / square_sum(gain)

    def rough(carry):
        count, size = carry
        return (count < 8) & jnp.logical_not(size <= 1e-6)

    _, size = lax.while_loop(rough, refining, (0, jnp.float32(1e9)))

    @pl.when(jnp.logical_not(size <= 1e-6))
    def _():
        left[:W, :] = matrix
        right[...] = target

        def eliminate(k, _):
            here = row[:, 0:1] == k
            pivot_left = left[pl.ds(k, 1), :]
            pivot_right = right[pl.ds(k, 1), :]
            values = jnp.sum(jnp.where(column == k, left[:W, :], 0.0), 1, keepdims=True)
            pivot = jnp.sum(jnp.where(here, values, 0.0))
            factor = jnp.where(here, (values - 1.0) / pivot, values / pivot)
            left[:W, :] = left[:W, :] - factor * pivot_left
            right[...] = right[...] - factor * pivot_right
            return 0

        lax.fori_loop(0, bands, eliminate, 0)


def solve_kernel(bands, core_ref, mine_ref, other_ref, weights_ref, left, right):
    core = core_ref[0]
    packed = jnp.concatenate([mine_ref[...], other_ref[...]], 0)
    swapped = jnp.concatenate([other_ref[...], mine_ref[...]], 0)
    packed = jnp.where(core == 0, packed, swapped)
    packed = jnp.concatenate([packed, jnp.zeros((W - bands, W), F32)], 0)
    row, column = indices((W, W))
    on_diagonal = row == column
    inside = (row < bands) & (column < bands)
    pixel_count = packed[0:1, bands + 3 : bands + 4]
    pair_count = packed[1:2, bands + 3 : bands + 4]

    def whole(triangle):
        return triangle + triangle.T - jnp.where(on_diagonal, triangle, 0.0)

    pixel = whole(jnp.where((column >= row) & (column <= bands), pltpu.roll(packed, W - 1, 1), 0.0))
    lower = jnp.where((column <= row) & inside, packed, 0.0)
    sums = jnp.where((column == bands) & (row < bands), pltpu.roll(packed, W - 2, 1), 0.0)
    pair = whole(lower + sums)

    def covariance(square, count):
        total = square[bands : bands + 1, :]
        total_rows = square[:, bands : bands + 1]
        return jnp.where(inside, (square - total_rows * total / count) / (count - 1.0), 0.0)

    signal = covariance(pixel, pixel_count)
    noise = covariance(pair, pair_count)
    combined = signal + noise
    mean = pixel[:, bands : bands + 1] / pixel_count
    diagonal = jnp.where(on_diagonal, combined, 0.0)
    scale_row = lax.rsqrt(jnp.where(column[0:1] < bands, jnp.sum(diagonal, 0, keepdims=True), 1.0))
    scale_column = lax.rsqrt(jnp.where(row[:, 0:1] < bands, jnp.sum(diagonal, 1, keepdims=True), 1.0))
    identity = jnp.where(on_diagonal, 1.0, 0.0)
    matrix = jnp.where(inside, combined * scale_column * scale_row, identity)
    target = noise * scale_column * scale_row

    coarse = matrix.astype(BF16)
    square = dot(coarse, coarse)
    shrink = lax.rsqrt(jnp.max(jnp.sum(jnp.abs(square), 1, keepdims=True), 0, keepdims=True))
    near = 2.0 * shrink * matrix - shrink * shrink * square
    inverse = 2.0 * shrink * identity - shrink * shrink * matrix

    def double(near, inverse):
        step = dot(near.astype(BF16), jnp.concatenate([near.astype(BF16), inverse.astype(BF16)], 1))
        return 2.0 * near - step[:, :W], 2.0 * inverse - step[:, W:]

    for _ in range(QUICK_STEPS):
        near, inverse = double(near, inverse)
    off = identity - dot3(matrix, inverse)
    inverse = inverse + dot(inverse.astype(BF16), off.astype(BF16))
    first = dot3(inverse, target)
    change = dot(inverse.astype(BF16), (target - dot3(matrix, first)).astype(BF16))
    right[...] = first + change
    off_size = square_sum(off)
    done = square_sum(change) * off_size * off_size <= 1e-8 * square_sum(first)

    @pl.when(jnp.logical_not(done & (off_size < 0.25)))
    def _():
        careful(matrix, target, identity, row, column, bands, left, right)

    gain = right[...] * scale_column * (1.0 / scale_row)
    shift = jnp.sum(jnp.where(row < bands, mean, 0.0) * gain, 0, keepdims=True)
    weights = jnp.where(row == bands, shift, jnp.where(inside, identity - gain, 0.0))
    high, low = split(weights)
    weights_ref[:W, :] = high
    weights_ref[W : 2 * W, :] = high
    weights_ref[2 * W :, :] = low


def solve(core, mine, other, bands):
    return pl.pallas_call(
        functools.partial(solve_kernel, bands),
        out_shape=pltpu.VMEM((3 * W, W), BF16),
        in_specs=[pl.BlockSpec(memory_space=pltpu.SMEM), in_vmem(), in_vmem()],
        out_specs=in_vmem(),
        scratch_shapes=[pltpu.VMEM((2 * W, W), F32), pltpu.VMEM((W, W), F32)],
        compiler_params=params(16),
        name="solve",
    )(core, mine, other)


def filter_kernel(halves_ref, valid_ref, weights_ref, out_hbm, staged, sems):
    rows, cols, bands = staged.shape
    copies = []
    for r in range(rows):
        halves = halves_ref[r * cols : (r + 1) * cols, :]
        result = dot(jnp.concatenate([halves, halves[:, :W]], 1), weights_ref[...])
        staged[r] = valid_ref[r // TILE][:, :bands] * result[:, :bands]
        copies.append(pltpu.make_async_copy(staged.at[pl.ds(r, 1)], out_hbm.at[pl.ds(r, 1)], sems.at[r]))
        copies[-1].start()
    for copy in copies:
        copy.wait()


def apply_filter(halves, valid, weights, shape):
    rows, cols, bands = shape
    pixels = rows * cols
    return pl.pallas_call(
        filter_kernel,
        out_shape=jax.ShapeDtypeStruct(shape, F32),
        in_specs=[in_vmem()] * 3,
        out_specs=in_hbm(),
        scratch_shapes=[pltpu.VMEM(shape, F32), pltpu.SemaphoreType.DMA((rows,))],
        compiler_params=params(24),
        cost_estimate=pl.CostEstimate(flops=3 * 2 * pixels * W * W, bytes_accessed=4 * pixels * W, transcendentals=0),
        name="filter",
    )(halves, valid, weights)


RING = 4


def permute(x, target):
    track, strip = lax.axis_size("track"), lax.axis_size("strip")
    pairs = []
    for i in range(track):
        for j in range(strip):
            y, z, chip, core = target(i // RING, i % RING, j // 2, j % 2)
            pairs.append((i * strip + j, (y * RING + z) * strip + chip * 2 + core))
    return lax.ppermute(x, ("track", "strip"), pairs)


def other_core(x):
    return permute(x, lambda y, z, chip, core: (y, z, chip, 1 - core))


PARTNER = {1: (1, 0, 3, 2), 2: (2, 3, 0, 1), 3: (3, 2, 1, 0)}


def ring_sum(x, axes):
    def exchanged(which):
        def target(y, z, chip, core):
            place = [y, z, chip]
            axis = axes[core]
            place[axis] = PARTNER[which if core == 0 else RING - which][place[axis]]
            return (*place, core)

        return permute(x, target)

    return lax.optimization_barrier(x + exchanged(1) + exchanged(3) + exchanged(2))


def per_device(cube, mask):
    bands = cube.shape[2]
    size = lax.axis_size("track")
    below = lax.ppermute(first_row(mask, cube), "track", [(i, i - 1) for i in range(1, size)])
    core = (lax.axis_index("strip") % 2).astype(jnp.int32)[None]
    halves, valid, last, pixel, pair, rest = moments(mask, cube)
    mine, other = pack(core, valid, last, below, pixel, pair, rest)
    total = mine + other_core(other)
    for axes in ((0, 1), (1, 2), (2, 0)):
        total = ring_sum(total, axes)
    weights = solve(core, total, other_core(total), bands)
    return apply_filter(halves, valid, weights, cube.shape)


def solution(mesh):
    return jax.shard_map(
        per_device,
        mesh=mesh,
        in_specs=(P("track", "strip", None), P("track", "strip")),
        out_specs=P("track", "strip", None),
        check_vma=False,
    )
```

```python
import functools

import jax
import jax.numpy as jnp
from jax import lax
from jax.experimental import pallas as pl
from jax.experimental.pallas import tpu as pltpu
from jax.sharding import PartitionSpec as P

TILE = 8
W = 256
F32 = jnp.float32
BF16 = jnp.bfloat16
MIB = 2**20


def split(x):
    high = x.astype(BF16)
    return high, (x - high.astype(F32)).astype(BF16)


def split3(x):
    high = x.astype(BF16)
    rest = x - high.astype(F32)
    middle = rest.astype(BF16)
    return high, middle, (rest - middle.astype(F32)).astype(BF16)


def dot(a, b):
    return lax.dot_general(a, b, (((1,), (0,)), ((), ())), preferred_element_type=F32)


def dot_t(a, b):
    return lax.dot_general(a, b, (((0,), (0,)), ((), ())), preferred_element_type=F32)


def dot3(a, b):
    a_high, a_low = split(a)
    b_high, b_low = split(b)
    return dot(
        jnp.concatenate([a_high, a_high, a_low], 1),
        jnp.concatenate([b_high, b_low, b_high], 0),
    )


def dot6(a, b):
    ah, am, al = split3(a)
    bh, bm, bl = split3(b)
    return dot(
        jnp.concatenate([ah, ah, am, ah, am, al], 1),
        jnp.concatenate([bh, bm, bh, bl, bm, bh], 0),
    )


def in_vmem():
    return pl.BlockSpec(memory_space=pltpu.VMEM)


def in_hbm():
    return pl.BlockSpec(memory_space=pltpu.HBM)


def params(mib):
    return pltpu.CompilerParams(vmem_limit_bytes=mib * MIB)


def fill_validity(mask_ref, tile_row, out_ref):
    for c in range(out_ref.shape[0] // TILE):
        value = mask_ref[tile_row, c].astype(F32)
        out_ref[c * TILE : (c + 1) * TILE, :] = jnp.full((TILE, out_ref.shape[1]), value, F32)


def fetch_row_kernel(cube_hbm, row_ref, sem):
    copy = pltpu.make_async_copy(cube_hbm.at[pl.ds(0, 1)], row_ref, sem)
    copy.start()
    copy.wait()


def join_row_kernel(mask_ref, row_ref, out_ref):
    fill_validity(mask_ref, 0, out_ref)
    out_ref[:, : row_ref.shape[2]] = row_ref[0]


def first_row(mask, cube):
    _, cols, bands = cube.shape
    row = pl.pallas_call(
        fetch_row_kernel,
        out_shape=pltpu.VMEM((1, cols, bands), F32),
        in_specs=[in_hbm()],
        out_specs=in_vmem(),
        scratch_shapes=[pltpu.SemaphoreType.DMA],
        compiler_params=params(50),
        name="fetch_row",
    )(cube)
    return pl.pallas_call(
        join_row_kernel,
        out_shape=pltpu.VMEM((cols, W), F32),
        in_specs=[pl.BlockSpec(memory_space=pltpu.SMEM), in_vmem()],
        out_specs=in_vmem(),
        compiler_params=params(12),
        name="join_row",
    )(mask, row)


GROUP = 4
BLOCK = 64


def moments_kernel(
    mask_hbm, cube_hbm, halves_ref, valid_ref, last_ref, pixel_ref, pair_ref, rest_ref, mask, raw, pairs_a, pairs_b, sems
):
    rows, cols, bands = raw.shape
    groups = rows // GROUP

    def fetch(g):
        at = pl.ds(g * GROUP, GROUP)
        return pltpu.make_async_copy(cube_hbm.at[at], raw.at[at], sems.at[g])

    mask_copy = pltpu.make_async_copy(mask_hbm, mask, sems.at[groups])
    mask_copy.start()
    for g in range(groups):
        fetch(g).start()
    pixel_ref[...] = jnp.zeros_like(pixel_ref)
    pair_ref[...] = jnp.zeros_like(pair_ref)
    for buffer in (halves_ref, pairs_a, pairs_b):
        count = buffer.shape[0]
        buffer[:, bands:W] = jnp.ones((count, W - bands), BF16)
        buffer[:, W + bands :] = jnp.zeros((count, W - bands), BF16)
    mask_copy.wait()

    def put(value, buffer, at, lanes, squares):
        count = value.shape[0]
        high = value.astype(BF16)
        low = (value - high.astype(F32)).astype(BF16)
        buffer[at : at + count, lanes] = high
        buffer[at : at + count, slice(W + lanes.start, W + lanes.stop)] = low
        parts = (low * low).reshape(count // 16, 16, -1)
        total = parts[0]
        for k in range(1, count // 16):
            total = total + parts[k]
        return squares + jnp.sum(total.astype(F32).reshape(2, 8, -1), 0)

    def product(ref, buffer):
        ref[...] += dot_t(buffer[:, :W], buffer[...])

    lane_halves = (slice(0, 128), slice(128, bands))
    squares = {(k, h): jnp.zeros((8, lanes.stop - lanes.start), F32) for k in range(2) for h, lanes in enumerate(lane_halves)}
    pending = []
    for g in range(groups):
        pairs = (pairs_a, pairs_b)[g % 2]
        halves = halves_ref.at[pl.ds(g * GROUP * cols, GROUP * cols)]
        fetch(g).wait()
        tile_row, within = divmod(g * GROUP, TILE)
        if within == 0:
            fill_validity(mask, tile_row, valid_ref.at[tile_row])
        for c in range(0, cols, BLOCK):
            if pending and c // BLOCK % 2 == 0:
                product(*pending.pop(0))
            block = slice(c, c + BLOCK)
            valid = valid_ref[tile_row, block, :128]
            for h, lanes in enumerate(lane_halves):
                weight = valid[:, : lanes.stop - lanes.start]
                previous = last_ref[block, lanes] if g else None
                for r in range(GROUP):
                    pixel = raw[g * GROUP + r, block, lanes] * weight
                    if previous is None:
                        difference = jnp.zeros_like(pixel)
                    else:
                        difference = pixel - previous
                        if within == 0 and r == 0:
                            difference = difference * (valid_ref[tile_row - 1, block, : weight.shape[1]] * weight)
                    previous = pixel
                    squares[0, h] = put(pixel, halves, r * cols + c, lanes, squares[0, h])
                    squares[1, h] = put(difference, pairs, r * cols + c, lanes, squares[1, h])
                last_ref[block, lanes] = previous
        for late in pending:
            product(*late)
        pending = [(pixel_ref, halves), (pair_ref, pairs)]
    for late in pending:
        product(*late)
    for k in range(2):
        rest_ref[k, :, bands:] = jnp.zeros((8, W - bands), F32)
        for h, lanes in enumerate(lane_halves):
            rest_ref[k, :, lanes] = squares[k, h]


def moments(mask, cube):
    rows, cols, bands = cube.shape
    pixels = rows * cols
    return pl.pallas_call(
        moments_kernel,
        out_shape=[
            pltpu.VMEM((pixels, 2 * W), BF16),
            pltpu.VMEM((rows // TILE, cols, W), F32),
            pltpu.VMEM((cols, bands), F32),
            pltpu.VMEM((W, 2 * W), F32),
            pltpu.VMEM((W, 2 * W), F32),
            pltpu.VMEM((2, 8, W), F32),
        ],
        in_specs=[in_hbm(), in_hbm()],
        out_specs=[in_vmem()] * 6,
        scratch_shapes=[
            pltpu.SMEM(mask.shape, jnp.int32),
            pltpu.VMEM(cube.shape, F32),
            pltpu.VMEM((GROUP * cols, 2 * W), BF16),
            pltpu.VMEM((GROUP * cols, 2 * W), BF16),
            pltpu.SemaphoreType.DMA((rows // GROUP + 1,)),
        ],
        compiler_params=params(40),
        cost_estimate=pl.CostEstimate(flops=4 * 2 * pixels * W * W, bytes_accessed=4 * pixels * W, transcendentals=0),
        name="moments",
    )(mask, cube)


def indices(shape):
    return lax.broadcasted_iota(jnp.int32, shape, 0), lax.broadcasted_iota(jnp.int32, shape, 1)


def pack_kernel(
    core_ref, valid_ref, last_ref, below_ref, pixel_ref, pair_ref, rest_ref, mine_ref, other_ref, packed, buffer
):
    bands = last_ref.shape[1]
    half = bands // 2
    row, column = indices((W, W))
    on_diagonal = row == column
    last_valid = valid_ref[valid_ref.shape[0] - 1]
    weight = last_valid * jnp.broadcast_to(below_ref[:, bands : bands + 1], last_valid.shape)
    difference = (below_ref[:, :bands] - last_ref[...]) * weight[:, :bands]
    high, low = split(difference)
    rest = difference - high.astype(F32)
    buffer[:, bands:W] = jnp.ones((buffer.shape[0], W - bands), BF16)
    buffer[:, W + bands :] = jnp.zeros((buffer.shape[0], W - bands), BF16)
    buffer[:, :bands] = high
    buffer[:, W : W + bands] = low
    pairs = pair_ref[...] + dot_t(buffer[:, :W], buffer[...])
    squares = jnp.sum(rest * rest, 0, keepdims=True)

    def whole(parts, squares):
        mixed = parts[:, W:]
        squares = jnp.concatenate([squares, jnp.zeros((1, W - bands), F32)], 1)
        return parts[:, :W] + mixed + mixed.T + jnp.where(on_diagonal, squares, 0.0)

    pixel = whole(pixel_ref[...], jnp.sum(rest_ref[0, :, :bands], 0, keepdims=True))
    pair = whole(pairs, squares + jnp.sum(rest_ref[1, :, :bands], 0, keepdims=True))
    valid = valid_ref[:, :, :128]
    inner = jnp.sum(valid, 0)
    seams = jnp.sum(valid[1:] * valid[:-1], 0)
    pixel_count = TILE * jnp.sum(inner, 0, keepdims=True)
    pair_count = jnp.sum((TILE - 1) * inner + seams + weight[:, :128], 0, keepdims=True)
    out = jnp.where(column <= row, pair, 0.0)
    out = jnp.where((column > row) & (column <= bands + 1), pltpu.roll(pixel, 1, 1), out)
    out = jnp.where(column == bands + 2, pltpu.roll(pair, 2, 1), out)
    counts = jnp.where(row == 0, pixel_count[:, :1], 0.0)
    counts = jnp.where(row == 1, pair_count[:, :1], counts)
    packed[...] = jnp.where(column == bands + 3, counts, out)
    core = core_ref[0]
    mine_ref[...] = packed[pl.ds(pl.multiple_of(core * half, 8), half), :]
    other_ref[...] = packed[pl.ds(pl.multiple_of((1 - core) * half, 8), half), :]


def pack(core, valid, last, below, pixel, pair, rest):
    cols, bands = last.shape
    half = pltpu.VMEM((bands // 2, W), F32)
    return pl.pallas_call(
        pack_kernel,
        out_shape=[half, half],
        in_specs=[pl.BlockSpec(memory_space=pltpu.SMEM)] + [in_vmem()] * 6,
        out_specs=[in_vmem()] * 2,
        scratch_shapes=[pltpu.VMEM((W, W), F32), pltpu.VMEM((cols, 2 * W), BF16)],
        compiler_params=params(12),
        name="pack",
    )(core, valid, last, below, pixel, pair, rest)


def square_sum(x):
    return jnp.sum(x * x)


QUICK_STEPS = 7


def careful(matrix, target, identity, row, column, bands, left, right):
    start = 1.0 / jnp.max(jnp.sum(jnp.abs(matrix), 1, keepdims=True))
    left[:W, :] = start * identity
    left[W:, :] = identity - start * matrix

    def more(carry):
        count, size = carry
        return (count < 24) & (size > 4e-6)

    def squaring(carry):
        count, _ = carry
        new = dot3(left[...], left[W:, :])
        left[:W, :] = left[:W, :] + new[:W]
        left[W:, :] = new[W:]
        return count + 1, square_sum(new[W:])

    lax.while_loop(more, squaring, (0, jnp.float32(1e9)))
    right[...] = dot3(left[:W, :], target)

    def refining(carry):
        count, _ = carry
        residual = target - dot6(matrix, right[...])
        change = dot3(left[:W, :], residual)
        gain = right[...] + change
        right[...] = gain
        return count + 1, square_sum(change) / square_sum(gain)

    def rough(carry):
        count, size = carry
        return (count < 8) & jnp.logical_not(size <= 1e-6)

    _, size = lax.while_loop(rough, refining, (0, jnp.float32(1e9)))

    @pl.when(jnp.logical_not(size <= 1e-6))
    def _():
        left[:W, :] = matrix
        right[...] = target

        def eliminate(k, _):
            here = row[:, 0:1] == k
            pivot_left = left[pl.ds(k, 1), :]
            pivot_right = right[pl.ds(k, 1), :]
            values = jnp.sum(jnp.where(column == k, left[:W, :], 0.0), 1, keepdims=True)
            pivot = jnp.sum(jnp.where(here, values, 0.0))
            factor = jnp.where(here, (values - 1.0) / pivot, values / pivot)
            left[:W, :] = left[:W, :] - factor * pivot_left
            right[...] = right[...] - factor * pivot_right
            return 0

        lax.fori_loop(0, bands, eliminate, 0)


def solve_kernel(bands, core_ref, mine_ref, other_ref, weights_ref, left, right):
    core = core_ref[0]
    packed = jnp.concatenate([mine_ref[...], other_ref[...]], 0)
    swapped = jnp.concatenate([other_ref[...], mine_ref[...]], 0)
    packed = jnp.where(core == 0, packed, swapped)
    packed = jnp.concatenate([packed, jnp.zeros((W - bands, W), F32)], 0)
    row, column = indices((W, W))
    on_diagonal = row == column
    inside = (row < bands) & (column < bands)
    pixel_count = packed[0:1, bands + 3 : bands + 4]
    pair_count = packed[1:2, bands + 3 : bands + 4]

    def whole(triangle):
        return triangle + triangle.T - jnp.where(on_diagonal, triangle, 0.0)

    pixel = whole(jnp.where((column >= row) & (column <= bands), pltpu.roll(packed, W - 1, 1), 0.0))
    lower = jnp.where((column <= row) & inside, packed, 0.0)
    sums = jnp.where((column == bands) & (row < bands), pltpu.roll(packed, W - 2, 1), 0.0)
    pair = whole(lower + sums)

    def covariance(square, count):
        total = square[bands : bands + 1, :]
        total_rows = square[:, bands : bands + 1]
        return jnp.where(inside, (square - total_rows * total / count) / (count - 1.0), 0.0)

    signal = covariance(pixel, pixel_count)
    noise = covariance(pair, pair_count)
    combined = signal + noise
    mean = pixel[:, bands : bands + 1] / pixel_count
    diagonal = jnp.where(on_diagonal, combined, 0.0)
    scale_row = lax.rsqrt(jnp.where(column[0:1] < bands, jnp.sum(diagonal, 0, keepdims=True), 1.0))
    scale_column = lax.rsqrt(jnp.where(row[:, 0:1] < bands, jnp.sum(diagonal, 1, keepdims=True), 1.0))
    identity = jnp.where(on_diagonal, 1.0, 0.0)
    matrix = jnp.where(inside, combined * scale_column * scale_row, identity)
    target = noise * scale_column * scale_row

    coarse = matrix.astype(BF16)
    square = dot(coarse, coarse)
    shrink = lax.rsqrt(jnp.max(jnp.sum(jnp.abs(square), 1, keepdims=True), 0, keepdims=True))
    near = 2.0 * shrink * matrix - shrink * shrink * square
    inverse = 2.0 * shrink * identity - shrink * shrink * matrix

    def double(near, inverse):
        step = dot(near.astype(BF16), jnp.concatenate([near.astype(BF16), inverse.astype(BF16)], 1))
        return 2.0 * near - step[:, :W], 2.0 * inverse - step[:, W:]

    for _ in range(QUICK_STEPS):
        near, inverse = double(near, inverse)
    off = identity - dot3(matrix, inverse)
    inverse = inverse + dot(inverse.astype(BF16), off.astype(BF16))
    first = dot3(inverse, target)
    change = dot(inverse.astype(BF16), (target - dot3(matrix, first)).astype(BF16))
    right[...] = first + change
    off_size = square_sum(off)
    done = square_sum(change) * off_size * off_size <= 1e-8 * square_sum(first)

    @pl.when(jnp.logical_not(done & (off_size < 0.25)))
    def _():
        careful(matrix, target, identity, row, column, bands, left, right)

    gain = right[...] * scale_column * (1.0 / scale_row)
    shift = jnp.sum(jnp.where(row < bands, mean, 0.0) * gain, 0, keepdims=True)
    weights = jnp.where(row == bands, shift, jnp.where(inside, identity - gain, 0.0))
    high, low = split(weights)
    weights_ref[:W, :] = high
    weights_ref[W : 2 * W, :] = high
    weights_ref[2 * W :, :] = low


def solve(core, mine, other, bands):
    return pl.pallas_call(
        functools.partial(solve_kernel, bands),
        out_shape=pltpu.VMEM((3 * W, W), BF16),
        in_specs=[pl.BlockSpec(memory_space=pltpu.SMEM), in_vmem(), in_vmem()],
        out_specs=in_vmem(),
        scratch_shapes=[pltpu.VMEM((2 * W, W), F32), pltpu.VMEM((W, W), F32)],
        compiler_params=params(16),
        name="solve",
    )(core, mine, other)


def filter_kernel(halves_ref, valid_ref, weights_ref, out_hbm, staged, sems):
    rows, cols, bands = staged.shape
    copies = []
    for r in range(rows):
        halves = halves_ref[r * cols : (r + 1) * cols, :]
        result = dot(jnp.concatenate([halves, halves[:, :W]], 1), weights_ref[...])
        staged[r] = valid_ref[r // TILE][:, :bands] * result[:, :bands]
        copies.append(pltpu.make_async_copy(staged.at[pl.ds(r, 1)], out_hbm.at[pl.ds(r, 1)], sems.at[r]))
        copies[-1].start()
    for copy in copies:
        copy.wait()


def apply_filter(halves, valid, weights, shape):
    rows, cols, bands = shape
    pixels = rows * cols
    return pl.pallas_call(
        filter_kernel,
        out_shape=jax.ShapeDtypeStruct(shape, F32),
        in_specs=[in_vmem()] * 3,
        out_specs=in_hbm(),
        scratch_shapes=[pltpu.VMEM(shape, F32), pltpu.SemaphoreType.DMA((rows,))],
        compiler_params=params(24),
        cost_estimate=pl.CostEstimate(flops=3 * 2 * pixels * W * W, bytes_accessed=4 * pixels * W, transcendentals=0),
        name="filter",
    )(halves, valid, weights)


RING = 4


def permute(x, target):
    track, strip = lax.axis_size("track"), lax.axis_size("strip")
    pairs = []
    for i in range(track):
        for j in range(strip):
            y, z, chip, core = target(i // RING, i % RING, j // 2, j % 2)
            pairs.append((i * strip + j, (y * RING + z) * strip + chip * 2 + core))
    return lax.ppermute(x, ("track", "strip"), pairs)


def other_core(x):
    return permute(x, lambda y, z, chip, core: (y, z, chip, 1 - core))


PARTNER = {1: (1, 0, 3, 2), 2: (2, 3, 0, 1), 3: (3, 2, 1, 0)}


def ring_sum(x, axes):
    def exchanged(which):
        def target(y, z, chip, core):
            place = [y, z, chip]
            axis = axes[core]
            place[axis] = PARTNER[which if core == 0 else RING - which][place[axis]]
            return (*place, core)

        return permute(x, target)

    return lax.optimization_barrier(x + exchanged(1) + exchanged(3) + exchanged(2))


def per_device(cube, mask):
    bands = cube.shape[2]
    size = lax.axis_size("track")
    below = lax.ppermute(first_row(mask, cube), "track", [(i, i - 1) for i in range(1, size)])
    core = (lax.axis_index("strip") % 2).astype(jnp.int32)[None]
    halves, valid, last, pixel, pair, rest = moments(mask, cube)
    mine, other = pack(core, valid, last, below, pixel, pair, rest)
    total = mine + other_core(other)
    for axes in ((0, 1), (1, 2), (2, 0)):
        total = ring_sum(total, axes)
    weights = solve(core, total, other_core(total), bands)
    return apply_filter(halves, valid, weights, cube.shape)


def solution(mesh):
    return jax.shard_map(
        per_device,
        mesh=mesh,
        in_specs=(P("track", "strip", None), P("track", "strip")),
        out_specs=P("track", "strip", None),
        check_vma=False,
    )
```

```python
import functools

import jax
import jax.numpy as jnp
from jax import lax
from jax.experimental import pallas as pl
from jax.experimental.pallas import tpu as pltpu
from jax.sharding import PartitionSpec as P

TILE = 8
W = 256
F32 = jnp.float32
BF16 = jnp.bfloat16
MIB = 2**20


def split(x):
    high = x.astype(BF16)
    return high, (x - high.astype(F32)).astype(BF16)


def split3(x):
    high = x.astype(BF16)
    rest = x - high.astype(F32)
    middle = rest.astype(BF16)
    return high, middle, (rest - middle.astype(F32)).astype(BF16)


def dot(a, b):
    return lax.dot_general(a, b, (((1,), (0,)), ((), ())), preferred_element_type=F32)


def dot_t(a, b):
    return lax.dot_general(a, b, (((0,), (0,)), ((), ())), preferred_element_type=F32)


def dot3(a, b):
    a_high, a_low = split(a)
    b_high, b_low = split(b)
    return dot(
        jnp.concatenate([a_high, a_high, a_low], 1),
        jnp.concatenate([b_high, b_low, b_high], 0),
    )


def dot6(a, b):
    ah, am, al = split3(a)
    bh, bm, bl = split3(b)
    return dot(
        jnp.concatenate([ah, ah, am, ah, am, al], 1),
        jnp.concatenate([bh, bm, bh, bl, bm, bh], 0),
    )


def in_vmem():
    return pl.BlockSpec(memory_space=pltpu.VMEM)


def in_hbm():
    return pl.BlockSpec(memory_space=pltpu.HBM)


def params(mib):
    return pltpu.CompilerParams(vmem_limit_bytes=mib * MIB)


def fill_validity(mask_ref, tile_row, out_ref):
    for c in range(out_ref.shape[0] // TILE):
        value = mask_ref[tile_row, c].astype(F32)
        out_ref[c * TILE : (c + 1) * TILE, :] = jnp.full((TILE, out_ref.shape[1]), value, F32)


def fetch_row_kernel(cube_hbm, row_ref, sem):
    copy = pltpu.make_async_copy(cube_hbm.at[pl.ds(0, 1)], row_ref, sem)
    copy.start()
    copy.wait()


def join_row_kernel(mask_ref, row_ref, out_ref):
    fill_validity(mask_ref, 0, out_ref)
    out_ref[:, : row_ref.shape[2]] = row_ref[0]


def first_row(mask, cube):
    _, cols, bands = cube.shape
    row = pl.pallas_call(
        fetch_row_kernel,
        out_shape=pltpu.VMEM((1, cols, bands), F32),
        in_specs=[in_hbm()],
        out_specs=in_vmem(),
        scratch_shapes=[pltpu.SemaphoreType.DMA],
        compiler_params=params(50),
        name="fetch_row",
    )(cube)
    return pl.pallas_call(
        join_row_kernel,
        out_shape=pltpu.VMEM((cols, W), F32),
        in_specs=[pl.BlockSpec(memory_space=pltpu.SMEM), in_vmem()],
        out_specs=in_vmem(),
        compiler_params=params(12),
        name="join_row",
    )(mask, row)


CUTS = ((0, 128), (128, 192))
BLOCK = 64
PIXEL_ONE, PAIR_ONE = 0, 1


def one_in(lane, count, width):
    return jnp.where(lax.broadcasted_iota(jnp.int32, (count, width), 1) == lane, 1.0, 0.0).astype(BF16)


def moments_kernel(
    mask_hbm, cube_hbm, halves_ref, valid_ref, last_ref, sums_ref, steps_ref, seams_ref, rest_ref, mask, raw, between_a, between_b, sems
):
    rows, cols, bands = raw.shape
    groups = [(t, c0, width) for t in range(rows // TILE) for c0, width in CUTS]

    def fetch(g):
        t, c0, width = groups[g]
        at = (pl.ds(t * TILE, TILE), pl.ds(c0, width))
        return pltpu.make_async_copy(cube_hbm.at[at], raw.at[at], sems.at[g])

    mask_copy = pltpu.make_async_copy(mask_hbm, mask, sems.at[len(groups)])
    mask_copy.start()
    for g in range(len(groups)):
        fetch(g).start()
    for ref in (sums_ref, steps_ref, seams_ref):
        ref[...] = jnp.zeros_like(ref)
    spare = W - bands
    for t, c0, width in groups:
        start = (t * cols + c0) * TILE
        for i in range(TILE):
            at = slice(start + i * width, start + (i + 1) * width)
            halves_ref[at, bands:W] = one_in(i % 2, width, spare)
            halves_ref[at, W + bands :] = jnp.zeros((width, spare), BF16)
    for buffer in (between_a, between_b):
        buffer[:, bands:W] = one_in(PAIR_ONE, buffer.shape[0], spare)
        buffer[:, W + bands :] = jnp.zeros((buffer.shape[0], spare), BF16)
    mask_copy.wait()

    def put(value, buffer, at, lanes, squares):
        count = value.shape[0]
        high = value.astype(BF16)
        low = (value - high.astype(F32)).astype(BF16)
        buffer[at : at + count, lanes] = high
        buffer[at : at + count, slice(W + lanes.start, W + lanes.stop)] = low
        parts = (low * low).reshape(count // 16, 16, -1)
        total = parts[0]
        for k in range(1, count // 16):
            total = total + parts[k]
        return squares + jnp.sum(total.astype(F32).reshape(2, 8, -1), 0)

    def product(ref, buffer, places, width):
        value = jnp.concatenate([buffer[at : at + width, :] for at in places], 0)
        ref[...] += dot_t(value[:, :W], value)

    lane_halves = (slice(0, 128), slice(128, bands))
    squares = {(k, h): jnp.zeros((8, lanes.stop - lanes.start), F32) for k in range(3) for h, lanes in enumerate(lane_halves)}
    pending = []
    for g, (t, c0, width) in enumerate(groups):
        between = (between_a, between_b)[g % 2]
        start = (t * cols + c0) * TILE
        fetch(g).wait()
        if c0 == 0:
            fill_validity(mask, t, valid_ref.at[t])
        gap = 1 if width == 128 else 2
        slot = 0
        for c in range(0, width, BLOCK):
            block = slice(c0 + c, c0 + c + BLOCK)
            valid = valid_ref[t, block, :128]
            for h, lanes in enumerate(lane_halves):
                if pending and slot % gap == 0:
                    product(*pending.pop(0))
                slot += 1
                weight = valid[:, : lanes.stop - lanes.start]
                previous = last_ref[block, lanes] if t else None
                for i in range(TILE // 2):
                    row = t * TILE + 2 * i
                    first = raw[row, block, lanes] * weight
                    second = raw[row + 1, block, lanes] * weight
                    if previous is None:
                        gone = jnp.zeros_like(first)
                    else:
                        gone = first - previous
                        if i == 0:
                            gone = gone * (valid_ref[t - 1, block, : weight.shape[1]] * weight)
                    previous = second
                    at = start + 2 * i * width + c
                    squares[0, h] = put(first + second, halves_ref, at, lanes, squares[0, h])
                    squares[1, h] = put(second - first, halves_ref, at + width, lanes, squares[1, h])
                    squares[2, h] = put(gone, between, i * width + c, lanes, squares[2, h])
                last_ref[block, lanes] = previous
        for late in pending:
            product(*late)
        pairs = range(TILE // 2)
        pending = [
            (sums_ref, halves_ref, [start + 2 * i * width for i in pairs], width),
            (steps_ref, halves_ref, [start + (2 * i + 1) * width for i in pairs], width),
            (seams_ref, between, [i * width for i in pairs], width),
        ]
    for late in pending:
        product(*late)
    for k in range(3):
        rest_ref[k, :, bands:] = jnp.zeros((8, W - bands), F32)
        for h, lanes in enumerate(lane_halves):
            rest_ref[k, :, lanes] = squares[k, h]


def moments(mask, cube):
    rows, cols, bands = cube.shape
    pixels = rows * cols
    widest = max(width for _, width in CUTS) * TILE // 2
    return pl.pallas_call(
        moments_kernel,
        out_shape=[
            pltpu.VMEM((pixels, 2 * W), BF16),
            pltpu.VMEM((rows // TILE, cols, W), F32),
            pltpu.VMEM((cols, bands), F32),
            pltpu.VMEM((W, 2 * W), F32),
            pltpu.VMEM((W, 2 * W), F32),
            pltpu.VMEM((W, 2 * W), F32),
            pltpu.VMEM((3, 8, W), F32),
        ],
        in_specs=[in_hbm(), in_hbm()],
        out_specs=[in_vmem()] * 7,
        scratch_shapes=[
            pltpu.SMEM(mask.shape, jnp.int32),
            pltpu.VMEM(cube.shape, F32),
            pltpu.VMEM((widest, 2 * W), BF16),
            pltpu.VMEM((widest, 2 * W), BF16),
            pltpu.SemaphoreType.DMA((rows // TILE * len(CUTS) + 1,)),
        ],
        compiler_params=params(40),
        cost_estimate=pl.CostEstimate(flops=3 * 2 * pixels * W * W, bytes_accessed=4 * pixels * W, transcendentals=0),
        name="moments",
    )(mask, cube)


def indices(shape):
    return lax.broadcasted_iota(jnp.int32, shape, 0), lax.broadcasted_iota(jnp.int32, shape, 1)


def pack_kernel(
    core_ref, valid_ref, last_ref, below_ref, sums_ref, steps_ref, seams_ref, rest_ref, mine_ref, other_ref, packed, buffer
):
    bands = last_ref.shape[1]
    half = bands // 2
    row, column = indices((W, W))
    on_diagonal = row == column
    last_valid = valid_ref[valid_ref.shape[0] - 1]
    weight = last_valid * jnp.broadcast_to(below_ref[:, bands : bands + 1], last_valid.shape)
    difference = (below_ref[:, :bands] - last_ref[...]) * weight[:, :bands]
    high, low = split(difference)
    rest = difference - high.astype(F32)
    buffer[:, bands:W] = one_in(PAIR_ONE, buffer.shape[0], W - bands)
    buffer[:, W + bands :] = jnp.zeros((buffer.shape[0], W - bands), BF16)
    buffer[:, :bands] = high
    buffer[:, W : W + bands] = low
    steps = steps_ref[...]
    seams = seams_ref[...] + dot_t(buffer[:, :W], buffer[...])
    rests = [jnp.sum(rest_ref[k, :, :bands], 0, keepdims=True) for k in range(3)]
    rests[2] = rests[2] + jnp.sum(rest * rest, 0, keepdims=True)

    def whole(parts, squares):
        mixed = parts[:, W:]
        squares = jnp.concatenate([squares, jnp.zeros((1, W - bands), F32)], 1)
        return parts[:, :W] + mixed + mixed.T + jnp.where(on_diagonal, squares, 0.0)

    pixel = whole(0.5 * (sums_ref[...] + steps), 0.5 * (rests[0] + rests[1]))
    pixel = jnp.where(column == bands + PIXEL_ONE, 2.0 * pixel, pixel)
    pair = whole(steps + seams, rests[1] + rests[2])
    valid = valid_ref[:, :, :128]
    inner = jnp.sum(valid, 0)
    crossing = jnp.sum(valid[1:] * valid[:-1], 0)
    pixel_count = TILE * jnp.sum(inner, 0, keepdims=True)
    pair_count = jnp.sum((TILE - 1) * inner + crossing + weight[:, :128], 0, keepdims=True)
    out = jnp.where(column <= row, pair, 0.0)
    out = jnp.where((column > row) & (column <= bands + 1), pltpu.roll(pixel, 1, 1), out)
    out = jnp.where(column == bands + 2, pltpu.roll(pair, 2 - PAIR_ONE, 1), out)
    counts = jnp.where(row == 0, pixel_count[:, :1], 0.0)
    counts = jnp.where(row == 1, pair_count[:, :1], counts)
    packed[...] = jnp.where(column == bands + 3, counts, out)
    core = core_ref[0]
    mine_ref[...] = packed[pl.ds(pl.multiple_of(core * half, 8), half), :]
    other_ref[...] = packed[pl.ds(pl.multiple_of((1 - core) * half, 8), half), :]


def pack(core, valid, last, below, sums, steps, seams, rest):
    cols, bands = last.shape
    half = pltpu.VMEM((bands // 2, W), F32)
    return pl.pallas_call(
        pack_kernel,
        out_shape=[half, half],
        in_specs=[pl.BlockSpec(memory_space=pltpu.SMEM)] + [in_vmem()] * 7,
        out_specs=[in_vmem()] * 2,
        scratch_shapes=[pltpu.VMEM((W, W), F32), pltpu.VMEM((cols, 2 * W), BF16)],
        compiler_params=params(12),
        name="pack",
    )(core, valid, last, below, sums, steps, seams, rest)


def square_sum(x):
    return jnp.sum(x * x)


QUICK_STEPS = 7


def careful(matrix, target, identity, row, column, bands, left, right):
    start = 1.0 / jnp.max(jnp.sum(jnp.abs(matrix), 1, keepdims=True))
    left[:W, :] = start * identity
    left[W:, :] = identity - start * matrix

    def more(carry):
        count, size = carry
        return (count < 24) & (size > 4e-6)

    def squaring(carry):
        count, _ = carry
        new = dot3(left[...], left[W:, :])
        left[:W, :] = left[:W, :] + new[:W]
        left[W:, :] = new[W:]
        return count + 1, square_sum(new[W:])

    lax.while_loop(more, squaring, (0, jnp.float32(1e9)))
    right[...] = dot3(left[:W, :], target)

    def refining(carry):
        count, _ = carry
        residual = target - dot6(matrix, right[...])
        change = dot3(left[:W, :], residual)
        gain = right[...] + change
        right[...] = gain
        return count + 1, square_sum(change) / square_sum(gain)

    def rough(carry):
        count, size = carry
        return (count < 8) & jnp.logical_not(size <= 1e-6)

    _, size = lax.while_loop(rough, refining, (0, jnp.float32(1e9)))

    @pl.when(jnp.logical_not(size <= 1e-6))
    def _():
        left[:W, :] = matrix
        right[...] = target

        def eliminate(k, _):
            here = row[:, 0:1] == k
            pivot_left = left[pl.ds(k, 1), :]
            pivot_right = right[pl.ds(k, 1), :]
            values = jnp.sum(jnp.where(column == k, left[:W, :], 0.0), 1, keepdims=True)
            pivot = jnp.sum(jnp.where(here, values, 0.0))
            factor = jnp.where(here, (values - 1.0) / pivot, values / pivot)
            left[:W, :] = left[:W, :] - factor * pivot_left
            right[...] = right[...] - factor * pivot_right
            return 0

        lax.fori_loop(0, bands, eliminate, 0)


def solve_kernel(bands, core_ref, mine_ref, other_ref, weights_ref, left, right):
    core = core_ref[0]
    packed = jnp.concatenate([mine_ref[...], other_ref[...]], 0)
    swapped = jnp.concatenate([other_ref[...], mine_ref[...]], 0)
    packed = jnp.where(core == 0, packed, swapped)
    packed = jnp.concatenate([packed, jnp.zeros((W - bands, W), F32)], 0)
    row, column = indices((W, W))
    on_diagonal = row == column
    inside = (row < bands) & (column < bands)
    pixel_count = packed[0:1, bands + 3 : bands + 4]
    pair_count = packed[1:2, bands + 3 : bands + 4]

    def whole(triangle):
        return triangle + triangle.T - jnp.where(on_diagonal, triangle, 0.0)

    pixel = whole(jnp.where((column >= row) & (column <= bands), pltpu.roll(packed, W - 1, 1), 0.0))
    lower = jnp.where((column <= row) & inside, packed, 0.0)
    sums = jnp.where((column == bands) & (row < bands), pltpu.roll(packed, W - 2, 1), 0.0)
    pair = whole(lower + sums)

    def covariance(square, count):
        total = square[bands : bands + 1, :]
        total_rows = square[:, bands : bands + 1]
        return jnp.where(inside, (square - total_rows * total / count) / (count - 1.0), 0.0)

    signal = covariance(pixel, pixel_count)
    noise = covariance(pair, pair_count)
    combined = signal + noise
    mean = pixel[:, bands : bands + 1] / pixel_count
    diagonal = jnp.where(on_diagonal, combined, 0.0)
    scale_row = lax.rsqrt(jnp.where(column[0:1] < bands, jnp.sum(diagonal, 0, keepdims=True), 1.0))
    scale_column = lax.rsqrt(jnp.where(row[:, 0:1] < bands, jnp.sum(diagonal, 1, keepdims=True), 1.0))
    identity = jnp.where(on_diagonal, 1.0, 0.0)
    matrix = jnp.where(inside, combined * scale_column * scale_row, identity)
    target = noise * scale_column * scale_row

    coarse = matrix.astype(BF16)
    square = dot(coarse, coarse)
    shrink = lax.rsqrt(jnp.max(jnp.sum(jnp.abs(square), 1, keepdims=True), 0, keepdims=True))
    near = 2.0 * shrink * matrix - shrink * shrink * square
    inverse = 2.0 * shrink * identity - shrink * shrink * matrix

    def double(near, inverse):
        step = dot(near.astype(BF16), jnp.concatenate([near.astype(BF16), inverse.astype(BF16)], 1))
        return 2.0 * near - step[:, :W], 2.0 * inverse - step[:, W:]

    for _ in range(QUICK_STEPS):
        near, inverse = double(near, inverse)
    off = identity - dot3(matrix, inverse)
    inverse = inverse + dot(inverse.astype(BF16), off.astype(BF16))
    first = dot3(inverse, target)
    change = dot(inverse.astype(BF16), (target - dot3(matrix, first)).astype(BF16))
    right[...] = first + change
    off_size = square_sum(off)
    done = square_sum(change) * off_size * off_size <= 1e-8 * square_sum(first)

    @pl.when(jnp.logical_not(done & (off_size < 0.25)))
    def _():
        careful(matrix, target, identity, row, column, bands, left, right)

    gain = right[...] * scale_column * (1.0 / scale_row)
    shift = jnp.sum(jnp.where(row < bands, mean, 0.0) * gain, 0, keepdims=True)
    weights = jnp.where(row == bands + PIXEL_ONE, shift, jnp.where(inside, 0.5 * (identity - gain), 0.0))
    high, low = split(weights)
    weights_ref[:W, :] = high
    weights_ref[W : 2 * W, :] = high
    weights_ref[2 * W :, :] = low


def solve(core, mine, other, bands):
    return pl.pallas_call(
        functools.partial(solve_kernel, bands),
        out_shape=pltpu.VMEM((3 * W, W), BF16),
        in_specs=[pl.BlockSpec(memory_space=pltpu.SMEM), in_vmem(), in_vmem()],
        out_specs=in_vmem(),
        scratch_shapes=[pltpu.VMEM((2 * W, W), F32), pltpu.VMEM((W, W), F32)],
        compiler_params=params(16),
        name="solve",
    )(core, mine, other)


def filter_kernel(halves_ref, valid_ref, weights_ref, out_hbm, staged, sems):
    rows, cols, bands = staged.shape
    copies = []
    for t in range(rows // TILE):
        for c0, width in CUTS:
            at = (t * cols + c0) * TILE
            valid = valid_ref.at[t, c0 : c0 + width, :bands]
            for i in range(TILE // 2):
                halves = halves_ref[at + 2 * i * width : at + 2 * (i + 1) * width, :]
                result = dot(jnp.concatenate([halves, halves[:, :W]], 1), weights_ref[...])
                half_sum, half_step = result[:width, :bands], result[width:, :bands]
                row = t * TILE + 2 * i
                staged[row, c0 : c0 + width] = valid[...] * (half_sum - half_step)
                staged[row + 1, c0 : c0 + width] = valid[...] * (half_sum + half_step)
                part = (pl.ds(row, 2), pl.ds(c0, width))
                copies.append(pltpu.make_async_copy(staged.at[part], out_hbm.at[part], sems.at[len(copies)]))
                copies[-1].start()
    for copy in copies:
        copy.wait()


def apply_filter(halves, valid, weights, shape):
    rows, cols, bands = shape
    pixels = rows * cols
    return pl.pallas_call(
        filter_kernel,
        out_shape=jax.ShapeDtypeStruct(shape, F32),
        in_specs=[in_vmem()] * 3,
        out_specs=in_hbm(),
        scratch_shapes=[pltpu.VMEM(shape, F32), pltpu.SemaphoreType.DMA((rows // 2 * len(CUTS),))],
        compiler_params=params(24),
        cost_estimate=pl.CostEstimate(flops=3 * 2 * pixels * W * W, bytes_accessed=4 * pixels * W, transcendentals=0),
        name="filter",
    )(halves, valid, weights)


RING = 4


def permute(x, target):
    track, strip = lax.axis_size("track"), lax.axis_size("strip")
    pairs = []
    for i in range(track):
        for j in range(strip):
            y, z, chip, core = target(i // RING, i % RING, j // 2, j % 2)
            pairs.append((i * strip + j, (y * RING + z) * strip + chip * 2 + core))
    return lax.ppermute(x, ("track", "strip"), pairs)


def other_core(x):
    return permute(x, lambda y, z, chip, core: (y, z, chip, 1 - core))


PARTNER = {1: (1, 0, 3, 2), 2: (2, 3, 0, 1), 3: (3, 2, 1, 0)}


def ring_sum(x, axes):
    def exchanged(which):
        def target(y, z, chip, core):
            place = [y, z, chip]
            axis = axes[core]
            place[axis] = PARTNER[which if core == 0 else RING - which][place[axis]]
            return (*place, core)

        return permute(x, target)

    return lax.optimization_barrier(x + exchanged(1) + exchanged(3) + exchanged(2))


def per_device(cube, mask):
    bands = cube.shape[2]
    size = lax.axis_size("track")
    below = lax.ppermute(first_row(mask, cube), "track", [(i, i - 1) for i in range(1, size)])
    core = (lax.axis_index("strip") % 2).astype(jnp.int32)[None]
    halves, valid, last, sums, steps, seams, rest = moments(mask, cube)
    mine, other = pack(core, valid, last, below, sums, steps, seams, rest)
    total = mine + other_core(other)
    for axes in ((0, 1), (1, 2), (2, 0)):
        total = ring_sum(total, axes)
    weights = solve(core, total, other_core(total), bands)
    return apply_filter(halves, valid, weights, cube.shape)


def solution(mesh):
    return jax.shard_map(
        per_device,
        mesh=mesh,
        in_specs=(P("track", "strip", None), P("track", "strip")),
        out_specs=P("track", "strip", None),
        check_vma=False,
    )
```

```python
import functools

import jax
import jax.numpy as jnp
from jax import lax
from jax.experimental import pallas as pl
from jax.experimental.pallas import tpu as pltpu
from jax.sharding import PartitionSpec as P

TILE = 8
W = 256
F32 = jnp.float32
BF16 = jnp.bfloat16
MIB = 2**20


def split(x):
    high = x.astype(BF16)
    return high, (x - high.astype(F32)).astype(BF16)


def split3(x):
    high = x.astype(BF16)
    rest = x - high.astype(F32)
    middle = rest.astype(BF16)
    return high, middle, (rest - middle.astype(F32)).astype(BF16)


def dot(a, b):
    return lax.dot_general(a, b, (((1,), (0,)), ((), ())), preferred_element_type=F32)


def dot_t(a, b):
    return lax.dot_general(a, b, (((0,), (0,)), ((), ())), preferred_element_type=F32)


def dot3(a, b):
    a_high, a_low = split(a)
    b_high, b_low = split(b)
    return dot(
        jnp.concatenate([a_high, a_high, a_low], 1),
        jnp.concatenate([b_high, b_low, b_high], 0),
    )


def dot6(a, b):
    ah, am, al = split3(a)
    bh, bm, bl = split3(b)
    return dot(
        jnp.concatenate([ah, ah, am, ah, am, al], 1),
        jnp.concatenate([bh, bm, bh, bl, bm, bh], 0),
    )


def in_vmem():
    return pl.BlockSpec(memory_space=pltpu.VMEM)


def in_hbm():
    return pl.BlockSpec(memory_space=pltpu.HBM)


def params(mib):
    return pltpu.CompilerParams(vmem_limit_bytes=mib * MIB)


def fill_validity(mask_ref, tile_row, out_ref):
    for c in range(out_ref.shape[0] // TILE):
        value = mask_ref[tile_row, c].astype(F32)
        out_ref[c * TILE : (c + 1) * TILE, :] = jnp.full((TILE, out_ref.shape[1]), value, F32)


def fetch_row_kernel(cube_hbm, row_ref, sem):
    copy = pltpu.make_async_copy(cube_hbm.at[pl.ds(cube_hbm.shape[0] - 1, 1)], row_ref, sem)
    copy.start()
    copy.wait()


def join_row_kernel(mask_ref, row_ref, out_ref):
    fill_validity(mask_ref, mask_ref.shape[0] - 1, out_ref)
    out_ref[:, : row_ref.shape[2]] = row_ref[0]


def final_row(mask, cube):
    _, cols, bands = cube.shape
    row = pl.pallas_call(
        fetch_row_kernel,
        out_shape=pltpu.VMEM((1, cols, bands), F32),
        in_specs=[in_hbm()],
        out_specs=in_vmem(),
        scratch_shapes=[pltpu.SemaphoreType.DMA],
        compiler_params=params(50),
        name="fetch_row",
    )(cube)
    return pl.pallas_call(
        join_row_kernel,
        out_shape=pltpu.VMEM((cols, W), F32),
        in_specs=[pl.BlockSpec(memory_space=pltpu.SMEM), in_vmem()],
        out_specs=in_vmem(),
        compiler_params=params(12),
        name="join_row",
    )(mask, row)


CUTS = ((0, 128), (128, 192))
BLOCK = 64
PIXEL_ONE, PAIR_ONE = 0, 1


def one_in(lane, count, width):
    return jnp.where(lax.broadcasted_iota(jnp.int32, (count, width), 1) == lane, 1.0, 0.0).astype(BF16)


def moments_kernel(
    mask_hbm, cube_hbm, halves_ref, valid_ref, first_ref, sums_ref, steps_ref, seams_ref, rest_ref, mask, raw, last, between_a, between_b, sems
):
    rows, cols, bands = raw.shape
    groups = [(t, c0, width) for t in range(rows // TILE) for c0, width in CUTS]

    def fetch(g):
        t, c0, width = groups[g]
        at = (pl.ds(t * TILE, TILE), pl.ds(c0, width))
        return pltpu.make_async_copy(cube_hbm.at[at], raw.at[at], sems.at[g])

    mask_copy = pltpu.make_async_copy(mask_hbm, mask, sems.at[len(groups)])
    mask_copy.start()
    for g in range(len(groups)):
        fetch(g).start()
    for ref in (sums_ref, steps_ref, seams_ref):
        ref[...] = jnp.zeros_like(ref)
    spare = W - bands
    for t, c0, width in groups:
        start = (t * cols + c0) * TILE
        for i in range(TILE):
            at = slice(start + i * width, start + (i + 1) * width)
            halves_ref[at, bands:W] = one_in(i % 2, width, spare)
            halves_ref[at, W + bands :] = jnp.zeros((width, spare), BF16)
    for buffer in (between_a, between_b):
        buffer[:, bands:W] = one_in(PAIR_ONE, buffer.shape[0], spare)
        buffer[:, W + bands :] = jnp.zeros((buffer.shape[0], spare), BF16)
    mask_copy.wait()

    def put(value, buffer, at, lanes, squares):
        count = value.shape[0]
        high = value.astype(BF16)
        low = (value - high.astype(F32)).astype(BF16)
        buffer[at : at + count, lanes] = high
        buffer[at : at + count, slice(W + lanes.start, W + lanes.stop)] = low
        parts = (low * low).reshape(count // 16, 16, -1)
        total = parts[0]
        for k in range(1, count // 16):
            total = total + parts[k]
        return squares + jnp.sum(total.astype(F32).reshape(2, 8, -1), 0)

    def product(ref, buffer, places, width):
        value = jnp.concatenate([buffer[at : at + width, :] for at in places], 0)
        ref[...] += dot_t(value[:, :W], value)

    lane_halves = (slice(0, 128), slice(128, bands))
    squares = {(k, h): jnp.zeros((8, lanes.stop - lanes.start), F32) for k in range(3) for h, lanes in enumerate(lane_halves)}
    pending = []
    for g, (t, c0, width) in enumerate(groups):
        between = (between_a, between_b)[g % 2]
        start = (t * cols + c0) * TILE
        fetch(g).wait()
        if c0 == 0:
            fill_validity(mask, t, valid_ref.at[t])
        gap = 1 if width == 128 else 2
        slot = 0
        for c in range(0, width, BLOCK):
            block = slice(c0 + c, c0 + c + BLOCK)
            valid = valid_ref[t, block, :128]
            for h, lanes in enumerate(lane_halves):
                if pending and slot % gap == 0:
                    product(*pending.pop(0))
                slot += 1
                weight = valid[:, : lanes.stop - lanes.start]
                previous = last[block, lanes] if t else None
                for i in range(TILE // 2):
                    row = t * TILE + 2 * i
                    first = raw[row, block, lanes] * weight
                    second = raw[row + 1, block, lanes] * weight
                    if previous is None:
                        first_ref[block, lanes] = first
                        gone = jnp.zeros_like(first)
                    else:
                        gone = first - previous
                        if i == 0:
                            gone = gone * (valid_ref[t - 1, block, : weight.shape[1]] * weight)
                    previous = second
                    at = start + 2 * i * width + c
                    squares[0, h] = put(first + second, halves_ref, at, lanes, squares[0, h])
                    squares[1, h] = put(second - first, halves_ref, at + width, lanes, squares[1, h])
                    squares[2, h] = put(gone, between, i * width + c, lanes, squares[2, h])
                last[block, lanes] = previous
        for late in pending:
            product(*late)
        pairs = range(TILE // 2)
        pending = [
            (sums_ref, halves_ref, [start + 2 * i * width for i in pairs], width),
            (steps_ref, halves_ref, [start + (2 * i + 1) * width for i in pairs], width),
            (seams_ref, between, [i * width for i in pairs], width),
        ]
    for late in pending:
        product(*late)
    for k in range(3):
        rest_ref[k, :, bands:] = jnp.zeros((8, W - bands), F32)
        for h, lanes in enumerate(lane_halves):
            rest_ref[k, :, lanes] = squares[k, h]


def moments(mask, cube):
    rows, cols, bands = cube.shape
    pixels = rows * cols
    widest = max(width for _, width in CUTS) * TILE // 2
    return pl.pallas_call(
        moments_kernel,
        out_shape=[
            pltpu.VMEM((pixels, 2 * W), BF16),
            pltpu.VMEM((rows // TILE, cols, W), F32),
            pltpu.VMEM((cols, bands), F32),
            pltpu.VMEM((W, 2 * W), F32),
            pltpu.VMEM((W, 2 * W), F32),
            pltpu.VMEM((W, 2 * W), F32),
            pltpu.VMEM((3, 8, W), F32),
        ],
        in_specs=[in_hbm(), in_hbm()],
        out_specs=[in_vmem()] * 7,
        scratch_shapes=[
            pltpu.SMEM(mask.shape, jnp.int32),
            pltpu.VMEM(cube.shape, F32),
            pltpu.VMEM((cols, bands), F32),
            pltpu.VMEM((widest, 2 * W), BF16),
            pltpu.VMEM((widest, 2 * W), BF16),
            pltpu.SemaphoreType.DMA((rows // TILE * len(CUTS) + 1,)),
        ],
        compiler_params=params(40),
        cost_estimate=pl.CostEstimate(flops=3 * 2 * pixels * W * W, bytes_accessed=4 * pixels * W, transcendentals=0),
        name="moments",
    )(mask, cube)


def indices(shape):
    return lax.broadcasted_iota(jnp.int32, shape, 0), lax.broadcasted_iota(jnp.int32, shape, 1)


def pack_kernel(
    core_ref, valid_ref, first_ref, above_ref, sums_ref, steps_ref, seams_ref, rest_ref, mine_ref, other_ref, packed, buffer
):
    bands = first_ref.shape[1]
    half = bands // 2
    row, column = indices((W, W))
    on_diagonal = row == column
    first_valid = valid_ref[0]
    weight = first_valid * jnp.broadcast_to(above_ref[:, bands : bands + 1], first_valid.shape)
    difference = (first_ref[...] - above_ref[:, :bands]) * weight[:, :bands]
    high, low = split(difference)
    rest = difference - high.astype(F32)
    buffer[:, bands:W] = one_in(PAIR_ONE, buffer.shape[0], W - bands)
    buffer[:, W + bands :] = jnp.zeros((buffer.shape[0], W - bands), BF16)
    buffer[:, :bands] = high
    buffer[:, W : W + bands] = low
    steps = steps_ref[...]
    seams = seams_ref[...] + dot_t(buffer[:, :W], buffer[...])
    rests = [jnp.sum(rest_ref[k, :, :bands], 0, keepdims=True) for k in range(3)]
    rests[2] = rests[2] + jnp.sum(rest * rest, 0, keepdims=True)

    def whole(parts, squares):
        mixed = parts[:, W:]
        squares = jnp.concatenate([squares, jnp.zeros((1, W - bands), F32)], 1)
        return parts[:, :W] + mixed + mixed.T + jnp.where(on_diagonal, squares, 0.0)

    pixel = whole(0.5 * (sums_ref[...] + steps), 0.5 * (rests[0] + rests[1]))
    pixel = jnp.where(column == bands + PIXEL_ONE, 2.0 * pixel, pixel)
    pair = whole(steps + seams, rests[1] + rests[2])
    valid = valid_ref[:, :, :128]
    inner = jnp.sum(valid, 0)
    crossing = jnp.sum(valid[1:] * valid[:-1], 0)
    pixel_count = TILE * jnp.sum(inner, 0, keepdims=True)
    pair_count = jnp.sum((TILE - 1) * inner + crossing + weight[:, :128], 0, keepdims=True)
    out = jnp.where(column <= row, pair, 0.0)
    out = jnp.where((column > row) & (column <= bands + 1), pltpu.roll(pixel, 1, 1), out)
    out = jnp.where(column == bands + 2, pltpu.roll(pair, 2 - PAIR_ONE, 1), out)
    counts = jnp.where(row == 0, pixel_count[:, :1], 0.0)
    counts = jnp.where(row == 1, pair_count[:, :1], counts)
    packed[...] = jnp.where(column == bands + 3, counts, out)
    core = core_ref[0]
    mine_ref[...] = packed[pl.ds(pl.multiple_of(core * half, 8), half), :]
    other_ref[...] = packed[pl.ds(pl.multiple_of((1 - core) * half, 8), half), :]


def pack(core, valid, first, above, sums, steps, seams, rest):
    cols, bands = first.shape
    half = pltpu.VMEM((bands // 2, W), F32)
    return pl.pallas_call(
        pack_kernel,
        out_shape=[half, half],
        in_specs=[pl.BlockSpec(memory_space=pltpu.SMEM)] + [in_vmem()] * 7,
        out_specs=[in_vmem()] * 2,
        scratch_shapes=[pltpu.VMEM((W, W), F32), pltpu.VMEM((cols, 2 * W), BF16)],
        compiler_params=params(12),
        name="pack",
    )(core, valid, first, above, sums, steps, seams, rest)


def square_sum(x):
    return jnp.sum(x * x)


QUICK_STEPS = 7


def careful(matrix, target, identity, row, column, bands, left, right):
    start = 1.0 / jnp.max(jnp.sum(jnp.abs(matrix), 1, keepdims=True))
    left[:W, :] = start * identity
    left[W:, :] = identity - start * matrix

    def more(carry):
        count, size = carry
        return (count < 24) & (size > 4e-6)

    def squaring(carry):
        count, _ = carry
        new = dot3(left[...], left[W:, :])
        left[:W, :] = left[:W, :] + new[:W]
        left[W:, :] = new[W:]
        return count + 1, square_sum(new[W:])

    lax.while_loop(more, squaring, (0, jnp.float32(1e9)))
    right[...] = dot3(left[:W, :], target)

    def refining(carry):
        count, _ = carry
        residual = target - dot6(matrix, right[...])
        change = dot3(left[:W, :], residual)
        gain = right[...] + change
        right[...] = gain
        return count + 1, square_sum(change) / square_sum(gain)

    def rough(carry):
        count, size = carry
        return (count < 8) & jnp.logical_not(size <= 1e-6)

    _, size = lax.while_loop(rough, refining, (0, jnp.float32(1e9)))

    @pl.when(jnp.logical_not(size <= 1e-6))
    def _():
        left[:W, :] = matrix
        right[...] = target

        def eliminate(k, _):
            here = row[:, 0:1] == k
            pivot_left = left[pl.ds(k, 1), :]
            pivot_right = right[pl.ds(k, 1), :]
            values = jnp.sum(jnp.where(column == k, left[:W, :], 0.0), 1, keepdims=True)
            pivot = jnp.sum(jnp.where(here, values, 0.0))
            factor = jnp.where(here, (values - 1.0) / pivot, values / pivot)
            left[:W, :] = left[:W, :] - factor * pivot_left
            right[...] = right[...] - factor * pivot_right
            return 0

        lax.fori_loop(0, bands, eliminate, 0)


def solve_kernel(bands, core_ref, mine_ref, other_ref, weights_ref, left, right):
    core = core_ref[0]
    packed = jnp.concatenate([mine_ref[...], other_ref[...]], 0)
    swapped = jnp.concatenate([other_ref[...], mine_ref[...]], 0)
    packed = jnp.where(core == 0, packed, swapped)
    packed = jnp.concatenate([packed, jnp.zeros((W - bands, W), F32)], 0)
    row, column = indices((W, W))
    on_diagonal = row == column
    inside = (row < bands) & (column < bands)
    pixel_count = packed[0:1, bands + 3 : bands + 4]
    pair_count = packed[1:2, bands + 3 : bands + 4]

    def whole(triangle):
        return triangle + triangle.T - jnp.where(on_diagonal, triangle, 0.0)

    pixel = whole(jnp.where((column >= row) & (column <= bands), pltpu.roll(packed, W - 1, 1), 0.0))
    lower = jnp.where((column <= row) & inside, packed, 0.0)
    sums = jnp.where((column == bands) & (row < bands), pltpu.roll(packed, W - 2, 1), 0.0)
    pair = whole(lower + sums)

    def covariance(square, count):
        total = square[bands : bands + 1, :]
        total_rows = square[:, bands : bands + 1]
        return jnp.where(inside, (square - total_rows * total / count) / (count - 1.0), 0.0)

    signal = covariance(pixel, pixel_count)
    noise = covariance(pair, pair_count)
    combined = signal + noise
    mean = pixel[:, bands : bands + 1] / pixel_count
    diagonal = jnp.where(on_diagonal, combined, 0.0)
    scale_row = lax.rsqrt(jnp.where(column[0:1] < bands, jnp.sum(diagonal, 0, keepdims=True), 1.0))
    scale_column = lax.rsqrt(jnp.where(row[:, 0:1] < bands, jnp.sum(diagonal, 1, keepdims=True), 1.0))
    identity = jnp.where(on_diagonal, 1.0, 0.0)
    matrix = jnp.where(inside, combined * scale_column * scale_row, identity)
    target = noise * scale_column * scale_row

    coarse = matrix.astype(BF16)
    square = dot(coarse, coarse)
    shrink = lax.rsqrt(jnp.max(jnp.sum(jnp.abs(square), 1, keepdims=True), 0, keepdims=True))
    near = 2.0 * shrink * matrix - shrink * shrink * square
    inverse = 2.0 * shrink * identity - shrink * shrink * matrix

    def double(near, inverse):
        step = dot(near.astype(BF16), jnp.concatenate([near.astype(BF16), inverse.astype(BF16)], 1))
        return 2.0 * near - step[:, :W], 2.0 * inverse - step[:, W:]

    for _ in range(QUICK_STEPS):
        near, inverse = double(near, inverse)
    off = identity - dot3(matrix, inverse)
    inverse = inverse + dot(inverse.astype(BF16), off.astype(BF16))
    first = dot3(inverse, target)
    change = dot(inverse.astype(BF16), (target - dot3(matrix, first)).astype(BF16))
    right[...] = first + change
    off_size = square_sum(off)
    done = square_sum(change) * off_size * off_size <= 1e-8 * square_sum(first)

    @pl.when(jnp.logical_not(done & (off_size < 0.25)))
    def _():
        careful(matrix, target, identity, row, column, bands, left, right)

    gain = right[...] * scale_column * (1.0 / scale_row)
    shift = jnp.sum(jnp.where(row < bands, mean, 0.0) * gain, 0, keepdims=True)
    weights = jnp.where(row == bands + PIXEL_ONE, shift, jnp.where(inside, 0.5 * (identity - gain), 0.0))
    high, low = split(weights)
    weights_ref[:W, :] = high
    weights_ref[W : 2 * W, :] = high
    weights_ref[2 * W :, :] = low


def solve(core, mine, other, bands):
    return pl.pallas_call(
        functools.partial(solve_kernel, bands),
        out_shape=pltpu.VMEM((3 * W, W), BF16),
        in_specs=[pl.BlockSpec(memory_space=pltpu.SMEM), in_vmem(), in_vmem()],
        out_specs=in_vmem(),
        scratch_shapes=[pltpu.VMEM((2 * W, W), F32), pltpu.VMEM((W, W), F32)],
        compiler_params=params(16),
        name="solve",
    )(core, mine, other)


def filter_kernel(halves_ref, valid_ref, weights_ref, out_hbm, staged, sems):
    rows, cols, bands = staged.shape
    copies = []
    for t in range(rows // TILE):
        for c0, width in CUTS:
            at = (t * cols + c0) * TILE
            valid = valid_ref.at[t, c0 : c0 + width, :bands]
            for i in range(TILE // 2):
                halves = halves_ref[at + 2 * i * width : at + 2 * (i + 1) * width, :]
                result = dot(jnp.concatenate([halves, halves[:, :W]], 1), weights_ref[...])
                half_sum, half_step = result[:width, :bands], result[width:, :bands]
                row = t * TILE + 2 * i
                staged[row, c0 : c0 + width] = valid[...] * (half_sum - half_step)
                staged[row + 1, c0 : c0 + width] = valid[...] * (half_sum + half_step)
                part = (pl.ds(row, 2), pl.ds(c0, width))
                copies.append(pltpu.make_async_copy(staged.at[part], out_hbm.at[part], sems.at[len(copies)]))
                copies[-1].start()
    for copy in copies:
        copy.wait()


def apply_filter(halves, valid, weights, shape):
    rows, cols, bands = shape
    pixels = rows * cols
    return pl.pallas_call(
        filter_kernel,
        out_shape=jax.ShapeDtypeStruct(shape, F32),
        in_specs=[in_vmem()] * 3,
        out_specs=in_hbm(),
        scratch_shapes=[pltpu.VMEM(shape, F32), pltpu.SemaphoreType.DMA((rows // 2 * len(CUTS),))],
        compiler_params=params(24),
        cost_estimate=pl.CostEstimate(flops=3 * 2 * pixels * W * W, bytes_accessed=4 * pixels * W, transcendentals=0),
        name="filter",
    )(halves, valid, weights)


RING = 4


def permute(x, target):
    track, strip = lax.axis_size("track"), lax.axis_size("strip")
    pairs = []
    for i in range(track):
        for j in range(strip):
            y, z, chip, core = target(i // RING, i % RING, j // 2, j % 2)
            pairs.append((i * strip + j, (y * RING + z) * strip + chip * 2 + core))
    return lax.ppermute(x, ("track", "strip"), pairs)


def other_core(x):
    return permute(x, lambda y, z, chip, core: (y, z, chip, 1 - core))


PARTNER = {1: (1, 0, 3, 2), 2: (2, 3, 0, 1), 3: (3, 2, 1, 0)}


def ring_sum(x, axes):
    def exchanged(which):
        def target(y, z, chip, core):
            place = [y, z, chip]
            axis = axes[core]
            place[axis] = PARTNER[which if core == 0 else RING - which][place[axis]]
            return (*place, core)

        return permute(x, target)

    return lax.optimization_barrier(x + exchanged(1) + exchanged(3) + exchanged(2))


def per_device(cube, mask):
    bands = cube.shape[2]
    size = lax.axis_size("track")
    above = lax.ppermute(final_row(mask, cube), "track", [(i, i + 1) for i in range(size - 1)])
    core = (lax.axis_index("strip") % 2).astype(jnp.int32)[None]
    halves, valid, first, sums, steps, seams, rest = moments(mask, cube)
    mine, other = pack(core, valid, first, above, sums, steps, seams, rest)
    total = mine + other_core(other)
    for axes in ((0, 1), (1, 2), (2, 0)):
        total = ring_sum(total, axes)
    weights = solve(core, total, other_core(total), bands)
    return apply_filter(halves, valid, weights, cube.shape)


def solution(mesh):
    return jax.shard_map(
        per_device,
        mesh=mesh,
        in_specs=(P("track", "strip", None), P("track", "strip")),
        out_specs=P("track", "strip", None),
        check_vma=False,
    )
```

```python
import functools

import jax
import jax.numpy as jnp
from jax import lax
from jax.experimental import pallas as pl
from jax.experimental.pallas import tpu as pltpu
from jax.sharding import PartitionSpec as P

TILE = 8
W = 256
F32 = jnp.float32
BF16 = jnp.bfloat16
MIB = 2**20


def split(x):
    high = x.astype(BF16)
    return high, (x - high.astype(F32)).astype(BF16)


def split3(x):
    high = x.astype(BF16)
    rest = x - high.astype(F32)
    middle = rest.astype(BF16)
    return high, middle, (rest - middle.astype(F32)).astype(BF16)


def dot(a, b):
    return lax.dot_general(a, b, (((1,), (0,)), ((), ())), preferred_element_type=F32)


def dot_t(a, b):
    return lax.dot_general(a, b, (((0,), (0,)), ((), ())), preferred_element_type=F32)


def dot3(a, b):
    a_high, a_low = split(a)
    b_high, b_low = split(b)
    return dot(
        jnp.concatenate([a_high, a_high, a_low], 1),
        jnp.concatenate([b_high, b_low, b_high], 0),
    )


def dot6(a, b):
    ah, am, al = split3(a)
    bh, bm, bl = split3(b)
    return dot(
        jnp.concatenate([ah, ah, am, ah, am, al], 1),
        jnp.concatenate([bh, bm, bh, bl, bm, bh], 0),
    )


def in_vmem():
    return pl.BlockSpec(memory_space=pltpu.VMEM)


def in_hbm():
    return pl.BlockSpec(memory_space=pltpu.HBM)


def params(mib):
    return pltpu.CompilerParams(vmem_limit_bytes=mib * MIB)


def fill_validity(mask_ref, tile_row, out_ref):
    for c in range(out_ref.shape[0] // TILE):
        value = mask_ref[tile_row, c].astype(F32)
        out_ref[c * TILE : (c + 1) * TILE, :] = jnp.full((TILE, out_ref.shape[1]), value, F32)


def fetch_row_kernel(cube_hbm, out_ref, sem):
    rows, cols, _ = cube_hbm.shape
    copy = pltpu.make_async_copy(cube_hbm.at[rows - 1], out_ref.at[pl.ds(0, cols)], sem)
    copy.start()
    copy.wait()


def join_row_kernel(mask_ref, row_ref, out_ref):
    rows, tiles = mask_ref.shape
    spare = out_ref.shape[0] - tiles * TILE
    flags = mask_ref[rows - 1 : rows, :].astype(F32)
    out_ref[tiles * TILE :, :tiles] = jnp.broadcast_to(flags, (spare, tiles))


def final_row(mask, cube):
    _, cols, bands = cube.shape
    out = pltpu.VMEM((cols + 8, bands), F32)
    row = pl.pallas_call(
        fetch_row_kernel,
        out_shape=out,
        in_specs=[in_hbm()],
        out_specs=in_vmem(),
        scratch_shapes=[pltpu.SemaphoreType.DMA],
        compiler_params=params(54),
        name="fetch_row",
    )(cube)
    return pl.pallas_call(
        join_row_kernel,
        out_shape=out,
        in_specs=[in_vmem(), in_vmem()],
        out_specs=in_vmem(),
        input_output_aliases={1: 0},
        compiler_params=params(12),
        name="join_row",
    )(mask, row)


CUTS = ((0, 128), (128, 192))
BLOCK = 64
PIXEL_ONE, PAIR_ONE = 0, 1


def one_in(lane, count, width):
    return jnp.where(lax.broadcasted_iota(jnp.int32, (count, width), 1) == lane, 1.0, 0.0).astype(BF16)


def moments_kernel(
    mask_hbm, cube_hbm, halves_ref, valid_ref, first_ref, sums_ref, steps_ref, seams_ref, rest_ref, mask, raw, last, between_a, between_b, sems
):
    rows, cols, bands = raw.shape
    groups = [(t, c0, width) for t in range(rows // TILE) for c0, width in CUTS]

    def fetch(g):
        t, c0, width = groups[g]
        at = (pl.ds(t * TILE, TILE), pl.ds(c0, width))
        return pltpu.make_async_copy(cube_hbm.at[at], raw.at[at], sems.at[g])

    mask_copy = pltpu.make_async_copy(mask_hbm, mask, sems.at[len(groups)])
    mask_copy.start()
    for g in range(len(groups)):
        fetch(g).start()
    for ref in (sums_ref, steps_ref, seams_ref):
        ref[...] = jnp.zeros_like(ref)
    spare = W - bands
    for t, c0, width in groups:
        start = (t * cols + c0) * TILE
        for i in range(TILE):
            at = slice(start + i * width, start + (i + 1) * width)
            halves_ref[at, bands:W] = one_in(i % 2, width, spare)
            halves_ref[at, W + bands :] = jnp.zeros((width, spare), BF16)
    for buffer in (between_a, between_b):
        buffer[:, bands:W] = one_in(PAIR_ONE, buffer.shape[0], spare)
        buffer[:, W + bands :] = jnp.zeros((buffer.shape[0], spare), BF16)
    mask_copy.wait()

    def put(value, buffer, at, lanes, squares):
        count = value.shape[0]
        high = value.astype(BF16)
        low = (value - high.astype(F32)).astype(BF16)
        buffer[at : at + count, lanes] = high
        buffer[at : at + count, slice(W + lanes.start, W + lanes.stop)] = low
        parts = (low * low).reshape(count // 16, 16, -1)
        total = parts[0]
        for k in range(1, count // 16):
            total = total + parts[k]
        return squares + jnp.sum(total.astype(F32).reshape(2, 8, -1), 0)

    def product(ref, buffer, places, width):
        value = jnp.concatenate([buffer[at : at + width, :] for at in places], 0)
        ref[...] += dot_t(value[:, :W], value)

    lane_halves = (slice(0, 128), slice(128, bands))
    squares = {(k, h): jnp.zeros((8, lanes.stop - lanes.start), F32) for k in range(3) for h, lanes in enumerate(lane_halves)}
    pending = []
    for g, (t, c0, width) in enumerate(groups):
        between = (between_a, between_b)[g % 2]
        start = (t * cols + c0) * TILE
        fetch(g).wait()
        if c0 == 0:
            fill_validity(mask, t, valid_ref.at[t])
        gap = 1 if width == 128 else 2
        slot = 0
        for c in range(0, width, BLOCK):
            block = slice(c0 + c, c0 + c + BLOCK)
            valid = valid_ref[t, block, :128]
            for h, lanes in enumerate(lane_halves):
                if pending and slot % gap == 0:
                    product(*pending.pop(0))
                slot += 1
                weight = valid[:, : lanes.stop - lanes.start]
                previous = last[block, lanes] if t else None
                for i in range(TILE // 2):
                    row = t * TILE + 2 * i
                    first = raw[row, block, lanes] * weight
                    second = raw[row + 1, block, lanes] * weight
                    if previous is None:
                        first_ref[block, lanes] = first
                        gone = jnp.zeros_like(first)
                    else:
                        gone = first - previous
                        if i == 0:
                            gone = gone * (valid_ref[t - 1, block, : weight.shape[1]] * weight)
                    previous = second
                    at = start + 2 * i * width + c
                    squares[0, h] = put(first + second, halves_ref, at, lanes, squares[0, h])
                    squares[1, h] = put(second - first, halves_ref, at + width, lanes, squares[1, h])
                    squares[2, h] = put(gone, between, i * width + c, lanes, squares[2, h])
                last[block, lanes] = previous
        for late in pending:
            product(*late)
        pairs = range(TILE // 2)
        pending = [
            (sums_ref, halves_ref, [start + 2 * i * width for i in pairs], width),
            (steps_ref, halves_ref, [start + (2 * i + 1) * width for i in pairs], width),
            (seams_ref, between, [i * width for i in pairs], width),
        ]
    for late in pending:
        product(*late)
    for k in range(3):
        rest_ref[k, :, bands:] = jnp.zeros((8, W - bands), F32)
        for h, lanes in enumerate(lane_halves):
            rest_ref[k, :, lanes] = squares[k, h]


def moments(mask, cube):
    rows, cols, bands = cube.shape
    pixels = rows * cols
    widest = max(width for _, width in CUTS) * TILE // 2
    return pl.pallas_call(
        moments_kernel,
        out_shape=[
            pltpu.VMEM((pixels, 2 * W), BF16),
            pltpu.VMEM((rows // TILE, cols, W), F32),
            pltpu.VMEM((cols, bands), F32),
            pltpu.VMEM((W, 2 * W), F32),
            pltpu.VMEM((W, 2 * W), F32),
            pltpu.VMEM((W, 2 * W), F32),
            pltpu.VMEM((3, 8, W), F32),
        ],
        in_specs=[in_hbm(), in_hbm()],
        out_specs=[in_vmem()] * 7,
        scratch_shapes=[
            pltpu.SMEM(mask.shape, jnp.int32),
            pltpu.VMEM(cube.shape, F32),
            pltpu.VMEM((cols, bands), F32),
            pltpu.VMEM((widest, 2 * W), BF16),
            pltpu.VMEM((widest, 2 * W), BF16),
            pltpu.SemaphoreType.DMA((rows // TILE * len(CUTS) + 1,)),
        ],
        compiler_params=params(40),
        cost_estimate=pl.CostEstimate(flops=3 * 2 * pixels * W * W, bytes_accessed=4 * pixels * W, transcendentals=0),
        name="moments",
    )(mask, cube)


def indices(shape):
    return lax.broadcasted_iota(jnp.int32, shape, 0), lax.broadcasted_iota(jnp.int32, shape, 1)


def pack_kernel(
    core_ref, track_ref, valid_ref, first_ref, above_ref, sums_ref, steps_ref, seams_ref, rest_ref, mine_ref, other_ref, packed, buffer
):
    bands = first_ref.shape[1]
    half = bands // 2
    row, column = indices((W, W))
    on_diagonal = row == column
    first_valid = valid_ref[0]
    cols = first_valid.shape[0]
    pixel_row, tile = indices((cols, 128))
    flags = jnp.where(tile == lax.shift_right_logical(pixel_row, 3), above_ref[cols : cols + 1, :128], 0.0)
    flags = jnp.where(track_ref[0] > 0, jnp.sum(flags, 1, keepdims=True), 0.0)
    weight = first_valid * jnp.broadcast_to(flags, first_valid.shape)
    difference = (first_ref[...] - above_ref[:cols, :]) * weight[:, :bands]
    high, low = split(difference)
    rest = difference - high.astype(F32)
    buffer[:, bands:W] = one_in(PAIR_ONE, buffer.shape[0], W - bands)
    buffer[:, W + bands :] = jnp.zeros((buffer.shape[0], W - bands), BF16)
    buffer[:, :bands] = high
    buffer[:, W : W + bands] = low
    steps = steps_ref[...]
    seams = seams_ref[...] + dot_t(buffer[:, :W], buffer[...])
    rests = [jnp.sum(rest_ref[k, :, :bands], 0, keepdims=True) for k in range(3)]
    rests[2] = rests[2] + jnp.sum(rest * rest, 0, keepdims=True)

    def whole(parts, squares):
        mixed = parts[:, W:]
        squares = jnp.concatenate([squares, jnp.zeros((1, W - bands), F32)], 1)
        return parts[:, :W] + mixed + mixed.T + jnp.where(on_diagonal, squares, 0.0)

    pixel = whole(0.5 * (sums_ref[...] + steps), 0.5 * (rests[0] + rests[1]))
    pixel = jnp.where(column == bands + PIXEL_ONE, 2.0 * pixel, pixel)
    pair = whole(steps + seams, rests[1] + rests[2])
    valid = valid_ref[:, :, :128]
    inner = jnp.sum(valid, 0)
    crossing = jnp.sum(valid[1:] * valid[:-1], 0)
    pixel_count = TILE * jnp.sum(inner, 0, keepdims=True)
    pair_count = jnp.sum((TILE - 1) * inner + crossing + weight[:, :128], 0, keepdims=True)
    out = jnp.where(column <= row, pair, 0.0)
    out = jnp.where((column > row) & (column <= bands + 1), pltpu.roll(pixel, 1, 1), out)
    out = jnp.where(column == bands + 2, pltpu.roll(pair, 2 - PAIR_ONE, 1), out)
    counts = jnp.where(row == 0, pixel_count[:, :1], 0.0)
    counts = jnp.where(row == 1, pair_count[:, :1], counts)
    packed[...] = jnp.where(column == bands + 3, counts, out)
    core = core_ref[0]
    mine_ref[...] = packed[pl.ds(pl.multiple_of(core * half, 8), half), :]
    other_ref[...] = packed[pl.ds(pl.multiple_of((1 - core) * half, 8), half), :]


def pack(core, track, valid, first, above, sums, steps, seams, rest):
    cols, bands = first.shape
    half = pltpu.VMEM((bands // 2, W), F32)
    return pl.pallas_call(
        pack_kernel,
        out_shape=[half, half],
        in_specs=[pl.BlockSpec(memory_space=pltpu.SMEM)] * 2 + [in_vmem()] * 7,
        out_specs=[in_vmem()] * 2,
        scratch_shapes=[pltpu.VMEM((W, W), F32), pltpu.VMEM((cols, 2 * W), BF16)],
        compiler_params=params(12),
        name="pack",
    )(core, track, valid, first, above, sums, steps, seams, rest)


def square_sum(x):
    return jnp.sum(x * x)


QUICK_STEPS = 7


def careful(matrix, target, identity, row, column, bands, left, right):
    start = 1.0 / jnp.max(jnp.sum(jnp.abs(matrix), 1, keepdims=True))
    left[:W, :] = start * identity
    left[W:, :] = identity - start * matrix

    def more(carry):
        count, size = carry
        return (count < 24) & (size > 4e-6)

    def squaring(carry):
        count, _ = carry
        new = dot3(left[...], left[W:, :])
        left[:W, :] = left[:W, :] + new[:W]
        left[W:, :] = new[W:]
        return count + 1, square_sum(new[W:])

    lax.while_loop(more, squaring, (0, jnp.float32(1e9)))
    right[...] = dot3(left[:W, :], target)

    def refining(carry):
        count, _ = carry
        residual = target - dot6(matrix, right[...])
        change = dot3(left[:W, :], residual)
        gain = right[...] + change
        right[...] = gain
        return count + 1, square_sum(change) / square_sum(gain)

    def rough(carry):
        count, size = carry
        return (count < 8) & jnp.logical_not(size <= 1e-6)

    _, size = lax.while_loop(rough, refining, (0, jnp.float32(1e9)))

    @pl.when(jnp.logical_not(size <= 1e-6))
    def _():
        left[:W, :] = matrix
        right[...] = target

        def eliminate(k, _):
            here = row[:, 0:1] == k
            pivot_left = left[pl.ds(k, 1), :]
            pivot_right = right[pl.ds(k, 1), :]
            values = jnp.sum(jnp.where(column == k, left[:W, :], 0.0), 1, keepdims=True)
            pivot = jnp.sum(jnp.where(here, values, 0.0))
            factor = jnp.where(here, (values - 1.0) / pivot, values / pivot)
            left[:W, :] = left[:W, :] - factor * pivot_left
            right[...] = right[...] - factor * pivot_right
            return 0

        lax.fori_loop(0, bands, eliminate, 0)


def solve_kernel(bands, core_ref, mine_ref, other_ref, weights_ref, left, right):
    core = core_ref[0]
    packed = jnp.concatenate([mine_ref[...], other_ref[...]], 0)
    swapped = jnp.concatenate([other_ref[...], mine_ref[...]], 0)
    packed = jnp.where(core == 0, packed, swapped)
    packed = jnp.concatenate([packed, jnp.zeros((W - bands, W), F32)], 0)
    row, column = indices((W, W))
    on_diagonal = row == column
    inside = (row < bands) & (column < bands)
    pixel_count = packed[0:1, bands + 3 : bands + 4]
    pair_count = packed[1:2, bands + 3 : bands + 4]

    def whole(triangle):
        return triangle + triangle.T - jnp.where(on_diagonal, triangle, 0.0)

    pixel = whole(jnp.where((column >= row) & (column <= bands), pltpu.roll(packed, W - 1, 1), 0.0))
    lower = jnp.where((column <= row) & inside, packed, 0.0)
    sums = jnp.where((column == bands) & (row < bands), pltpu.roll(packed, W - 2, 1), 0.0)
    pair = whole(lower + sums)

    def covariance(square, count):
        total = square[bands : bands + 1, :]
        total_rows = square[:, bands : bands + 1]
        return jnp.where(inside, (square - total_rows * total / count) / (count - 1.0), 0.0)

    signal = covariance(pixel, pixel_count)
    noise = covariance(pair, pair_count)
    combined = signal + noise
    mean = pixel[:, bands : bands + 1] / pixel_count
    diagonal = jnp.where(on_diagonal, combined, 0.0)
    scale_row = lax.rsqrt(jnp.where(column[0:1] < bands, jnp.sum(diagonal, 0, keepdims=True), 1.0))
    scale_column = lax.rsqrt(jnp.where(row[:, 0:1] < bands, jnp.sum(diagonal, 1, keepdims=True), 1.0))
    identity = jnp.where(on_diagonal, 1.0, 0.0)
    matrix = jnp.where(inside, combined * scale_column * scale_row, identity)
    target = noise * scale_column * scale_row

    coarse = matrix.astype(BF16)
    square = dot(coarse, coarse)
    shrink = lax.rsqrt(jnp.max(jnp.sum(jnp.abs(square), 1, keepdims=True), 0, keepdims=True))
    near = 2.0 * shrink * matrix - shrink * shrink * square
    inverse = 2.0 * shrink * identity - shrink * shrink * matrix

    def double(near, inverse):
        step = dot(near.astype(BF16), jnp.concatenate([near.astype(BF16), inverse.astype(BF16)], 1))
        return 2.0 * near - step[:, :W], 2.0 * inverse - step[:, W:]

    for _ in range(QUICK_STEPS):
        near, inverse = double(near, inverse)
    off = identity - dot3(matrix, inverse)
    inverse = inverse + dot(inverse.astype(BF16), off.astype(BF16))
    first = dot3(inverse, target)
    change = dot(inverse.astype(BF16), (target - dot3(matrix, first)).astype(BF16))
    right[...] = first + change
    off_size = square_sum(off)
    done = square_sum(change) * off_size * off_size <= 1e-8 * square_sum(first)

    @pl.when(jnp.logical_not(done & (off_size < 0.25)))
    def _():
        careful(matrix, target, identity, row, column, bands, left, right)

    gain = right[...] * scale_column * (1.0 / scale_row)
    shift = jnp.sum(jnp.where(row < bands, mean, 0.0) * gain, 0, keepdims=True)
    weights = jnp.where(row == bands + PIXEL_ONE, shift, jnp.where(inside, 0.5 * (identity - gain), 0.0))
    high, low = split(weights)
    weights_ref[:W, :] = high
    weights_ref[W : 2 * W, :] = high
    weights_ref[2 * W :, :] = low


def solve(core, mine, other, bands):
    return pl.pallas_call(
        functools.partial(solve_kernel, bands),
        out_shape=pltpu.VMEM((3 * W, W), BF16),
        in_specs=[pl.BlockSpec(memory_space=pltpu.SMEM), in_vmem(), in_vmem()],
        out_specs=in_vmem(),
        scratch_shapes=[pltpu.VMEM((2 * W, W), F32), pltpu.VMEM((W, W), F32)],
        compiler_params=params(16),
        name="solve",
    )(core, mine, other)


def filter_kernel(halves_ref, valid_ref, weights_ref, out_hbm, staged, sems):
    rows, cols, bands = staged.shape
    copies = []
    for t in range(rows // TILE):
        for c0, width in CUTS:
            at = (t * cols + c0) * TILE
            valid = valid_ref.at[t, c0 : c0 + width, :bands]
            for i in range(TILE // 2):
                halves = halves_ref[at + 2 * i * width : at + 2 * (i + 1) * width, :]
                result = dot(jnp.concatenate([halves, halves[:, :W]], 1), weights_ref[...])
                half_sum, half_step = result[:width, :bands], result[width:, :bands]
                row = t * TILE + 2 * i
                staged[row, c0 : c0 + width] = valid[...] * (half_sum - half_step)
                staged[row + 1, c0 : c0 + width] = valid[...] * (half_sum + half_step)
                part = (pl.ds(row, 2), pl.ds(c0, width))
                copies.append(pltpu.make_async_copy(staged.at[part], out_hbm.at[part], sems.at[len(copies)]))
                copies[-1].start()
    for copy in copies:
        copy.wait()


def apply_filter(halves, valid, weights, shape):
    rows, cols, bands = shape
    pixels = rows * cols
    return pl.pallas_call(
        filter_kernel,
        out_shape=jax.ShapeDtypeStruct(shape, F32),
        in_specs=[in_vmem()] * 3,
        out_specs=in_hbm(),
        scratch_shapes=[pltpu.VMEM(shape, F32), pltpu.SemaphoreType.DMA((rows // 2 * len(CUTS),))],
        compiler_params=params(24),
        cost_estimate=pl.CostEstimate(flops=3 * 2 * pixels * W * W, bytes_accessed=4 * pixels * W, transcendentals=0),
        name="filter",
    )(halves, valid, weights)


RING = 4


def permute(x, target):
    track, strip = lax.axis_size("track"), lax.axis_size("strip")
    pairs = []
    for i in range(track):
        for j in range(strip):
            y, z, chip, core = target(i // RING, i % RING, j // 2, j % 2)
            pairs.append((i * strip + j, (y * RING + z) * strip + chip * 2 + core))
    return lax.ppermute(x, ("track", "strip"), pairs)


def other_core(x):
    return permute(x, lambda y, z, chip, core: (y, z, chip, 1 - core))


PARTNER = {1: (1, 0, 3, 2), 2: (2, 3, 0, 1), 3: (3, 2, 1, 0)}


def ring_sum(x, axes):
    def exchanged(which):
        def target(y, z, chip, core):
            place = [y, z, chip]
            axis = axes[core]
            place[axis] = PARTNER[which if core == 0 else RING - which][place[axis]]
            return (*place, core)

        return permute(x, target)

    return lax.optimization_barrier(x + exchanged(1) + exchanged(3) + exchanged(2))


def per_device(cube, mask):
    bands = cube.shape[2]
    size = lax.axis_size("track")
    above = lax.ppermute(final_row(mask, cube), "track", [(i, (i + 1) % size) for i in range(size)])
    core = (lax.axis_index("strip") % 2).astype(jnp.int32)[None]
    track = lax.axis_index("track").astype(jnp.int32)[None]
    halves, valid, first, sums, steps, seams, rest = moments(mask, cube)
    mine, other = pack(core, track, valid, first, above, sums, steps, seams, rest)
    total = mine + other_core(other)
    for axes in ((0, 1), (1, 2), (2, 0)):
        total = ring_sum(total, axes)
    weights = solve(core, total, other_core(total), bands)
    return apply_filter(halves, valid, weights, cube.shape)


def solution(mesh):
    return jax.shard_map(
        per_device,
        mesh=mesh,
        in_specs=(P("track", "strip", None), P("track", "strip")),
        out_specs=P("track", "strip", None),
        check_vma=False,
    )
```

```python
import functools

import jax
import jax.numpy as jnp
from jax import lax
from jax.experimental import pallas as pl
from jax.experimental.pallas import tpu as pltpu
from jax.sharding import PartitionSpec as P

TILE = 8
W = 256
F32 = jnp.float32
BF16 = jnp.bfloat16
MIB = 2**20


def split(x):
    high = x.astype(BF16)
    return high, (x - high.astype(F32)).astype(BF16)


def split3(x):
    high = x.astype(BF16)
    rest = x - high.astype(F32)
    middle = rest.astype(BF16)
    return high, middle, (rest - middle.astype(F32)).astype(BF16)


def dot(a, b):
    return lax.dot_general(a, b, (((1,), (0,)), ((), ())), preferred_element_type=F32)


def dot_t(a, b):
    return lax.dot_general(a, b, (((0,), (0,)), ((), ())), preferred_element_type=F32)


def dot3(a, b):
    a_high, a_low = split(a)
    b_high, b_low = split(b)
    return dot(
        jnp.concatenate([a_high, a_high, a_low], 1),
        jnp.concatenate([b_high, b_low, b_high], 0),
    )


def dot6(a, b):
    ah, am, al = split3(a)
    bh, bm, bl = split3(b)
    return dot(
        jnp.concatenate([ah, ah, am, ah, am, al], 1),
        jnp.concatenate([bh, bm, bh, bl, bm, bh], 0),
    )


def in_vmem():
    return pl.BlockSpec(memory_space=pltpu.VMEM)


def in_hbm():
    return pl.BlockSpec(memory_space=pltpu.HBM)


def params(mib):
    return pltpu.CompilerParams(vmem_limit_bytes=mib * MIB)


def fill_validity(mask_ref, tile_row, out_ref):
    for c in range(out_ref.shape[0] // TILE):
        value = mask_ref[tile_row, c].astype(F32)
        out_ref[c * TILE : (c + 1) * TILE, :] = jnp.full((TILE, out_ref.shape[1]), value, F32)


def folding(cols, bands):
    keep = cols * bands // W
    return keep, cols - keep, W - bands


def fetch_row_kernel(cube_hbm, out_ref, sem):
    copy = pltpu.make_async_copy(cube_hbm.at[cube_hbm.shape[0] - 1], out_ref, sem)
    copy.start()
    copy.wait()


def fold_row_kernel(mask_ref, row_ref, out_ref):
    rows, tiles = mask_ref.shape
    cols, bands = row_ref.shape
    keep, left, spare = folding(cols, bands)
    out_ref[:keep, :bands] = row_ref[:keep, :]
    for j in range(bands // spare):
        out_ref[j * left : (j + 1) * left, bands:] = row_ref[keep:, j * spare : (j + 1) * spare]
    flags = mask_ref[rows - 1 : rows, :].astype(F32)
    out_ref[keep:, :tiles] = jnp.broadcast_to(flags, (out_ref.shape[0] - keep, tiles))


def unfold_row(row_ref, out_ref):
    cols, bands = out_ref.shape
    keep, left, spare = folding(cols, bands)
    out_ref[:keep, :] = row_ref[:keep, :bands]
    for j in range(bands // spare):
        out_ref[keep:, j * spare : (j + 1) * spare] = row_ref[j * left : (j + 1) * left, bands:]


def final_row(mask, cube):
    _, cols, bands = cube.shape
    row = pl.pallas_call(
        fetch_row_kernel,
        out_shape=pltpu.VMEM((cols, bands), F32),
        in_specs=[in_hbm()],
        out_specs=in_vmem(),
        scratch_shapes=[pltpu.SemaphoreType.DMA],
        compiler_params=params(54),
        name="fetch_row",
    )(cube)
    return pl.pallas_call(
        fold_row_kernel,
        out_shape=pltpu.VMEM((folding(cols, bands)[0] + 8, W), F32),
        in_specs=[in_vmem(), in_vmem()],
        out_specs=in_vmem(),
        compiler_params=params(12),
        name="fold_row",
    )(mask, row)


CUTS = ((0, 128), (128, 192))
BLOCK = 64
PIXEL_ONE, PAIR_ONE = 0, 1


def one_in(lane, count, width):
    return jnp.where(lax.broadcasted_iota(jnp.int32, (count, width), 1) == lane, 1.0, 0.0).astype(BF16)


def moments_kernel(
    mask_hbm, cube_hbm, halves_ref, valid_ref, first_ref, sums_ref, steps_ref, seams_ref, rest_ref, mask, raw, last, between_a, between_b, sems
):
    rows, cols, bands = raw.shape
    groups = [(t, c0, width) for t in range(rows // TILE) for c0, width in CUTS]

    def fetch(g):
        t, c0, width = groups[g]
        at = (pl.ds(t * TILE, TILE), pl.ds(c0, width))
        return pltpu.make_async_copy(cube_hbm.at[at], raw.at[at], sems.at[g])

    mask_copy = pltpu.make_async_copy(mask_hbm, mask, sems.at[len(groups)])
    mask_copy.start()
    for g in range(len(groups)):
        fetch(g).start()
    for ref in (sums_ref, steps_ref, seams_ref):
        ref[...] = jnp.zeros_like(ref)
    spare = W - bands
    for t, c0, width in groups:
        start = (t * cols + c0) * TILE
        for i in range(TILE):
            at = slice(start + i * width, start + (i + 1) * width)
            halves_ref[at, bands:W] = one_in(i % 2, width, spare)
            halves_ref[at, W + bands :] = jnp.zeros((width, spare), BF16)
    for buffer in (between_a, between_b):
        buffer[:, bands:W] = one_in(PAIR_ONE, buffer.shape[0], spare)
        buffer[:, W + bands :] = jnp.zeros((buffer.shape[0], spare), BF16)
    mask_copy.wait()

    def put(value, buffer, at, lanes, squares):
        count = value.shape[0]
        high = value.astype(BF16)
        low = (value - high.astype(F32)).astype(BF16)
        buffer[at : at + count, lanes] = high
        buffer[at : at + count, slice(W + lanes.start, W + lanes.stop)] = low
        parts = (low * low).reshape(count // 16, 16, -1)
        total = parts[0]
        for k in range(1, count // 16):
            total = total + parts[k]
        return squares + jnp.sum(total.astype(F32).reshape(2, 8, -1), 0)

    def product(ref, buffer, places, width):
        value = jnp.concatenate([buffer[at : at + width, :] for at in places], 0)
        ref[...] += dot_t(value[:, :W], value)

    lane_halves = (slice(0, 128), slice(128, bands))
    squares = {(k, h): jnp.zeros((8, lanes.stop - lanes.start), F32) for k in range(3) for h, lanes in enumerate(lane_halves)}
    pending = []
    for g, (t, c0, width) in enumerate(groups):
        between = (between_a, between_b)[g % 2]
        start = (t * cols + c0) * TILE
        fetch(g).wait()
        if c0 == 0:
            fill_validity(mask, t, valid_ref.at[t])
        gap = 1 if width == 128 else 2
        slot = 0
        for c in range(0, width, BLOCK):
            block = slice(c0 + c, c0 + c + BLOCK)
            valid = valid_ref[t, block, :128]
            for h, lanes in enumerate(lane_halves):
                if pending and slot % gap == 0:
                    product(*pending.pop(0))
                slot += 1
                weight = valid[:, : lanes.stop - lanes.start]
                previous = last[block, lanes] if t else None
                for i in range(TILE // 2):
                    row = t * TILE + 2 * i
                    first = raw[row, block, lanes] * weight
                    second = raw[row + 1, block, lanes] * weight
                    if previous is None:
                        first_ref[block, lanes] = first
                        gone = jnp.zeros_like(first)
                    else:
                        gone = first - previous
                        if i == 0:
                            gone = gone * (valid_ref[t - 1, block, : weight.shape[1]] * weight)
                    previous = second
                    at = start + 2 * i * width + c
                    squares[0, h] = put(first + second, halves_ref, at, lanes, squares[0, h])
                    squares[1, h] = put(second - first, halves_ref, at + width, lanes, squares[1, h])
                    squares[2, h] = put(gone, between, i * width + c, lanes, squares[2, h])
                last[block, lanes] = previous
        for late in pending:
            product(*late)
        pairs = range(TILE // 2)
        pending = [
            (sums_ref, halves_ref, [start + 2 * i * width for i in pairs], width),
            (steps_ref, halves_ref, [start + (2 * i + 1) * width for i in pairs], width),
            (seams_ref, between, [i * width for i in pairs], width),
        ]
    for late in pending:
        product(*late)
    for k in range(3):
        rest_ref[k, :, bands:] = jnp.zeros((8, W - bands), F32)
        for h, lanes in enumerate(lane_halves):
            rest_ref[k, :, lanes] = squares[k, h]


def moments(mask, cube):
    rows, cols, bands = cube.shape
    pixels = rows * cols
    widest = max(width for _, width in CUTS) * TILE // 2
    return pl.pallas_call(
        moments_kernel,
        out_shape=[
            pltpu.VMEM((pixels, 2 * W), BF16),
            pltpu.VMEM((rows // TILE, cols, W), F32),
            pltpu.VMEM((cols, bands), F32),
            pltpu.VMEM((W, 2 * W), F32),
            pltpu.VMEM((W, 2 * W), F32),
            pltpu.VMEM((W, 2 * W), F32),
            pltpu.VMEM((3, 8, W), F32),
        ],
        in_specs=[in_hbm(), in_hbm()],
        out_specs=[in_vmem()] * 7,
        scratch_shapes=[
            pltpu.SMEM(mask.shape, jnp.int32),
            pltpu.VMEM(cube.shape, F32),
            pltpu.VMEM((cols, bands), F32),
            pltpu.VMEM((widest, 2 * W), BF16),
            pltpu.VMEM((widest, 2 * W), BF16),
            pltpu.SemaphoreType.DMA((rows // TILE * len(CUTS) + 1,)),
        ],
        compiler_params=params(40),
        cost_estimate=pl.CostEstimate(flops=3 * 2 * pixels * W * W, bytes_accessed=4 * pixels * W, transcendentals=0),
        name="moments",
    )(mask, cube)


def indices(shape):
    return lax.broadcasted_iota(jnp.int32, shape, 0), lax.broadcasted_iota(jnp.int32, shape, 1)


def pack_kernel(
    core_ref, track_ref, valid_ref, first_ref, above_ref, sums_ref, steps_ref, seams_ref, rest_ref, mine_ref, other_ref, packed, buffer, above_row
):
    bands = first_ref.shape[1]
    half = bands // 2
    row, column = indices((W, W))
    on_diagonal = row == column
    first_valid = valid_ref[0]
    cols = first_valid.shape[0]
    pixel_row, tile = indices((cols, 128))
    keep = folding(cols, bands)[0]
    unfold_row(above_ref, above_row)
    flags = jnp.where(tile == lax.shift_right_logical(pixel_row, 3), above_ref[keep : keep + 1, :128], 0.0)
    flags = jnp.where(track_ref[0] > 0, jnp.sum(flags, 1, keepdims=True), 0.0)
    weight = first_valid * jnp.broadcast_to(flags, first_valid.shape)
    difference = (first_ref[...] - above_row[...]) * weight[:, :bands]
    high, low = split(difference)
    rest = difference - high.astype(F32)
    buffer[:, bands:W] = one_in(PAIR_ONE, buffer.shape[0], W - bands)
    buffer[:, W + bands :] = jnp.zeros((buffer.shape[0], W - bands), BF16)
    buffer[:, :bands] = high
    buffer[:, W : W + bands] = low
    steps = steps_ref[...]
    seams = seams_ref[...] + dot_t(buffer[:, :W], buffer[...])
    rests = [jnp.sum(rest_ref[k, :, :bands], 0, keepdims=True) for k in range(3)]
    rests[2] = rests[2] + jnp.sum(rest * rest, 0, keepdims=True)

    def whole(parts, squares):
        mixed = parts[:, W:]
        squares = jnp.concatenate([squares, jnp.zeros((1, W - bands), F32)], 1)
        return parts[:, :W] + mixed + mixed.T + jnp.where(on_diagonal, squares, 0.0)

    pixel = whole(0.5 * (sums_ref[...] + steps), 0.5 * (rests[0] + rests[1]))
    pixel = jnp.where(column == bands + PIXEL_ONE, 2.0 * pixel, pixel)
    pair = whole(steps + seams, rests[1] + rests[2])
    valid = valid_ref[:, :, :128]
    inner = jnp.sum(valid, 0)
    crossing = jnp.sum(valid[1:] * valid[:-1], 0)
    pixel_count = TILE * jnp.sum(inner, 0, keepdims=True)
    pair_count = jnp.sum((TILE - 1) * inner + crossing + weight[:, :128], 0, keepdims=True)
    out = jnp.where(column <= row, pair, 0.0)
    out = jnp.where((column > row) & (column <= bands + 1), pltpu.roll(pixel, 1, 1), out)
    out = jnp.where(column == bands + 2, pltpu.roll(pair, 2 - PAIR_ONE, 1), out)
    counts = jnp.where(row == 0, pixel_count[:, :1], 0.0)
    counts = jnp.where(row == 1, pair_count[:, :1], counts)
    packed[...] = jnp.where(column == bands + 3, counts, out)
    core = core_ref[0]
    mine_ref[...] = packed[pl.ds(pl.multiple_of(core * half, 8), half), :]
    other_ref[...] = packed[pl.ds(pl.multiple_of((1 - core) * half, 8), half), :]


def pack(core, track, valid, first, above, sums, steps, seams, rest):
    cols, bands = first.shape
    half = pltpu.VMEM((bands // 2, W), F32)
    return pl.pallas_call(
        pack_kernel,
        out_shape=[half, half],
        in_specs=[pl.BlockSpec(memory_space=pltpu.SMEM)] * 2 + [in_vmem()] * 7,
        out_specs=[in_vmem()] * 2,
        scratch_shapes=[pltpu.VMEM((W, W), F32), pltpu.VMEM((cols, 2 * W), BF16), pltpu.VMEM((cols, bands), F32)],
        compiler_params=params(12),
        name="pack",
    )(core, track, valid, first, above, sums, steps, seams, rest)


def square_sum(x):
    return jnp.sum(x * x)


QUICK_STEPS = 7


def careful(matrix, target, identity, row, column, bands, left, right):
    start = 1.0 / jnp.max(jnp.sum(jnp.abs(matrix), 1, keepdims=True))
    left[:W, :] = start * identity
    left[W:, :] = identity - start * matrix

    def more(carry):
        count, size = carry
        return (count < 24) & (size > 4e-6)

    def squaring(carry):
        count, _ = carry
        new = dot3(left[...], left[W:, :])
        left[:W, :] = left[:W, :] + new[:W]
        left[W:, :] = new[W:]
        return count + 1, square_sum(new[W:])

    lax.while_loop(more, squaring, (0, jnp.float32(1e9)))
    right[...] = dot3(left[:W, :], target)

    def refining(carry):
        count, _ = carry
        residual = target - dot6(matrix, right[...])
        change = dot3(left[:W, :], residual)
        gain = right[...] + change
        right[...] = gain
        return count + 1, square_sum(change) / square_sum(gain)

    def rough(carry):
        count, size = carry
        return (count < 8) & jnp.logical_not(size <= 1e-6)

    _, size = lax.while_loop(rough, refining, (0, jnp.float32(1e9)))

    @pl.when(jnp.logical_not(size <= 1e-6))
    def _():
        left[:W, :] = matrix
        right[...] = target

        def eliminate(k, _):
            here = row[:, 0:1] == k
            pivot_left = left[pl.ds(k, 1), :]
            pivot_right = right[pl.ds(k, 1), :]
            values = jnp.sum(jnp.where(column == k, left[:W, :], 0.0), 1, keepdims=True)
            pivot = jnp.sum(jnp.where(here, values, 0.0))
            factor = jnp.where(here, (values - 1.0) / pivot, values / pivot)
            left[:W, :] = left[:W, :] - factor * pivot_left
            right[...] = right[...] - factor * pivot_right
            return 0

        lax.fori_loop(0, bands, eliminate, 0)


def solve_kernel(bands, core_ref, mine_ref, other_ref, weights_ref, left, right):
    core = core_ref[0]
    packed = jnp.concatenate([mine_ref[...], other_ref[...]], 0)
    swapped = jnp.concatenate([other_ref[...], mine_ref[...]], 0)
    packed = jnp.where(core == 0, packed, swapped)
    packed = jnp.concatenate([packed, jnp.zeros((W - bands, W), F32)], 0)
    row, column = indices((W, W))
    on_diagonal = row == column
    inside = (row < bands) & (column < bands)
    pixel_count = packed[0:1, bands + 3 : bands + 4]
    pair_count = packed[1:2, bands + 3 : bands + 4]

    def whole(triangle):
        return triangle + triangle.T - jnp.where(on_diagonal, triangle, 0.0)

    pixel = whole(jnp.where((column >= row) & (column <= bands), pltpu.roll(packed, W - 1, 1), 0.0))
    lower = jnp.where((column <= row) & inside, packed, 0.0)
    sums = jnp.where((column == bands) & (row < bands), pltpu.roll(packed, W - 2, 1), 0.0)
    pair = whole(lower + sums)

    def covariance(square, count):
        total = square[bands : bands + 1, :]
        total_rows = square[:, bands : bands + 1]
        return jnp.where(inside, (square - total_rows * total / count) / (count - 1.0), 0.0)

    signal = covariance(pixel, pixel_count)
    noise = covariance(pair, pair_count)
    combined = signal + noise
    mean = pixel[:, bands : bands + 1] / pixel_count
    diagonal = jnp.where(on_diagonal, combined, 0.0)
    scale_row = lax.rsqrt(jnp.where(column[0:1] < bands, jnp.sum(diagonal, 0, keepdims=True), 1.0))
    scale_column = lax.rsqrt(jnp.where(row[:, 0:1] < bands, jnp.sum(diagonal, 1, keepdims=True), 1.0))
    identity = jnp.where(on_diagonal, 1.0, 0.0)
    matrix = jnp.where(inside, combined * scale_column * scale_row, identity)
    target = noise * scale_column * scale_row

    coarse = matrix.astype(BF16)
    square = dot(coarse, coarse)
    shrink = lax.rsqrt(jnp.max(jnp.sum(jnp.abs(square), 1, keepdims=True), 0, keepdims=True))
    near = 2.0 * shrink * matrix - shrink * shrink * square
    inverse = 2.0 * shrink * identity - shrink * shrink * matrix

    def double(near, inverse):
        step = dot(near.astype(BF16), jnp.concatenate([near.astype(BF16), inverse.astype(BF16)], 1))
        return 2.0 * near - step[:, :W], 2.0 * inverse - step[:, W:]

    for _ in range(QUICK_STEPS):
        near, inverse = double(near, inverse)
    off = identity - dot3(matrix, inverse)
    inverse = inverse + dot(inverse.astype(BF16), off.astype(BF16))
    first = dot3(inverse, target)
    change = dot(inverse.astype(BF16), (target - dot3(matrix, first)).astype(BF16))
    right[...] = first + change
    off_size = square_sum(off)
    done = square_sum(change) * off_size * off_size <= 1e-8 * square_sum(first)

    @pl.when(jnp.logical_not(done & (off_size < 0.25)))
    def _():
        careful(matrix, target, identity, row, column, bands, left, right)

    gain = right[...] * scale_column * (1.0 / scale_row)
    shift = jnp.sum(jnp.where(row < bands, mean, 0.0) * gain, 0, keepdims=True)
    weights = jnp.where(row == bands + PIXEL_ONE, shift, jnp.where(inside, 0.5 * (identity - gain), 0.0))
    high, low = split(weights)
    weights_ref[:W, :] = high
    weights_ref[W : 2 * W, :] = high
    weights_ref[2 * W :, :] = low


def solve(core, mine, other, bands):
    return pl.pallas_call(
        functools.partial(solve_kernel, bands),
        out_shape=pltpu.VMEM((3 * W, W), BF16),
        in_specs=[pl.BlockSpec(memory_space=pltpu.SMEM), in_vmem(), in_vmem()],
        out_specs=in_vmem(),
        scratch_shapes=[pltpu.VMEM((2 * W, W), F32), pltpu.VMEM((W, W), F32)],
        compiler_params=params(16),
        name="solve",
    )(core, mine, other)


def filter_kernel(halves_ref, valid_ref, weights_ref, out_hbm, staged, sems):
    rows, cols, bands = staged.shape
    copies = []
    for t in range(rows // TILE):
        for c0, width in CUTS:
            at = (t * cols + c0) * TILE
            valid = valid_ref.at[t, c0 : c0 + width, :bands]
            for i in range(TILE // 2):
                halves = halves_ref[at + 2 * i * width : at + 2 * (i + 1) * width, :]
                result = dot(jnp.concatenate([halves, halves[:, :W]], 1), weights_ref[...])
                half_sum, half_step = result[:width, :bands], result[width:, :bands]
                row = t * TILE + 2 * i
                staged[row, c0 : c0 + width] = valid[...] * (half_sum - half_step)
                staged[row + 1, c0 : c0 + width] = valid[...] * (half_sum + half_step)
                part = (pl.ds(row, 2), pl.ds(c0, width))
                copies.append(pltpu.make_async_copy(staged.at[part], out_hbm.at[part], sems.at[len(copies)]))
                copies[-1].start()
    for copy in copies:
        copy.wait()


def apply_filter(halves, valid, weights, shape):
    rows, cols, bands = shape
    pixels = rows * cols
    return pl.pallas_call(
        filter_kernel,
        out_shape=jax.ShapeDtypeStruct(shape, F32),
        in_specs=[in_vmem()] * 3,
        out_specs=in_hbm(),
        scratch_shapes=[pltpu.VMEM(shape, F32), pltpu.SemaphoreType.DMA((rows // 2 * len(CUTS),))],
        compiler_params=params(24),
        cost_estimate=pl.CostEstimate(flops=3 * 2 * pixels * W * W, bytes_accessed=4 * pixels * W, transcendentals=0),
        name="filter",
    )(halves, valid, weights)


RING = 4


def permute(x, target):
    track, strip = lax.axis_size("track"), lax.axis_size("strip")
    pairs = []
    for i in range(track):
        for j in range(strip):
            y, z, chip, core = target(i // RING, i % RING, j // 2, j % 2)
            pairs.append((i * strip + j, (y * RING + z) * strip + chip * 2 + core))
    return lax.ppermute(x, ("track", "strip"), pairs)


def other_core(x):
    return permute(x, lambda y, z, chip, core: (y, z, chip, 1 - core))


PARTNER = {1: (1, 0, 3, 2), 2: (2, 3, 0, 1), 3: (3, 2, 1, 0)}


def ring_sum(x, axes):
    def exchanged(which):
        def target(y, z, chip, core):
            place = [y, z, chip]
            axis = axes[core]
            place[axis] = PARTNER[which if core == 0 else RING - which][place[axis]]
            return (*place, core)

        return permute(x, target)

    return lax.optimization_barrier(x + exchanged(1) + exchanged(3) + exchanged(2))


def per_device(cube, mask):
    bands = cube.shape[2]
    size = lax.axis_size("track")
    above = lax.ppermute(final_row(mask, cube), "track", [(i, (i + 1) % size) for i in range(size)])
    core = (lax.axis_index("strip") % 2).astype(jnp.int32)[None]
    track = lax.axis_index("track").astype(jnp.int32)[None]
    halves, valid, first, sums, steps, seams, rest = moments(mask, cube)
    mine, other = pack(core, track, valid, first, above, sums, steps, seams, rest)
    total = mine + other_core(other)
    for axes in ((0, 1), (1, 2), (2, 0)):
        total = ring_sum(total, axes)
    weights = solve(core, total, other_core(total), bands)
    return apply_filter(halves, valid, weights, cube.shape)


def solution(mesh):
    return jax.shard_map(
        per_device,
        mesh=mesh,
        in_specs=(P("track", "strip", None), P("track", "strip")),
        out_specs=P("track", "strip", None),
        check_vma=False,
    )
```

```python
import functools

import jax
import jax.numpy as jnp
from jax import lax
from jax.experimental import pallas as pl
from jax.experimental.pallas import tpu as pltpu
from jax.sharding import PartitionSpec as P

TILE = 8
W = 256
F32 = jnp.float32
BF16 = jnp.bfloat16
MIB = 2**20


def split(x):
    high = x.astype(BF16)
    return high, (x - high.astype(F32)).astype(BF16)


def split3(x):
    high = x.astype(BF16)
    rest = x - high.astype(F32)
    middle = rest.astype(BF16)
    return high, middle, (rest - middle.astype(F32)).astype(BF16)


def dot(a, b):
    return lax.dot_general(a, b, (((1,), (0,)), ((), ())), preferred_element_type=F32)


def dot_t(a, b):
    return lax.dot_general(a, b, (((0,), (0,)), ((), ())), preferred_element_type=F32)


def dot3(a, b):
    a_high, a_low = split(a)
    b_high, b_low = split(b)
    return dot(
        jnp.concatenate([a_high, a_high, a_low], 1),
        jnp.concatenate([b_high, b_low, b_high], 0),
    )


def dot6(a, b):
    ah, am, al = split3(a)
    bh, bm, bl = split3(b)
    return dot(
        jnp.concatenate([ah, ah, am, ah, am, al], 1),
        jnp.concatenate([bh, bm, bh, bl, bm, bh], 0),
    )


def in_vmem():
    return pl.BlockSpec(memory_space=pltpu.VMEM)


def in_hbm():
    return pl.BlockSpec(memory_space=pltpu.HBM)


def params(mib):
    return pltpu.CompilerParams(vmem_limit_bytes=mib * MIB)


def fill_validity(mask_ref, tile_row, out_ref):
    for c in range(out_ref.shape[0] // TILE):
        value = mask_ref[tile_row, c].astype(F32)
        out_ref[c * TILE : (c + 1) * TILE, :] = jnp.full((TILE, out_ref.shape[1]), value, F32)


def folding(cols, bands):
    keep = cols * bands // W
    return keep, cols - keep, W - bands


def fetch_row_kernel(cube_hbm, out_ref, sem):
    copy = pltpu.make_async_copy(cube_hbm.at[cube_hbm.shape[0] - 1], out_ref, sem)
    copy.start()
    copy.wait()


def fold_row_kernel(mask_ref, row_ref, out_ref):
    rows, tiles = mask_ref.shape
    cols, bands = row_ref.shape
    keep, left, spare = folding(cols, bands)
    out_ref[:keep, :bands] = row_ref[:keep, :]
    for j in range(bands // spare):
        out_ref[j * left : (j + 1) * left, bands:] = row_ref[keep:, j * spare : (j + 1) * spare]
    flags = mask_ref[rows - 1 : rows, :].astype(F32)
    out_ref[keep:, :tiles] = jnp.broadcast_to(flags, (out_ref.shape[0] - keep, tiles))


def unfold_row(row_ref, out_ref):
    cols, bands = out_ref.shape
    keep, left, spare = folding(cols, bands)
    out_ref[:keep, :] = row_ref[:keep, :bands]
    for j in range(bands // spare):
        out_ref[keep:, j * spare : (j + 1) * spare] = row_ref[j * left : (j + 1) * left, bands:]


def final_row(mask, cube):
    _, cols, bands = cube.shape
    row = pl.pallas_call(
        fetch_row_kernel,
        out_shape=pltpu.VMEM((cols, bands), F32),
        in_specs=[in_hbm()],
        out_specs=in_vmem(),
        scratch_shapes=[pltpu.SemaphoreType.DMA],
        compiler_params=params(54),
        name="fetch_row",
    )(cube)
    return pl.pallas_call(
        fold_row_kernel,
        out_shape=pltpu.VMEM((folding(cols, bands)[0] + 8, W), F32),
        in_specs=[in_vmem(), in_vmem()],
        out_specs=in_vmem(),
        compiler_params=params(12),
        name="fold_row",
    )(mask, row)


CUTS = ((0, 128), (128, 192))
BLOCK = 64
PIXEL_ONE, PAIR_ONE = 0, 1


def one_in(lane, count, width):
    return jnp.where(lax.broadcasted_iota(jnp.int32, (count, width), 1) == lane, 1.0, 0.0).astype(BF16)


def moments_kernel(
    mask_hbm, cube_hbm, halves_ref, valid_ref, first_ref, sums_ref, steps_ref, seams_ref, rest_ref, mask, raw, last, between_a, between_b, sems
):
    rows, cols, bands = raw.shape
    groups = [(t, c0, width) for t in range(rows // TILE) for c0, width in CUTS]

    def fetch(g):
        t, c0, width = groups[g]
        at = (pl.ds(t * TILE, TILE), pl.ds(c0, width))
        return pltpu.make_async_copy(cube_hbm.at[at], raw.at[at], sems.at[g])

    mask_copy = pltpu.make_async_copy(mask_hbm, mask, sems.at[len(groups)])
    mask_copy.start()
    for g in range(len(groups)):
        fetch(g).start()
    for ref in (sums_ref, steps_ref, seams_ref):
        ref[...] = jnp.zeros_like(ref)
    spare = W - bands
    for t, c0, width in groups:
        start = (t * cols + c0) * TILE
        for i in range(TILE):
            at = slice(start + i * width, start + (i + 1) * width)
            halves_ref[at, bands:W] = one_in(i % 2, width, spare)
            halves_ref[at, W + bands :] = jnp.zeros((width, spare), BF16)
    for buffer in (between_a, between_b):
        buffer[:, bands:W] = one_in(PAIR_ONE, buffer.shape[0], spare)
        buffer[:, W + bands :] = jnp.zeros((buffer.shape[0], spare), BF16)
    mask_copy.wait()

    def put(value, buffer, at, lanes, squares):
        count = value.shape[0]
        high = value.astype(BF16)
        low = (value - high.astype(F32)).astype(BF16)
        buffer[at : at + count, lanes] = high
        buffer[at : at + count, slice(W + lanes.start, W + lanes.stop)] = low
        parts = (low * low).reshape(count // 16, 16, -1)
        total = parts[0]
        for k in range(1, count // 16):
            total = total + parts[k]
        return squares + jnp.sum(total.astype(F32).reshape(2, 8, -1), 0)

    def product(ref, buffer, places, width):
        value = jnp.concatenate([buffer[at : at + width, :] for at in places], 0)
        ref[...] += dot_t(value[:, :W], value)

    lane_halves = (slice(0, 128), slice(128, bands))
    squares = {(k, h): jnp.zeros((8, lanes.stop - lanes.start), F32) for k in range(3) for h, lanes in enumerate(lane_halves)}
    pending = []
    for g, (t, c0, width) in enumerate(groups):
        between = (between_a, between_b)[g % 2]
        start = (t * cols + c0) * TILE
        fetch(g).wait()
        if c0 == 0:
            fill_validity(mask, t, valid_ref.at[t])
        gap = 1 if width == 128 else 2
        slot = 0
        for c in range(0, width, BLOCK):
            block = slice(c0 + c, c0 + c + BLOCK)
            valid = valid_ref[t, block, :128]
            for h, lanes in enumerate(lane_halves):
                if pending and slot % gap == 0:
                    product(*pending.pop(0))
                slot += 1
                weight = valid[:, : lanes.stop - lanes.start]
                previous = last[block, lanes] if t else None
                for i in range(TILE // 2):
                    row = t * TILE + 2 * i
                    first = raw[row, block, lanes] * weight
                    second = raw[row + 1, block, lanes] * weight
                    if previous is None:
                        first_ref[block, lanes] = first
                        gone = jnp.zeros_like(first)
                    else:
                        gone = first - previous
                        if i == 0:
                            gone = gone * (valid_ref[t - 1, block, : weight.shape[1]] * weight)
                    previous = second
                    at = start + 2 * i * width + c
                    squares[0, h] = put(first + second, halves_ref, at, lanes, squares[0, h])
                    squares[1, h] = put(second - first, halves_ref, at + width, lanes, squares[1, h])
                    squares[2, h] = put(gone, between, i * width + c, lanes, squares[2, h])
                last[block, lanes] = previous
        for late in pending:
            product(*late)
        pairs = range(TILE // 2)
        pending = [
            (sums_ref, halves_ref, [start + 2 * i * width for i in pairs], width),
            (steps_ref, halves_ref, [start + (2 * i + 1) * width for i in pairs], width),
            (seams_ref, between, [i * width for i in pairs], width),
        ]
    for late in pending:
        product(*late)
    for k in range(3):
        rest_ref[k, :, bands:] = jnp.zeros((8, W - bands), F32)
        for h, lanes in enumerate(lane_halves):
            rest_ref[k, :, lanes] = squares[k, h]


def moments(mask, cube):
    rows, cols, bands = cube.shape
    pixels = rows * cols
    widest = max(width for _, width in CUTS) * TILE // 2
    return pl.pallas_call(
        moments_kernel,
        out_shape=[
            pltpu.VMEM((pixels, 2 * W), BF16),
            pltpu.VMEM((rows // TILE, cols, W), F32),
            pltpu.VMEM((cols, bands), F32),
            pltpu.VMEM((W, 2 * W), F32),
            pltpu.VMEM((W, 2 * W), F32),
            pltpu.VMEM((W, 2 * W), F32),
            pltpu.VMEM((3, 8, W), F32),
        ],
        in_specs=[in_hbm(), in_hbm()],
        out_specs=[in_vmem()] * 7,
        scratch_shapes=[
            pltpu.SMEM(mask.shape, jnp.int32),
            pltpu.VMEM(cube.shape, F32),
            pltpu.VMEM((cols, bands), F32),
            pltpu.VMEM((widest, 2 * W), BF16),
            pltpu.VMEM((widest, 2 * W), BF16),
            pltpu.SemaphoreType.DMA((rows // TILE * len(CUTS) + 1,)),
        ],
        compiler_params=params(40),
        cost_estimate=pl.CostEstimate(flops=3 * 2 * pixels * W * W, bytes_accessed=4 * pixels * W, transcendentals=0),
        name="moments",
    )(mask, cube)


def indices(shape):
    return lax.broadcasted_iota(jnp.int32, shape, 0), lax.broadcasted_iota(jnp.int32, shape, 1)


def pack_kernel(
    core_ref, track_ref, valid_ref, first_ref, above_ref, sums_ref, steps_ref, seams_ref, rest_ref, mine_ref, other_ref, packed, buffer, above_row
):
    bands = first_ref.shape[1]
    half = bands // 2
    row, column = indices((W, W))
    on_diagonal = row == column
    first_valid = valid_ref[0]
    cols = first_valid.shape[0]
    pixel_row, tile = indices((cols, 128))
    keep = folding(cols, bands)[0]
    unfold_row(above_ref, above_row)
    flags = jnp.where(tile == lax.shift_right_logical(pixel_row, 3), above_ref[keep : keep + 1, :128], 0.0)
    flags = jnp.where(track_ref[0] > 0, jnp.sum(flags, 1, keepdims=True), 0.0)
    weight = first_valid * jnp.broadcast_to(flags, first_valid.shape)
    difference = (first_ref[...] - above_row[...]) * weight[:, :bands]
    high, low = split(difference)
    rest = difference - high.astype(F32)
    buffer[:, bands:W] = one_in(PAIR_ONE, buffer.shape[0], W - bands)
    buffer[:, W + bands :] = jnp.zeros((buffer.shape[0], W - bands), BF16)
    buffer[:, :bands] = high
    buffer[:, W : W + bands] = low
    steps = steps_ref[...]
    seams = seams_ref[...] + dot_t(buffer[:, :W], buffer[...])
    rests = [jnp.sum(rest_ref[k, :, :bands], 0, keepdims=True) for k in range(3)]
    rests[2] = rests[2] + jnp.sum(rest * rest, 0, keepdims=True)

    def whole(parts, squares):
        mixed = parts[:, W:]
        squares = jnp.concatenate([squares, jnp.zeros((1, W - bands), F32)], 1)
        return parts[:, :W] + mixed + mixed.T + jnp.where(on_diagonal, squares, 0.0)

    pixel = whole(0.5 * (sums_ref[...] + steps), 0.5 * (rests[0] + rests[1]))
    pixel = jnp.where(column == bands + PIXEL_ONE, 2.0 * pixel, pixel)
    pair = whole(steps + seams, rests[1] + rests[2])
    valid = valid_ref[:, :, :128]
    inner = jnp.sum(valid, 0)
    crossing = jnp.sum(valid[1:] * valid[:-1], 0)
    pixel_count = TILE * jnp.sum(inner, 0, keepdims=True)
    pair_count = jnp.sum((TILE - 1) * inner + crossing + weight[:, :128], 0, keepdims=True)
    out = jnp.where(column <= row, pair, 0.0)
    out = jnp.where((column > row) & (column <= bands + 1), pltpu.roll(pixel, 1, 1), out)
    out = jnp.where(column == bands + 2, pltpu.roll(pair, 2 - PAIR_ONE, 1), out)
    counts = jnp.where(row == 0, pixel_count[:, :1], 0.0)
    counts = jnp.where(row == 1, pair_count[:, :1], counts)
    packed[...] = jnp.where(column == bands + 3, counts, out)
    core = core_ref[0]
    mine_ref[...] = packed[pl.ds(pl.multiple_of(core * half, 8), half), :]
    other_ref[...] = packed[pl.ds(pl.multiple_of((1 - core) * half, 8), half), :]


def pack(core, track, valid, first, above, sums, steps, seams, rest):
    cols, bands = first.shape
    half = pltpu.VMEM((bands // 2, W), F32)
    return pl.pallas_call(
        pack_kernel,
        out_shape=[half, half],
        in_specs=[pl.BlockSpec(memory_space=pltpu.SMEM)] * 2 + [in_vmem()] * 7,
        out_specs=[in_vmem()] * 2,
        scratch_shapes=[pltpu.VMEM((W, W), F32), pltpu.VMEM((cols, 2 * W), BF16), pltpu.VMEM((cols, bands), F32)],
        compiler_params=params(12),
        name="pack",
    )(core, track, valid, first, above, sums, steps, seams, rest)


def square_sum(x):
    return jnp.sum(x * x)


QUICK_STEPS = 7


def careful(matrix, target, identity, row, column, bands, left, right):
    start = 1.0 / jnp.max(jnp.sum(jnp.abs(matrix), 1, keepdims=True))
    left[:W, :] = start * identity
    left[W:, :] = identity - start * matrix

    def more(carry):
        count, size = carry
        return (count < 24) & (size > 4e-6)

    def squaring(carry):
        count, _ = carry
        new = dot3(left[...], left[W:, :])
        left[:W, :] = left[:W, :] + new[:W]
        left[W:, :] = new[W:]
        return count + 1, square_sum(new[W:])

    lax.while_loop(more, squaring, (0, jnp.float32(1e9)))
    right[...] = dot3(left[:W, :], target)

    def refining(carry):
        count, _ = carry
        residual = target - dot6(matrix, right[...])
        change = dot3(left[:W, :], residual)
        gain = right[...] + change
        right[...] = gain
        return count + 1, square_sum(change) / square_sum(gain)

    def rough(carry):
        count, size = carry
        return (count < 8) & jnp.logical_not(size <= 1e-6)

    _, size = lax.while_loop(rough, refining, (0, jnp.float32(1e9)))

    @pl.when(jnp.logical_not(size <= 1e-6))
    def _():
        left[:W, :] = matrix
        right[...] = target

        def eliminate(k, _):
            here = row[:, 0:1] == k
            pivot_left = left[pl.ds(k, 1), :]
            pivot_right = right[pl.ds(k, 1), :]
            values = jnp.sum(jnp.where(column == k, left[:W, :], 0.0), 1, keepdims=True)
            pivot = jnp.sum(jnp.where(here, values, 0.0))
            factor = jnp.where(here, (values - 1.0) / pivot, values / pivot)
            left[:W, :] = left[:W, :] - factor * pivot_left
            right[...] = right[...] - factor * pivot_right
            return 0

        lax.fori_loop(0, bands, eliminate, 0)


def solve_kernel(bands, core_ref, mine_ref, other_ref, weights_ref, left, right):
    core = core_ref[0]
    packed = jnp.concatenate([mine_ref[...], other_ref[...]], 0)
    swapped = jnp.concatenate([other_ref[...], mine_ref[...]], 0)
    packed = jnp.where(core == 0, packed, swapped)
    packed = jnp.concatenate([packed, jnp.zeros((W - bands, W), F32)], 0)
    row, column = indices((W, W))
    on_diagonal = row == column
    inside = (row < bands) & (column < bands)
    pixel_count = packed[0:1, bands + 3 : bands + 4]
    pair_count = packed[1:2, bands + 3 : bands + 4]

    def whole(triangle):
        return triangle + triangle.T - jnp.where(on_diagonal, triangle, 0.0)

    pixel = whole(jnp.where((column >= row) & (column <= bands), pltpu.roll(packed, W - 1, 1), 0.0))
    lower = jnp.where((column <= row) & inside, packed, 0.0)
    sums = jnp.where((column == bands) & (row < bands), pltpu.roll(packed, W - 2, 1), 0.0)
    pair = whole(lower + sums)

    def covariance(square, count):
        total = square[bands : bands + 1, :]
        total_rows = square[:, bands : bands + 1]
        return jnp.where(inside, (square - total_rows * total / count) / (count - 1.0), 0.0)

    signal = covariance(pixel, pixel_count)
    noise = covariance(pair, pair_count)
    combined = signal + noise
    mean = pixel[:, bands : bands + 1] / pixel_count
    diagonal = jnp.where(on_diagonal, combined, 0.0)
    scale_row = lax.rsqrt(jnp.where(column[0:1] < bands, jnp.sum(diagonal, 0, keepdims=True), 1.0))
    scale_column = lax.rsqrt(jnp.where(row[:, 0:1] < bands, jnp.sum(diagonal, 1, keepdims=True), 1.0))
    identity = jnp.where(on_diagonal, 1.0, 0.0)
    matrix = jnp.where(inside, combined * scale_column * scale_row, identity)
    target = noise * scale_column * scale_row

    coarse = matrix.astype(BF16)
    square = dot(coarse, coarse)
    shrink = lax.rsqrt(jnp.max(jnp.sum(jnp.abs(square), 1, keepdims=True), 0, keepdims=True))
    near = 2.0 * shrink * matrix - shrink * shrink * square
    inverse = 2.0 * shrink * identity - shrink * shrink * matrix

    def double(near, inverse):
        step = dot(near.astype(BF16), jnp.concatenate([near.astype(BF16), inverse.astype(BF16)], 1))
        return 2.0 * near - step[:, :W], 2.0 * inverse - step[:, W:]

    for _ in range(QUICK_STEPS):
        near, inverse = double(near, inverse)
    off = identity - dot3(matrix, inverse)
    inverse = inverse + dot(inverse.astype(BF16), off.astype(BF16))
    first = dot3(inverse, target)
    change = dot(inverse.astype(BF16), (target - dot3(matrix, first)).astype(BF16))
    right[...] = first + change
    off_size = square_sum(off)
    done = square_sum(change) * off_size * off_size <= 1e-8 * square_sum(first)

    @pl.when(jnp.logical_not(done & (off_size < 0.25)))
    def _():
        careful(matrix, target, identity, row, column, bands, left, right)

    gain = right[...] * scale_column * (1.0 / scale_row)
    shift = jnp.sum(jnp.where(row < bands, mean, 0.0) * gain, 0, keepdims=True)
    weights = jnp.where(row == bands + PIXEL_ONE, shift, jnp.where(inside, 0.5 * (identity - gain), 0.0))
    high, low = split(weights)
    weights_ref[:W, :] = high
    weights_ref[W : 2 * W, :] = high
    weights_ref[2 * W :, :] = low


def solve(core, mine, other, bands):
    return pl.pallas_call(
        functools.partial(solve_kernel, bands),
        out_shape=pltpu.VMEM((3 * W, W), BF16),
        in_specs=[pl.BlockSpec(memory_space=pltpu.SMEM), in_vmem(), in_vmem()],
        out_specs=in_vmem(),
        scratch_shapes=[pltpu.VMEM((2 * W, W), F32), pltpu.VMEM((W, W), F32)],
        compiler_params=params(16),
        name="solve",
    )(core, mine, other)


def filter_kernel(halves_ref, valid_ref, weights_ref, out_hbm, staged, sems):
    rows, cols, bands = staged.shape
    copies = []
    for t in range(rows // TILE):
        for c0, width in CUTS:
            at = (t * cols + c0) * TILE
            valid = valid_ref.at[t, c0 : c0 + width, :bands]
            for i in range(TILE // 2):
                halves = halves_ref[at + 2 * i * width : at + 2 * (i + 1) * width, :]
                result = dot(jnp.concatenate([halves, halves[:, :W]], 1), weights_ref[...])
                half_sum, half_step = result[:width, :bands], result[width:, :bands]
                row = t * TILE + 2 * i
                staged[row, c0 : c0 + width] = valid[...] * (half_sum - half_step)
                staged[row + 1, c0 : c0 + width] = valid[...] * (half_sum + half_step)
                part = (pl.ds(row, 2), pl.ds(c0, width))
                copies.append(pltpu.make_async_copy(staged.at[part], out_hbm.at[part], sems.at[len(copies)]))
                copies[-1].start()
    for copy in copies:
        copy.wait()


def apply_filter(halves, valid, weights, shape):
    rows, cols, bands = shape
    pixels = rows * cols
    return pl.pallas_call(
        filter_kernel,
        out_shape=jax.ShapeDtypeStruct(shape, F32),
        in_specs=[in_vmem()] * 3,
        out_specs=in_hbm(),
        scratch_shapes=[pltpu.VMEM(shape, F32), pltpu.SemaphoreType.DMA((rows // 2 * len(CUTS),))],
        compiler_params=params(24),
        cost_estimate=pl.CostEstimate(flops=3 * 2 * pixels * W * W, bytes_accessed=4 * pixels * W, transcendentals=0),
        name="filter",
    )(halves, valid, weights)


RING = 4


def permute(x, target):
    track, strip = lax.axis_size("track"), lax.axis_size("strip")
    pairs = []
    for i in range(track):
        for j in range(strip):
            y, z, chip, core = target(i // RING, i % RING, j // 2, j % 2)
            pairs.append((i * strip + j, (y * RING + z) * strip + chip * 2 + core))
    return lax.ppermute(x, ("track", "strip"), pairs)


def other_core(x):
    return permute(x, lambda y, z, chip, core: (y, z, chip, 1 - core))


PARTNER = {1: (1, 0, 3, 2), 2: (2, 3, 0, 1), 3: (3, 2, 1, 0)}


def ring_sum(x, axes):
    def exchanged(which):
        def target(y, z, chip, core):
            place = [y, z, chip]
            axis = axes[core]
            place[axis] = PARTNER[which if core == 0 else RING - which][place[axis]]
            return (*place, core)

        return permute(x, target)

    return lax.optimization_barrier(x + exchanged(1) + exchanged(3) + exchanged(2))


def per_device(cube, mask):
    bands = cube.shape[2]
    size = lax.axis_size("track")
    above = lax.ppermute(final_row(mask, cube), "track", [(i, (i + 1) % size) for i in range(size)])
    core = (lax.axis_index("strip") % 2).astype(jnp.int32)[None]
    track = lax.axis_index("track").astype(jnp.int32)[None]
    halves, valid, first, sums, steps, seams, rest = moments(mask, cube)
    mine, other = pack(core, track, valid, first, above, sums, steps, seams, rest)
    total = mine + other_core(other)
    for axes in ((2, 0), (0, 1), (1, 2)):
        total = ring_sum(total, axes)
    weights = solve(core, total, other_core(total), bands)
    return apply_filter(halves, valid, weights, cube.shape)


def solution(mesh):
    return jax.shard_map(
        per_device,
        mesh=mesh,
        in_specs=(P("track", "strip", None), P("track", "strip")),
        out_specs=P("track", "strip", None),
        check_vma=False,
    )
```

```python
import functools

import jax
import jax.numpy as jnp
from jax import lax
from jax.experimental import pallas as pl
from jax.experimental.pallas import tpu as pltpu
from jax.sharding import PartitionSpec as P

TILE = 8
W = 256
F32 = jnp.float32
BF16 = jnp.bfloat16
MIB = 2**20


def split(x):
    high = x.astype(BF16)
    return high, (x - high.astype(F32)).astype(BF16)


def split3(x):
    high = x.astype(BF16)
    rest = x - high.astype(F32)
    middle = rest.astype(BF16)
    return high, middle, (rest - middle.astype(F32)).astype(BF16)


def dot(a, b):
    return lax.dot_general(a, b, (((1,), (0,)), ((), ())), preferred_element_type=F32)


def dot_t(a, b):
    return lax.dot_general(a, b, (((0,), (0,)), ((), ())), preferred_element_type=F32)


def dot3(a, b):
    a_high, a_low = split(a)
    b_high, b_low = split(b)
    return dot(
        jnp.concatenate([a_high, a_high, a_low], 1),
        jnp.concatenate([b_high, b_low, b_high], 0),
    )


def dot6(a, b):
    ah, am, al = split3(a)
    bh, bm, bl = split3(b)
    return dot(
        jnp.concatenate([ah, ah, am, ah, am, al], 1),
        jnp.concatenate([bh, bm, bh, bl, bm, bh], 0),
    )


def in_vmem():
    return pl.BlockSpec(memory_space=pltpu.VMEM)


def in_hbm():
    return pl.BlockSpec(memory_space=pltpu.HBM)


def params(mib):
    return pltpu.CompilerParams(vmem_limit_bytes=mib * MIB)


def fill_validity(mask_ref, tile_row, out_ref):
    for c in range(out_ref.shape[0] // TILE):
        value = mask_ref[tile_row, c].astype(F32)
        out_ref[c * TILE : (c + 1) * TILE, :] = jnp.full((TILE, out_ref.shape[1]), value, F32)


def folding(cols, bands):
    keep = cols * bands // W
    return keep, cols - keep, W - bands


def fetch_row_kernel(cube_hbm, out_ref, sem):
    copy = pltpu.make_async_copy(cube_hbm.at[cube_hbm.shape[0] - 1], out_ref, sem)
    copy.start()
    copy.wait()


def fold_row_kernel(mask_ref, row_ref, out_ref):
    rows, tiles = mask_ref.shape
    cols, bands = row_ref.shape
    keep, left, spare = folding(cols, bands)
    out_ref[:keep, :bands] = row_ref[:keep, :]
    for j in range(bands // spare):
        out_ref[j * left : (j + 1) * left, bands:] = row_ref[keep:, j * spare : (j + 1) * spare]
    flags = mask_ref[rows - 1 : rows, :].astype(F32)
    out_ref[keep:, :tiles] = jnp.broadcast_to(flags, (out_ref.shape[0] - keep, tiles))


def unfold_row(row_ref, out_ref):
    cols, bands = out_ref.shape
    keep, left, spare = folding(cols, bands)
    out_ref[:keep, :] = row_ref[:keep, :bands]
    for j in range(bands // spare):
        out_ref[keep:, j * spare : (j + 1) * spare] = row_ref[j * left : (j + 1) * left, bands:]


def final_row(mask, cube):
    _, cols, bands = cube.shape
    row = pl.pallas_call(
        fetch_row_kernel,
        out_shape=pltpu.VMEM((cols, bands), F32),
        in_specs=[in_hbm()],
        out_specs=in_vmem(),
        scratch_shapes=[pltpu.SemaphoreType.DMA],
        compiler_params=params(54),
        name="fetch_row",
    )(cube)
    return pl.pallas_call(
        fold_row_kernel,
        out_shape=pltpu.VMEM((folding(cols, bands)[0] + 8, W), F32),
        in_specs=[in_vmem(), in_vmem()],
        out_specs=in_vmem(),
        compiler_params=params(12),
        name="fold_row",
    )(mask, row)


CUTS = ((0, 128), (128, 192))
BLOCK = 64
PIXEL_ONE, PAIR_ONE = 0, 1


def one_in(lane, count, width):
    return jnp.where(lax.broadcasted_iota(jnp.int32, (count, width), 1) == lane, 1.0, 0.0).astype(BF16)


def moments_kernel(
    mask_hbm, cube_hbm, halves_ref, valid_ref, first_ref, sums_ref, steps_ref, seams_ref, rest_ref, mask, raw, last, between_a, between_b, sems
):
    rows, cols, bands = raw.shape
    groups = [(t, c0, width) for t in range(rows // TILE) for c0, width in CUTS]

    def fetch(g):
        t, c0, width = groups[g]
        at = (pl.ds(t * TILE, TILE), pl.ds(c0, width))
        return pltpu.make_async_copy(cube_hbm.at[at], raw.at[at], sems.at[g])

    mask_copy = pltpu.make_async_copy(mask_hbm, mask, sems.at[len(groups)])
    mask_copy.start()
    for g in range(len(groups)):
        fetch(g).start()
    for ref in (sums_ref, steps_ref, seams_ref):
        ref[...] = jnp.zeros_like(ref)
    spare = W - bands
    for t, c0, width in groups:
        start = (t * cols + c0) * TILE
        for i in range(TILE):
            at = slice(start + i * width, start + (i + 1) * width)
            halves_ref[at, bands:W] = one_in(i % 2, width, spare)
            halves_ref[at, W + bands :] = jnp.zeros((width, spare), BF16)
    for buffer in (between_a, between_b):
        buffer[:, bands:W] = one_in(PAIR_ONE, buffer.shape[0], spare)
        buffer[:, W + bands :] = jnp.zeros((buffer.shape[0], spare), BF16)
    mask_copy.wait()

    def put(value, buffer, at, lanes, squares):
        count = value.shape[0]
        high = value.astype(BF16)
        low = (value - high.astype(F32)).astype(BF16)
        buffer[at : at + count, lanes] = high
        buffer[at : at + count, slice(W + lanes.start, W + lanes.stop)] = low
        parts = (low * low).reshape(count // 16, 16, -1)
        total = parts[0]
        for k in range(1, count // 16):
            total = total + parts[k]
        return squares + jnp.sum(total.astype(F32).reshape(2, 8, -1), 0)

    def product(ref, buffer, places, width):
        value = jnp.concatenate([buffer[at : at + width, :] for at in places], 0)
        ref[...] += dot_t(value[:, :W], value)

    lane_halves = (slice(0, 128), slice(128, bands))
    squares = {(k, h): jnp.zeros((8, lanes.stop - lanes.start), F32) for k in range(3) for h, lanes in enumerate(lane_halves)}
    pending = []
    for g, (t, c0, width) in enumerate(groups):
        between = (between_a, between_b)[g % 2]
        start = (t * cols + c0) * TILE
        fetch(g).wait()
        if c0 == 0:
            fill_validity(mask, t, valid_ref.at[t])
        gap = 1 if width == 128 else 2
        slot = 0
        for c in range(0, width, BLOCK):
            block = slice(c0 + c, c0 + c + BLOCK)
            valid = valid_ref[t, block, :128]
            for h, lanes in enumerate(lane_halves):
                if pending and slot % gap == 0:
                    product(*pending.pop(0))
                slot += 1
                weight = valid[:, : lanes.stop - lanes.start]
                previous = last[block, lanes] if t else None
                for i in range(TILE // 2):
                    row = t * TILE + 2 * i
                    first = raw[row, block, lanes] * weight
                    second = raw[row + 1, block, lanes] * weight
                    if previous is None:
                        first_ref[block, lanes] = first
                        gone = jnp.zeros_like(first)
                    else:
                        gone = first - previous
                        if i == 0:
                            gone = gone * (valid_ref[t - 1, block, : weight.shape[1]] * weight)
                    previous = second
                    at = start + 2 * i * width + c
                    squares[0, h] = put(first + second, halves_ref, at, lanes, squares[0, h])
                    squares[1, h] = put(second - first, halves_ref, at + width, lanes, squares[1, h])
                    squares[2, h] = put(gone, between, i * width + c, lanes, squares[2, h])
                last[block, lanes] = previous
        for late in pending:
            product(*late)
        pairs = range(TILE // 2)
        pending = [
            (sums_ref, halves_ref, [start + 2 * i * width for i in pairs], width),
            (steps_ref, halves_ref, [start + (2 * i + 1) * width for i in pairs], width),
            (seams_ref, between, [i * width for i in pairs], width),
        ]
    for late in pending:
        product(*late)
    for k in range(3):
        rest_ref[k, :, bands:] = jnp.zeros((8, W - bands), F32)
        for h, lanes in enumerate(lane_halves):
            rest_ref[k, :, lanes] = squares[k, h]


def moments(mask, cube):
    rows, cols, bands = cube.shape
    pixels = rows * cols
    widest = max(width for _, width in CUTS) * TILE // 2
    return pl.pallas_call(
        moments_kernel,
        out_shape=[
            pltpu.VMEM((pixels, 2 * W), BF16),
            pltpu.VMEM((rows // TILE, cols, W), F32),
            pltpu.VMEM((cols, bands), F32),
            pltpu.VMEM((W, 2 * W), F32),
            pltpu.VMEM((W, 2 * W), F32),
            pltpu.VMEM((W, 2 * W), F32),
            pltpu.VMEM((3, 8, W), F32),
        ],
        in_specs=[in_hbm(), in_hbm()],
        out_specs=[in_vmem()] * 7,
        scratch_shapes=[
            pltpu.SMEM(mask.shape, jnp.int32),
            pltpu.VMEM(cube.shape, F32),
            pltpu.VMEM((cols, bands), F32),
            pltpu.VMEM((widest, 2 * W), BF16),
            pltpu.VMEM((widest, 2 * W), BF16),
            pltpu.SemaphoreType.DMA((rows // TILE * len(CUTS) + 1,)),
        ],
        compiler_params=params(40),
        cost_estimate=pl.CostEstimate(flops=3 * 2 * pixels * W * W, bytes_accessed=4 * pixels * W, transcendentals=0),
        name="moments",
    )(mask, cube)


def indices(shape):
    return lax.broadcasted_iota(jnp.int32, shape, 0), lax.broadcasted_iota(jnp.int32, shape, 1)


def pack_kernel(
    core_ref, track_ref, valid_ref, first_ref, above_ref, sums_ref, steps_ref, seams_ref, rest_ref, mine_ref, other_ref, packed, buffer, above_row
):
    bands = first_ref.shape[1]
    half = bands // 2
    row, column = indices((W, W))
    on_diagonal = row == column
    first_valid = valid_ref[0]
    cols = first_valid.shape[0]
    pixel_row, tile = indices((cols, 128))
    keep = folding(cols, bands)[0]
    unfold_row(above_ref, above_row)
    flags = jnp.where(tile == lax.shift_right_logical(pixel_row, 3), above_ref[keep : keep + 1, :128], 0.0)
    flags = jnp.where(track_ref[0] > 0, jnp.sum(flags, 1, keepdims=True), 0.0)
    weight = first_valid * jnp.broadcast_to(flags, first_valid.shape)
    difference = (first_ref[...] - above_row[...]) * weight[:, :bands]
    high, low = split(difference)
    rest = difference - high.astype(F32)
    buffer[:, bands:W] = one_in(PAIR_ONE, buffer.shape[0], W - bands)
    buffer[:, W + bands :] = jnp.zeros((buffer.shape[0], W - bands), BF16)
    buffer[:, :bands] = high
    buffer[:, W : W + bands] = low
    steps = steps_ref[...]
    seams = seams_ref[...] + dot_t(buffer[:, :W], buffer[...])
    rests = [jnp.sum(rest_ref[k, :, :bands], 0, keepdims=True) for k in range(3)]
    rests[2] = rests[2] + jnp.sum(rest * rest, 0, keepdims=True)

    def whole(parts, squares):
        mixed = parts[:, W:]
        squares = jnp.concatenate([squares, jnp.zeros((1, W - bands), F32)], 1)
        return parts[:, :W] + mixed + mixed.T + jnp.where(on_diagonal, squares, 0.0)

    pixel = whole(0.5 * (sums_ref[...] + steps), 0.5 * (rests[0] + rests[1]))
    pixel = jnp.where(column == bands + PIXEL_ONE, 2.0 * pixel, pixel)
    pair = whole(steps + seams, rests[1] + rests[2])
    valid = valid_ref[:, :, :128]
    inner = jnp.sum(valid, 0)
    crossing = jnp.sum(valid[1:] * valid[:-1], 0)
    pixel_count = TILE * jnp.sum(inner, 0, keepdims=True)
    pair_count = jnp.sum((TILE - 1) * inner + crossing + weight[:, :128], 0, keepdims=True)
    out = jnp.where(column <= row, pair, 0.0)
    out = jnp.where((column > row) & (column <= bands + 1), pltpu.roll(pixel, 1, 1), out)
    out = jnp.where(column == bands + 2, pltpu.roll(pair, 2 - PAIR_ONE, 1), out)
    counts = jnp.where(row == 0, pixel_count[:, :1], 0.0)
    counts = jnp.where(row == 1, pair_count[:, :1], counts)
    packed[...] = jnp.where(column == bands + 3, counts, out)
    core = core_ref[0]
    mine_ref[...] = packed[pl.ds(pl.multiple_of(core * half, 8), half), :]
    other_ref[...] = packed[pl.ds(pl.multiple_of((1 - core) * half, 8), half), :]


def pack(core, track, valid, first, above, sums, steps, seams, rest):
    cols, bands = first.shape
    half = pltpu.VMEM((bands // 2, W), F32)
    return pl.pallas_call(
        pack_kernel,
        out_shape=[half, half],
        in_specs=[pl.BlockSpec(memory_space=pltpu.SMEM)] * 2 + [in_vmem()] * 7,
        out_specs=[in_vmem()] * 2,
        scratch_shapes=[pltpu.VMEM((W, W), F32), pltpu.VMEM((cols, 2 * W), BF16), pltpu.VMEM((cols, bands), F32)],
        compiler_params=params(12),
        name="pack",
    )(core, track, valid, first, above, sums, steps, seams, rest)


def square_sum(x):
    return jnp.sum(x * x)


QUICK_STEPS = 7


def careful(matrix, target, identity, row, column, bands, left, right):
    start = 1.0 / jnp.max(jnp.sum(jnp.abs(matrix), 1, keepdims=True))
    left[:W, :] = start * identity
    left[W:, :] = identity - start * matrix

    def more(carry):
        count, size = carry
        return (count < 24) & (size > 4e-6)

    def squaring(carry):
        count, _ = carry
        new = dot3(left[...], left[W:, :])
        left[:W, :] = left[:W, :] + new[:W]
        left[W:, :] = new[W:]
        return count + 1, square_sum(new[W:])

    lax.while_loop(more, squaring, (0, jnp.float32(1e9)))
    right[...] = dot3(left[:W, :], target)

    def refining(carry):
        count, _ = carry
        residual = target - dot6(matrix, right[...])
        change = dot3(left[:W, :], residual)
        gain = right[...] + change
        right[...] = gain
        return count + 1, square_sum(change) / square_sum(gain)

    def rough(carry):
        count, size = carry
        return (count < 8) & jnp.logical_not(size <= 1e-6)

    _, size = lax.while_loop(rough, refining, (0, jnp.float32(1e9)))

    @pl.when(jnp.logical_not(size <= 1e-6))
    def _():
        left[:W, :] = matrix
        right[...] = target

        def eliminate(k, _):
            here = row[:, 0:1] == k
            pivot_left = left[pl.ds(k, 1), :]
            pivot_right = right[pl.ds(k, 1), :]
            values = jnp.sum(jnp.where(column == k, left[:W, :], 0.0), 1, keepdims=True)
            pivot = jnp.sum(jnp.where(here, values, 0.0))
            factor = jnp.where(here, (values - 1.0) / pivot, values / pivot)
            left[:W, :] = left[:W, :] - factor * pivot_left
            right[...] = right[...] - factor * pivot_right
            return 0

        lax.fori_loop(0, bands, eliminate, 0)


def solve_kernel(bands, core_ref, mine_ref, other_ref, weights_ref, left, right):
    core = core_ref[0]
    packed = jnp.concatenate([mine_ref[...], other_ref[...]], 0)
    swapped = jnp.concatenate([other_ref[...], mine_ref[...]], 0)
    packed = jnp.where(core == 0, packed, swapped)
    packed = jnp.concatenate([packed, jnp.zeros((W - bands, W), F32)], 0)
    row, column = indices((W, W))
    on_diagonal = row == column
    inside = (row < bands) & (column < bands)
    pixel_count = packed[0:1, bands + 3 : bands + 4]
    pair_count = packed[1:2, bands + 3 : bands + 4]

    def whole(triangle):
        return triangle + triangle.T - jnp.where(on_diagonal, triangle, 0.0)

    pixel = whole(jnp.where((column >= row) & (column <= bands), pltpu.roll(packed, W - 1, 1), 0.0))
    lower = jnp.where((column <= row) & inside, packed, 0.0)
    sums = jnp.where((column == bands) & (row < bands), pltpu.roll(packed, W - 2, 1), 0.0)
    pair = whole(lower + sums)

    def covariance(square, count):
        total = square[bands : bands + 1, :]
        total_rows = square[:, bands : bands + 1]
        return jnp.where(inside, (square - total_rows * total / count) / (count - 1.0), 0.0)

    signal = covariance(pixel, pixel_count)
    noise = covariance(pair, pair_count)
    combined = signal + noise
    mean = pixel[:, bands : bands + 1] / pixel_count
    diagonal = jnp.where(on_diagonal, combined, 0.0)
    scale_row = lax.rsqrt(jnp.where(column[0:1] < bands, jnp.sum(diagonal, 0, keepdims=True), 1.0))
    scale_column = lax.rsqrt(jnp.where(row[:, 0:1] < bands, jnp.sum(diagonal, 1, keepdims=True), 1.0))
    identity = jnp.where(on_diagonal, 1.0, 0.0)
    matrix = jnp.where(inside, combined * scale_column * scale_row, identity)
    target = noise * scale_column * scale_row

    coarse = matrix.astype(BF16)
    square = dot(coarse, coarse)
    shrink = lax.rsqrt(jnp.max(jnp.sum(jnp.abs(square), 1, keepdims=True), 0, keepdims=True))
    near = 2.0 * shrink * matrix - shrink * shrink * square
    inverse = 2.0 * shrink * identity - shrink * shrink * matrix

    def double(near, inverse):
        step = dot(near.astype(BF16), jnp.concatenate([near.astype(BF16), inverse.astype(BF16)], 1))
        return 2.0 * near - step[:, :W], 2.0 * inverse - step[:, W:]

    for _ in range(QUICK_STEPS):
        near, inverse = double(near, inverse)
    off = identity - dot3(matrix, inverse)
    inverse = inverse + dot(inverse.astype(BF16), off.astype(BF16))
    first = dot3(inverse, target)
    change = dot(inverse.astype(BF16), (target - dot3(matrix, first)).astype(BF16))
    right[...] = first + change
    off_size = square_sum(off)
    done = square_sum(change) * off_size * off_size <= 1e-8 * square_sum(first)

    @pl.when(jnp.logical_not(done & (off_size < 0.25)))
    def _():
        careful(matrix, target, identity, row, column, bands, left, right)

    gain = right[...] * scale_column * (1.0 / scale_row)
    shift = jnp.sum(jnp.where(row < bands, mean, 0.0) * gain, 0, keepdims=True)
    weights = jnp.where(row == bands + PIXEL_ONE, shift, jnp.where(inside, 0.5 * (identity - gain), 0.0))
    high, low = split(weights)
    weights_ref[:W, :] = high
    weights_ref[W : 2 * W, :] = high
    weights_ref[2 * W :, :] = low


def solve(core, mine, other, bands):
    return pl.pallas_call(
        functools.partial(solve_kernel, bands),
        out_shape=pltpu.VMEM((3 * W, W), BF16),
        in_specs=[pl.BlockSpec(memory_space=pltpu.SMEM), in_vmem(), in_vmem()],
        out_specs=in_vmem(),
        scratch_shapes=[pltpu.VMEM((2 * W, W), F32), pltpu.VMEM((W, W), F32)],
        compiler_params=params(16),
        name="solve",
    )(core, mine, other)


def filter_kernel(halves_ref, valid_ref, weights_ref, out_hbm, staged, sems):
    rows, cols, bands = staged.shape
    copies = []
    for t in range(rows // TILE):
        for c0, width in CUTS:
            at = (t * cols + c0) * TILE
            valid = valid_ref.at[t, c0 : c0 + width, :bands]
            for i in range(TILE // 2):
                halves = halves_ref[at + 2 * i * width : at + 2 * (i + 1) * width, :]
                result = dot(jnp.concatenate([halves, halves[:, :W]], 1), weights_ref[...])
                half_sum, half_step = result[:width, :bands], result[width:, :bands]
                row = t * TILE + 2 * i
                staged[row, c0 : c0 + width] = valid[...] * (half_sum - half_step)
                staged[row + 1, c0 : c0 + width] = valid[...] * (half_sum + half_step)
                part = (pl.ds(row, 2), pl.ds(c0, width))
                copies.append(pltpu.make_async_copy(staged.at[part], out_hbm.at[part], sems.at[len(copies)]))
                copies[-1].start()
    for copy in copies:
        copy.wait()


def apply_filter(halves, valid, weights, shape):
    rows, cols, bands = shape
    pixels = rows * cols
    return pl.pallas_call(
        filter_kernel,
        out_shape=jax.ShapeDtypeStruct(shape, F32),
        in_specs=[in_vmem()] * 3,
        out_specs=in_hbm(),
        scratch_shapes=[pltpu.VMEM(shape, F32), pltpu.SemaphoreType.DMA((rows // 2 * len(CUTS),))],
        compiler_params=params(24),
        cost_estimate=pl.CostEstimate(flops=3 * 2 * pixels * W * W, bytes_accessed=4 * pixels * W, transcendentals=0),
        name="filter",
    )(halves, valid, weights)


RING = 4


def permute(x, target):
    track, strip = lax.axis_size("track"), lax.axis_size("strip")
    pairs = []
    for i in range(track):
        for j in range(strip):
            y, z, chip, core = target(i // RING, i % RING, j // 2, j % 2)
            pairs.append((i * strip + j, (y * RING + z) * strip + chip * 2 + core))
    return lax.ppermute(x, ("track", "strip"), pairs)


def other_core(x):
    return permute(x, lambda y, z, chip, core: (y, z, chip, 1 - core))


PARTNER = {1: (1, 0, 3, 2), 2: (2, 3, 0, 1), 3: (3, 2, 1, 0)}


def ring_sum(x, axes):
    def exchanged(which):
        def target(y, z, chip, core):
            place = [y, z, chip]
            axis = axes[core]
            place[axis] = PARTNER[which if core == 0 else RING - which][place[axis]]
            return (*place, core)

        return permute(x, target)

    return lax.optimization_barrier(x + exchanged(1) + exchanged(3) + exchanged(2))


def per_device(cube, mask):
    bands = cube.shape[2]
    size = lax.axis_size("track")
    above = lax.ppermute(final_row(mask, cube), "track", [(i, (i + 1) % size) for i in range(size)])
    core = (lax.axis_index("strip") % 2).astype(jnp.int32)[None]
    track = lax.axis_index("track").astype(jnp.int32)[None]
    halves, valid, first, sums, steps, seams, rest = moments(mask, cube)
    mine, other = pack(core, track, valid, first, above, sums, steps, seams, rest)
    total = mine + other_core(other)
    for axes in ((2, 0), (0, 2), (1, 1)):
        total = ring_sum(total, axes)
    weights = solve(core, total, other_core(total), bands)
    return apply_filter(halves, valid, weights, cube.shape)


def solution(mesh):
    return jax.shard_map(
        per_device,
        mesh=mesh,
        in_specs=(P("track", "strip", None), P("track", "strip")),
        out_specs=P("track", "strip", None),
        check_vma=False,
    )
```
